32 devices in a mesh: groups: 2 (over y), blk: 8 (over z, x), heads: 2 (over core).
Axes of the slice: x: 2, y: 2, z: 4, core: 2. Of those that a mesh axis runs over, the one named last changes fastest.
Arguments:
- queries: bfloat16 [16, 64, 128], P(('groups', 'blk'), 'heads'), parts along dimension 0, may hold values from -256 to 256
- prefix_keys: bfloat16 [4096, 8, 128], P(('groups', 'blk'), 'heads'), parts along dimension 0, may hold values from -12 to 12
- prefix_values: bfloat16 [4096, 8, 128], P(('groups', 'blk'), 'heads'), parts along dimension 0, may hold values from -12 to 12
- suffix_pool: bfloat16 [48, 2, 16, 8, 128], P(('groups', 'blk'), None, None, 'heads'), parts along dimension 0, may hold values from -8.375 to 8.375
- page_owner: int32 [6, 8], P('groups'), parts along dimension 0, may hold values from 0 to 7, as said below
- page_slot: int32 [6, 8], P('groups'), parts along dimension 0, may hold values from 0 to 2, as said below
- suffix_len: int32 [6], P('groups'), parts along dimension 0, may hold values from 1 to 128, as said below
- row_request: int32 [16], P('groups'), parts along dimension 0, may hold values from 0 to 2, as said below
Outputs:
- attn_out: bfloat16 [16, 64, 128], P(('groups', 'blk'), 'heads'), parts along dimension 0
The draws below stay inside these ranges and needn't reach their ends.
There are 2 independent parts, one for each index of `groups`. The reference program is written for one: setup_inputs(seed, part) draws one part's arguments, and reference() takes and returns one part's arrays. A program takes and returns all parts, laid end to end along the dimension named above; each array names one. Nothing has to cross between parts.
Inputs may be any that keep to these rules, and one draw needn't show every extreme that they name: `row_request`: rows 0 to 5 belong to one request, whose last 6 suffix tokens they are, in order; each later row is the only row of its request; every request has rows. `suffix_len`: counts the rows' own tokens; the prefill span's request has 6 or more, and some other request has exactly 128. Each request has one page on every blk index: page j lies on (page_owner[r, 0] + j) modulo the number of blk indices. `page_slot`: A local slot of the owner's pool; two requests never share a slot on one owner.
All inputs are finite; a program needn't handle non-finite values.
Results may differ from the reference program's by a relative error of at most 0.005.
Values may be sent and summed in bfloat16 or wider, within the bound.
No kernel may reach another device: no remote copies, remote signals or barrier semaphores. Data moves between devices by JAX's collectives and lax.ppermute only.
A program may use at most 64 MiB of HBM per device.

```python
import math
import jax
import jax.numpy as jnp
from jax import lax

QH = 64
KVH = 8
HD = 128
PAGE = 16
PREFIX = 2048
ROWS = 8
DECODE = 2
SPAN = 6
REQ = 3
SUF_MAX = 128
N_BLK = 8


def key_table(key):
    normal_keys = jnp.clip(jax.random.normal(jax.random.fold_in(key, 11), (PREFIX, KVH, HD), jnp.float32), -5.0, 5.0)
    keys_drawn = normal_keys
    return keys_drawn


def draw_prefix_keys(key, part):
    return key_table(key).astype(jnp.bfloat16)


def draw_queries(key, part):
    drawn = 3.0 * jnp.clip(jax.random.normal(jax.random.fold_in(key, 21), (ROWS, QH, HD), jnp.float32), -6.0, 6.0)
    return drawn.astype(jnp.bfloat16)


def request_tables(key):
    base_key = jax.random.fold_in(key, 31)
    req_order = jax.random.permutation(jax.random.fold_in(base_key, 1), REQ).astype(jnp.int32)
    row_req = jnp.concatenate([jnp.full((SPAN,), req_order[0], jnp.int32), req_order[1:]])
    lengths = jax.random.randint(jax.random.fold_in(base_key, 2), (REQ,), 1, SUF_MAX + 1)
    lengths = lengths.at[req_order[0]].set(jax.random.randint(jax.random.fold_in(base_key, 3), (), SPAN, SUF_MAX + 1))
    longest = req_order[1 + jax.random.randint(jax.random.fold_in(base_key, 4), (), 0, DECODE)]
    lengths = lengths.at[longest].set(SUF_MAX)
    page_count = SUF_MAX // PAGE
    home_owner = jax.random.randint(jax.random.fold_in(base_key, 5), (REQ,), 0, page_count)
    owner_table = (home_owner[:, None] + jnp.arange(page_count)[None, :]) % page_count
    slot_perms = jax.vmap(lambda sub_key: jax.random.permutation(sub_key, REQ))(jax.random.split(jax.random.fold_in(base_key, 6), page_count))
    slot_table = slot_perms[owner_table, jnp.arange(REQ)[:, None]]
    return (row_req.astype(jnp.int32), lengths.astype(jnp.int32), owner_table.astype(jnp.int32), slot_table.astype(jnp.int32))


def draw_row_request(key, part):
    return request_tables(key)[0]


def draw_suffix_len(key, part):
    return request_tables(key)[1]


def draw_page_owner(key, part):
    return request_tables(key)[2]


def draw_page_slot(key, part):
    return request_tables(key)[3]


def levels(key, dims, pieces, low, top_value):
    loudness, own = 1.0, jax.random.fold_in(key, 6)
    for dim, parts in pieces:
        heights = jnp.exp(jax.random.uniform(jax.random.fold_in(own, dim), (parts,), jnp.float32, low / len(pieces), top_value / len(pieces)))
        loudness = loudness * jnp.repeat(heights, dims[dim] // parts).reshape([-1 if axis == dim else 1 for axis in range(len(dims))])
    return loudness


def gaussian(stream_key, dims, width, limit, shards=(), kind=jnp.bfloat16):
    entries = jax.random.normal(stream_key, dims, jnp.float32) * width
    if len(shards) > 0:
        entries = levels(stream_key, dims, shards, -0.22, 0.18) * entries
    return jnp.clip(entries, min=-limit, max=limit).astype(kind)


def setup_inputs(seed: int = 0, part: int = 0) -> dict:
    keys = jax.random.split(jax.random.key(seed), 9)
    part_keys = jax.random.split(jax.random.fold_in(keys[8], part), 9)
    return {
        "queries": draw_queries(jax.random.fold_in(jax.random.fold_in(keys[8], part), 71), part),
        "prefix_keys": draw_prefix_keys(jax.random.fold_in(jax.random.fold_in(keys[8], part), 71), part),
        "prefix_values": gaussian(part_keys[2], (PREFIX, KVH, HD), 2.0, 12.0, ((0, 8), (1, 2))),
        "suffix_pool": gaussian(part_keys[3], (REQ * N_BLK, 2, PAGE, KVH, HD), 1.4, 8.375, ((0, 8), (3, 2))),
        "page_owner": draw_page_owner(jax.random.fold_in(jax.random.fold_in(keys[8], part), 71), part),
        "page_slot": draw_page_slot(jax.random.fold_in(jax.random.fold_in(keys[8], part), 71), part),
        "suffix_len": draw_suffix_len(jax.random.fold_in(jax.random.fold_in(keys[8], part), 71), part),
        "row_request": draw_row_request(jax.random.fold_in(jax.random.fold_in(keys[8], part), 71), part),
    }


def reference(queries, prefix_keys, prefix_values, suffix_pool, page_owner, page_slot, suffix_len, row_request):
    group = QH // KVH
    score_scale = 1.0 / math.sqrt(HD)
    keys_wide = prefix_keys.astype(jnp.float32)
    values_wide = prefix_values.astype(jnp.float32)
    pool_rows = (page_owner * REQ + page_slot).astype(jnp.int32)
    row_order = jnp.arange(ROWS, dtype=jnp.int32)
    same_req = row_request[:, None] == row_request[None, :]
    later_rows = lax.optimization_barrier(jnp.sum((same_req & (row_order[None, :] > row_order[:, None])).astype(jnp.int32), axis=1))
    limits = (suffix_len[row_request] - later_rows).astype(jnp.int32)
    token_pos = jnp.arange(SUF_MAX, dtype=jnp.int32)

    def one_row(packed):
        query_row, request, row_limit = packed
        grouped = query_row.astype(jnp.float32).reshape(KVH, group, HD)
        page_data = suffix_pool[pool_rows[request]].astype(jnp.float32)
        suffix_keys = page_data[:, 0].reshape(SUF_MAX, KVH, HD)
        suffix_values = page_data[:, 1].reshape(SUF_MAX, KVH, HD)
        prefix_scores = jnp.einsum('gqd,kgd->gqk', grouped, keys_wide) * score_scale
        suffix_scores = jnp.einsum('gqd,kgd->gqk', grouped, suffix_keys) * score_scale
        visible = token_pos < row_limit
        highest = jnp.maximum(lax.optimization_barrier(jnp.max(prefix_scores, axis=-1)), lax.optimization_barrier(jnp.max(jnp.where(visible, suffix_scores, -jnp.inf), axis=-1)))
        prefix_probs = jnp.exp(prefix_scores - highest[..., None])
        suffix_probs = jnp.where(visible, jnp.exp(suffix_scores - highest[..., None]), 0.0)
        denominator = lax.optimization_barrier(jnp.sum(prefix_probs, axis=-1)) + lax.optimization_barrier(jnp.sum(suffix_probs, axis=-1))
        rounded_prefix = lax.optimization_barrier(prefix_probs.astype(jnp.bfloat16)).astype(jnp.float32)
        rounded_suffix = lax.optimization_barrier(suffix_probs.astype(jnp.bfloat16)).astype(jnp.float32)
        mixed = jnp.einsum('gqk,kgd->gqd', rounded_prefix, values_wide)
        mixed = mixed + jnp.einsum('gqk,kgd->gqd', rounded_suffix, suffix_values)
        return (mixed / denominator[..., None]).reshape(QH, HD).astype(jnp.bfloat16)
    return lax.map(one_row, (queries, row_request, limits))
```

```python
import math

import jax
import jax.numpy as jnp
from jax import lax
from jax.sharding import PartitionSpec as P


def on_device(
    queries, prefix_keys, prefix_values, suffix_pool, page_owner, page_slot, suffix_len, row_request
):
    block_count = lax.axis_size("blk")
    self_index = lax.axis_index("blk")
    rows_dev, qheads, head_dim = queries.shape
    slots, _, page_len, kv_heads, _ = suffix_pool.shape
    row_count = row_request.shape[0]
    req_count = suffix_len.shape[0]
    prefix_len = prefix_keys.shape[0]
    group = qheads // kv_heads
    score_scale = 1.0 / math.sqrt(head_dim)

    spread = jnp.broadcast_to(queries[None], (block_count,) + queries.shape)
    all_rows = lax.all_to_all(spread, "blk", split_axis=0, concat_axis=0, tiled=True)
    grouped = all_rows.reshape(row_count, kv_heads, group, head_dim)

    row_order = jnp.arange(row_count, dtype=jnp.int32)
    same_req = row_request[:, None] == row_request[None, :]
    later_rows = jnp.sum(
        (same_req & (row_order[None, :] > row_order[:, None])).astype(jnp.int32), axis=1
    )
    one_hot = (row_request[:, None] == jnp.arange(req_count, dtype=jnp.int32)[None, :]).astype(
        jnp.int32
    )
    limits = jnp.sum(one_hot * suffix_len[None, :], axis=1) - later_rows
    home_owner = jnp.sum(one_hot * page_owner[None, :, 0], axis=1)
    own_slot = jnp.sum(jnp.where(page_owner == self_index, page_slot, 0), axis=1)
    row_slot = jnp.sum(one_hot * own_slot[None, :], axis=1)
    page_index = (self_index - home_owner) % block_count
    token = page_index[:, None] * page_len + jnp.arange(page_len, dtype=jnp.int32)[None, :]
    in_slot = row_slot[:, None] == jnp.arange(slots, dtype=jnp.int32)[None, :]
    visible = (in_slot[:, :, None] & (token < limits[:, None])[:, None, :]).reshape(
        row_count, slots * page_len
    )
    shown = jnp.concatenate([jnp.ones((row_count, prefix_len), bool), visible], axis=1)
    keys = jnp.concatenate(
        [prefix_keys, suffix_pool[:, 0].reshape(slots * page_len, kv_heads, head_dim)], axis=0
    )
    values = jnp.concatenate(
        [prefix_values, suffix_pool[:, 1].reshape(slots * page_len, kv_heads, head_dim)], axis=0
    )
    scores = (
        jnp.einsum("rgqd,kgd->rgqk", grouped, keys, preferred_element_type=jnp.float32)
        * score_scale
    )
    scores = jnp.where(shown[:, None, None, :], scores, -jnp.inf)
    top = jnp.max(scores, axis=-1)
    probs = jnp.exp(scores - top[..., None])
    total = jnp.sum(probs, axis=-1)
    mixed = jnp.einsum(
        "rgqk,kgd->rgqd",
        probs.astype(jnp.bfloat16),
        values,
        preferred_element_type=jnp.float32,
    )
    stats = jnp.stack(
        [top.reshape(row_count, qheads), total.reshape(row_count, qheads)], axis=1
    ).reshape(row_count, 2 * qheads)
    stat_rows = -(-2 * qheads // head_dim)
    stats = jnp.pad(stats, ((0, 0), (0, stat_rows * head_dim - 2 * qheads)))
    parcel = jnp.concatenate(
        [mixed.reshape(row_count, qheads, head_dim), stats.reshape(row_count, stat_rows, head_dim)],
        axis=1,
    ).reshape(block_count, rows_dev, qheads + stat_rows, head_dim)
    parcel = lax.all_to_all(parcel, "blk", split_axis=0, concat_axis=0, tiled=True)
    stats = parcel[:, :, qheads:].reshape(block_count, rows_dev, -1)
    part_max = stats[:, :, :qheads]
    part_sum = stats[:, :, qheads : 2 * qheads]
    weight = jnp.exp(part_max - jnp.max(part_max, axis=0)[None])
    return (
        jnp.sum(parcel[:, :, :qheads] * weight[..., None], axis=0)
        / jnp.sum(part_sum * weight, axis=0)[..., None]
    ).astype(jnp.bfloat16)


def solution(mesh):
    placed = (
        P(("groups", "blk"), "heads", None),
        P(("groups", "blk"), "heads", None),
        P(("groups", "blk"), "heads", None),
        P(("groups", "blk"), None, None, "heads", None),
        P("groups", None),
        P("groups", None),
        P("groups"),
        P("groups"),
    )
    return jax.shard_map(
        on_device,
        mesh=mesh,
        in_specs=placed,
        out_specs=P(("groups", "blk"), "heads", None),
        check_vma=False,
    )
```

```python
import math

import jax
import jax.numpy as jnp
from jax import lax
from jax.sharding import PartitionSpec as P


def exchange(value, bit):
    size = lax.axis_size("blk")
    return lax.ppermute(value, "blk", [(i, i ^ bit) for i in range(size)])


def row_tables(rows, page_owner, page_slot, suffix_len, row_request):
    row_count = row_request.shape[0]
    req_count = suffix_len.shape[0]
    row_order = jnp.arange(row_count, dtype=jnp.int32)
    same_req = row_request[rows][:, None] == row_request[None, :]
    later = jnp.sum((same_req & (row_order[None, :] > rows[:, None])).astype(jnp.int32), axis=1)
    one_hot = row_request[rows][:, None] == jnp.arange(req_count, dtype=jnp.int32)[None, :]
    limits = jnp.sum(jnp.where(one_hot, suffix_len[None, :], 0), axis=1) - later
    home = jnp.sum(jnp.where(one_hot, page_owner[None, :, 0], 0), axis=1)
    return one_hot, limits, home


def visible_pages(device, one_hot, limits, home, page_owner, page_slot, slots, page_len):
    block_count = lax.axis_size("blk")
    own_slot = jnp.sum(jnp.where(page_owner == device, page_slot, 0), axis=1)
    row_slot = jnp.sum(jnp.where(one_hot, own_slot[None, :], 0), axis=1)
    page_index = (device - home) % block_count
    token = page_index[:, None] * page_len + jnp.arange(page_len, dtype=jnp.int32)[None, :]
    in_slot = row_slot[:, None] == jnp.arange(slots, dtype=jnp.int32)[None, :]
    shown = in_slot[:, :, None] & (token < limits[:, None])[:, None, :]
    return shown.reshape(limits.shape[0], slots * page_len)


def attend(grouped, parts):
    score_scale = 1.0 / math.sqrt(grouped.shape[-1])
    scored = []
    for keys, _, shown in parts:
        scores = (
            jnp.einsum("rgqd,kgd->rgqk", grouped, keys, preferred_element_type=jnp.float32)
            * score_scale
        )
        if shown is not None:
            scores = jnp.where(shown[:, None, None, :], scores, -jnp.inf)
        scored.append(scores)
    top = jnp.max(scored[0], axis=-1)
    for scores in scored[1:]:
        top = jnp.maximum(top, jnp.max(scores, axis=-1))
    total = 0.0
    mixed = 0.0
    for scores, (_, values, _) in zip(scored, parts):
        probs = jnp.exp(scores - top[..., None])
        total = total + jnp.sum(probs, axis=-1)
        mixed = mixed + jnp.einsum(
            "rgqk,kgd->rgqd",
            probs.astype(jnp.bfloat16),
            values,
            preferred_element_type=jnp.float32,
        )
    return top, total, mixed


def pack(top, total, mixed):
    rows, qheads, head_dim = mixed.shape
    stat_rows = -(-2 * qheads // head_dim)
    stats = jnp.concatenate([top, total], axis=1)
    stats = jnp.pad(stats, ((0, 0), (0, stat_rows * head_dim - 2 * qheads)))
    return jnp.concatenate([mixed, stats.reshape(rows, stat_rows, head_dim)], axis=1)


def unpack(parcel, qheads):
    stats = parcel[:, qheads:].reshape(parcel.shape[0], -1)
    return stats[:, :qheads], stats[:, qheads : 2 * qheads], parcel[:, :qheads]


def merge(first, second):
    top = jnp.maximum(first[0], second[0])
    first_weight = jnp.exp(first[0] - top)
    second_weight = jnp.exp(second[0] - top)
    return (
        top,
        first[1] * first_weight + second[1] * second_weight,
        first[2] * first_weight[..., None] + second[2] * second_weight[..., None],
    )


def on_device(
    queries, prefix_keys, prefix_values, suffix_pool, page_owner, page_slot, suffix_len, row_request
):
    block_count = lax.axis_size("blk")
    me = lax.axis_index("blk")
    rows_dev, qheads, head_dim = queries.shape
    slots, _, page_len, kv_heads, _ = suffix_pool.shape
    bits = [1 << b for b in range(1, block_count.bit_length() - 1)]

    far_keys = exchange(prefix_keys, 1)
    held = queries
    for bit in bits:
        held = jnp.concatenate([held, exchange(held, bit)], axis=0)
    far_values = exchange(prefix_values, 1)
    far_pool = exchange(suffix_pool, 1)
    held_count = held.shape[0]

    order = jnp.arange(held_count, dtype=jnp.int32)
    rows = (me ^ ((order // rows_dev) * 2)) * rows_dev + order % rows_dev
    one_hot, limits, home = row_tables(rows, page_owner, page_slot, suffix_len, row_request)
    parts = [(prefix_keys, prefix_values, None), (far_keys, far_values, None)]
    for device, pool in ((me, suffix_pool), (me ^ 1, far_pool)):
        shown = visible_pages(device, one_hot, limits, home, page_owner, page_slot, slots, page_len)
        pages = pool.reshape(slots, 2, page_len, kv_heads, head_dim)
        parts.append(
            (
                pages[:, 0].reshape(slots * page_len, kv_heads, head_dim),
                pages[:, 1].reshape(slots * page_len, kv_heads, head_dim),
                shown,
            )
        )
    grouped = held.reshape(held_count, kv_heads, qheads // kv_heads, head_dim)
    top, total, mixed = attend(grouped, parts)
    part = (
        top.reshape(held_count, qheads),
        total.reshape(held_count, qheads),
        mixed.reshape(held_count, qheads, head_dim),
    )
    for bit in reversed(bits):
        half = part[0].shape[0] // 2
        sent = pack(*(value[half:] for value in part))
        part = merge(tuple(value[:half] for value in part), unpack(exchange(sent, bit), qheads))
    return (part[2] / part[1][..., None]).astype(jnp.bfloat16)


def solution(mesh):
    placed = (
        P(("groups", "blk"), "heads", None),
        P(("groups", "blk"), "heads", None),
        P(("groups", "blk"), "heads", None),
        P(("groups", "blk"), None, None, "heads", None),
        P("groups", None),
        P("groups", None),
        P("groups"),
        P("groups"),
    )
    return jax.shard_map(
        on_device,
        mesh=mesh,
        in_specs=placed,
        out_specs=P(("groups", "blk"), "heads", None),
        check_vma=False,
    )
```

```python
import functools
import math

import jax
import jax.numpy as jnp
from jax import lax
from jax.experimental import pallas as pl
from jax.experimental.pallas import tpu as pltpu
from jax.sharding import PartitionSpec as P

VMEM_BYTES = 40 * 1024 * 1024
STAT_ROWS = 16
CHUNK = 4


def exchange(value, even_bit, odd_bit):
    blocks = lax.axis_size("blk")
    cores = lax.axis_size("heads")
    pairs = [
        (b * cores + c, (b ^ (odd_bit if c % 2 else even_bit)) * cores + c)
        for b in range(blocks)
        for c in range(cores)
    ]
    return lax.ppermute(value, ("blk", "heads"), pairs)


def loop(count, body):
    if count <= 4:
        for i in range(count):
            body(i)
    else:
        lax.fori_loop(0, count, lambda i, carry: (body(i), carry)[1], 0)


def spread_rows(qheads, lanes):
    sub = lax.broadcasted_iota(jnp.int32, (qheads, lanes), 0)
    lane = lax.broadcasted_iota(jnp.int32, (qheads, lanes), 1)
    return sub == lane


def to_row(column, diagonal):
    return jnp.sum(jnp.where(diagonal, column, 0.0), axis=0, keepdims=True)


def to_column(row, diagonal):
    return jnp.sum(jnp.where(diagonal, row, 0.0), axis=1, keepdims=True)


def split(value):
    high = value.astype(jnp.bfloat16).astype(jnp.float32)
    return high, (value - high).astype(jnp.bfloat16).astype(jnp.float32)


def stat_block(top_row, total_row):
    top_high, top_low = split(top_row)
    total_high, total_low = split(total_row)
    blank = jnp.zeros((STAT_ROWS - 4, top_row.shape[1]), jnp.float32)
    return jnp.concatenate([top_high, top_low, total_high, total_low, blank], axis=0)


def suffix_rows(bulk_ref, start, slots, page_rows):
    return jnp.concatenate(
        [bulk_ref[start + s * 2 * page_rows : start + s * 2 * page_rows + page_rows] for s in range(slots)],
        axis=0,
    )


def attend(query, bulk_ref, bias, sizes):
    kv_heads, group, prefix_rows, slots, page_rows, scale = sizes
    rows = query.shape[0]
    qheads = kv_heads * group
    suffix_count = slots * page_rows
    key = bulk_ref[0:prefix_rows]
    value = bulk_ref[prefix_rows : 2 * prefix_rows]
    page_key = suffix_rows(bulk_ref, 2 * prefix_rows, slots, page_rows)
    page_value = suffix_rows(bulk_ref, 2 * prefix_rows + page_rows, slots, page_rows)
    contract = (((1,), (1,)), ((), ()))
    near = lax.dot_general(query, key, contract, preferred_element_type=jnp.float32)
    page = lax.dot_general(query, page_key, contract, preferred_element_type=jnp.float32)

    def own_head(width):
        row = lax.broadcasted_iota(jnp.int32, (rows, width), 0)
        column = lax.broadcasted_iota(jnp.int32, (rows, width), 1)
        return (row % qheads) // group == column % kv_heads

    near = jnp.where(own_head(prefix_rows), near, -jnp.inf)
    page = jnp.where(own_head(suffix_count), page, -jnp.inf) + bias
    top = jnp.maximum(
        jnp.max(near, axis=1, keepdims=True), jnp.max(page, axis=1, keepdims=True)
    )
    near = jnp.exp2((near - top) * scale)
    page = jnp.exp2((page - top) * scale)
    total = jnp.sum(near, axis=1, keepdims=True) + jnp.sum(page, axis=1, keepdims=True)
    mixed = jnp.dot(near.astype(jnp.bfloat16), value, preferred_element_type=jnp.float32)
    mixed = mixed + jnp.dot(
        page.astype(jnp.bfloat16), page_value, preferred_element_type=jnp.float32
    )
    return top, total, mixed


def chunk_bias(bias_ref, first, count, qheads):
    return jnp.concatenate(
        [
            jnp.broadcast_to(bias_ref[pl.ds(first + j, 1), :], (qheads, bias_ref.shape[1]))
            for j in range(count)
        ],
        axis=0,
    )


def bias_kernel(
    place_ref, owner_ref, slot_ref, len_ref, request_ref, near_ref, far_ref, *, rows_dev, page_len, kv_heads, blocks
):
    row_total = near_ref.shape[0]
    width = near_ref.shape[1]
    me, query_bit, key_bit = place_ref[0], place_ref[1], place_ref[2]
    all_rows = request_ref.shape[0]
    column = lax.broadcasted_iota(jnp.int32, (1, width), 1)

    def one(i):
        place = i // rows_dev
        device = me ^ jnp.where(place % 2 == 1, query_bit, 0) ^ ((place // 2) * 4)
        row = device * rows_dev + i % rows_dev
        request = request_ref[row]

        def count(j, later):
            return later + jnp.where((request_ref[j] == request) & (j > row), 1, 0)

        if all_rows <= 16:
            later = jnp.int32(0)
            for j in range(all_rows):
                later = count(j, later)
        else:
            later = lax.fori_loop(0, all_rows, count, jnp.int32(0))
        limit = len_ref[request] - later
        for holder, out_ref in ((me, near_ref), (me ^ key_bit, far_ref)):
            page = lax.rem(holder - owner_ref[request, 0] + blocks, blocks)
            shown = jnp.clip(limit - page * page_len, 0, page_len) * kv_heads
            first = slot_ref[request, page] * (page_len * kv_heads)
            out_ref[pl.ds(i, 1), :] = jnp.where(
                (column >= first) & (column < first + shown), 0.0, -jnp.inf
            )

    loop(row_total, one)


def near_kernel(first_ref, second_ref, bulk_ref, bias_ref, mixed_ref, top_ref, total_ref, *, sizes):
    half, qheads, head_dim = first_ref.shape
    chunk = min(CHUNK, half * 2)
    part = chunk // 2

    def one(i):
        base = i * part
        query = jnp.concatenate(
            [
                first_ref[pl.ds(base, part)].reshape(part * qheads, head_dim),
                second_ref[pl.ds(base, part)].reshape(part * qheads, head_dim),
            ],
            axis=0,
        )
        bias = jnp.concatenate(
            [
                chunk_bias(bias_ref, base, part, qheads),
                chunk_bias(bias_ref, half + base, part, qheads),
            ],
            axis=0,
        )
        top, total, mixed = attend(query, bulk_ref, bias, sizes)
        mixed_ref[i] = mixed
        top_ref[i] = jnp.broadcast_to(top, mixed.shape)
        total_ref[i] = jnp.broadcast_to(total, mixed.shape)

    loop(half // part, one)


def far_kernel(
    first_ref, second_ref, bulk_ref, bias_ref, mixed_ref, top_ref, total_ref,
    send_ref, keep_ref, stat_ref, *, sizes,
):
    half, qheads, head_dim = first_ref.shape
    scale = sizes[-1]
    chunk = min(CHUNK, half * 2)
    part = chunk // 2
    diagonal = spread_rows(qheads, head_dim)

    def one(i):
        base = i * part
        query = jnp.concatenate(
            [
                first_ref[pl.ds(base, part)].reshape(part * qheads, head_dim),
                second_ref[pl.ds(base, part)].reshape(part * qheads, head_dim),
            ],
            axis=0,
        )
        bias = jnp.concatenate(
            [
                chunk_bias(bias_ref, base, part, qheads),
                chunk_bias(bias_ref, half + base, part, qheads),
            ],
            axis=0,
        )
        top, total, mixed = attend(query, bulk_ref, bias, sizes)
        near_top = top_ref[i][:, :1]
        high, low = split(jnp.maximum(near_top, top))
        point = high + low
        near_scale = jnp.exp2((near_top - point) * scale)
        far_scale = jnp.exp2((top - point) * scale)
        total = total_ref[i][:, :1] * near_scale + total * far_scale
        mixed = (mixed_ref[i] * near_scale + mixed * far_scale) / total
        for j in range(part):
            rows = slice(j * qheads, (j + 1) * qheads)
            keep_ref[base + j] = mixed[rows]
            stat_ref[base + j, 0:1] = to_row(point[rows], diagonal)
            stat_ref[base + j, 1:2] = to_row(total[rows], diagonal)
            rows = slice((part + j) * qheads, (part + j + 1) * qheads)
            stats = stat_block(to_row(point[rows], diagonal), to_row(total[rows], diagonal))
            send_ref[base + j] = jnp.concatenate([mixed[rows], stats], axis=0).astype(jnp.bfloat16)

    loop(half // part, one)


def merge_rows(keep, top, total, parcel, qheads, diagonal, scale):
    stats = parcel[qheads:]
    other_top = stats[0:1] + stats[1:2]
    other_total = stats[2:3] + stats[3:4]
    point = jnp.maximum(top, other_top)
    own = total * jnp.exp2((top - point) * scale)
    other = other_total * jnp.exp2((other_top - point) * scale)
    total = own + other
    weight = to_column(other / total, diagonal)
    return keep + (parcel[:qheads] - keep) * weight, point, total


def merge_kernel(keep_in, stat_in, parcel_ref, send_ref, keep_ref, stat_ref, *, scale):
    count, qheads, head_dim = keep_in.shape
    diagonal = spread_rows(qheads, head_dim)
    half = count // 2

    def merged(i):
        return merge_rows(
            keep_in[i], stat_in[i, 0:1], stat_in[i, 1:2], parcel_ref[i].astype(jnp.float32),
            qheads, diagonal, scale,
        )

    def one(i):
        mixed, top, total = merged(half + i)
        send_ref[i] = jnp.concatenate([mixed, stat_block(top, total)], axis=0).astype(jnp.bfloat16)
        keep_ref[i], stat_ref[i, 0:1], stat_ref[i, 1:2] = merged(i)

    loop(half, one)


def last_kernel(keep_in, stat_in, parcel_ref, out_ref, *, scale):
    count, qheads, head_dim = keep_in.shape
    diagonal = spread_rows(qheads, head_dim)

    def one(i):
        mixed, _, _ = merge_rows(
            keep_in[i], stat_in[i, 0:1], stat_in[i, 1:2], parcel_ref[i].astype(jnp.float32),
            qheads, diagonal, scale,
        )
        out_ref[i] = mixed.astype(out_ref.dtype)

    loop(count, one)


def call(kernel, outs, operands, scalars=0, **static):
    return pl.pallas_call(
        functools.partial(kernel, **static),
        out_shape=outs,
        in_specs=[pl.BlockSpec(memory_space=pltpu.SMEM)] * scalars
        + [pl.BlockSpec(memory_space=pltpu.VMEM)] * (len(operands) - scalars),
        compiler_params=pltpu.CompilerParams(vmem_limit_bytes=VMEM_BYTES),
    )(*operands)


def on_device(
    queries, prefix_keys, prefix_values, suffix_pool, page_owner, page_slot, suffix_len, row_request
):
    blocks = lax.axis_size("blk")
    me = lax.axis_index("blk")
    odd_core = lax.axis_index("heads") % 2
    rows_dev, qheads, head_dim = queries.shape
    slots, _, page_len, kv_heads, _ = suffix_pool.shape
    prefix_rows = prefix_keys.shape[0] * kv_heads
    page_rows = page_len * kv_heads
    scale = math.log2(math.e) / math.sqrt(head_dim)
    sizes = (kv_heads, qheads // kv_heads, prefix_rows, slots, page_rows, scale)
    shared_bits = [1 << b for b in range(2, blocks.bit_length() - 1)]

    bulk = jnp.concatenate(
        [
            prefix_keys.reshape(prefix_rows, head_dim),
            prefix_values.reshape(prefix_rows, head_dim),
            suffix_pool.reshape(slots * 2 * page_rows, head_dim),
        ],
        axis=0,
    )
    far_bulk = exchange(bulk, 2, 1)
    first = queries
    second = exchange(first, 1, 2)
    for bit in shared_bits:
        first = jnp.concatenate([first, second], axis=0)
        second = exchange(first, bit, bit)
    half = first.shape[0]
    rows = 2 * half

    place = jnp.stack([me, 1 + odd_core, 2 - odd_core]).astype(jnp.int32)
    table = jax.ShapeDtypeStruct((rows, slots * page_rows), jnp.float32)
    near_bias, far_bias = call(
        bias_kernel, (table, table), (place, page_owner, page_slot, suffix_len, row_request), 5,
        rows_dev=rows_dev, page_len=page_len, kv_heads=kv_heads, blocks=blocks,
    )
    chunk = min(CHUNK, rows)
    block = jax.ShapeDtypeStruct((rows // chunk, chunk * qheads, head_dim), jnp.float32)
    near = call(
        near_kernel, (block, block, block), (first, second, bulk, near_bias), sizes=sizes
    )

    def parcel(count):
        return (
            jax.ShapeDtypeStruct((count, qheads + STAT_ROWS, head_dim), jnp.bfloat16),
            jax.ShapeDtypeStruct((count, qheads, head_dim), jnp.float32),
            jax.ShapeDtypeStruct((count, 8, head_dim), jnp.float32),
        )

    send, keep, stats = call(
        far_kernel, parcel(half), (first, second, far_bulk, far_bias, *near), sizes=sizes
    )
    for bit in reversed(shared_bits):
        arrived = exchange(send, bit, bit)
        half //= 2
        send, keep, stats = call(merge_kernel, parcel(half), (keep, stats, arrived), scale=scale)
    arrived = exchange(send, 1, 2)
    return call(
        last_kernel, jax.ShapeDtypeStruct(queries.shape, queries.dtype), (keep, stats, arrived),
        scale=scale,
    )


def solution(mesh):
    placed = (
        P(("groups", "blk"), "heads", None),
        P(("groups", "blk"), "heads", None),
        P(("groups", "blk"), "heads", None),
        P(("groups", "blk"), None, None, "heads", None),
        P("groups", None),
        P("groups", None),
        P("groups"),
        P("groups"),
    )
    return jax.shard_map(
        on_device,
        mesh=mesh,
        in_specs=placed,
        out_specs=P(("groups", "blk"), "heads", None),
        check_vma=False,
    )
```

```python
import functools
import math

import jax
import jax.numpy as jnp
from jax import lax
from jax.experimental import pallas as pl
from jax.experimental.pallas import tpu as pltpu
from jax.sharding import PartitionSpec as P

VMEM_BYTES = 40 * 1024 * 1024
STAT_ROWS = 16
CHUNK = 4


def exchange(value, even_bit, odd_bit):
    blocks = lax.axis_size("blk")
    cores = lax.axis_size("heads")
    pairs = [
        (b * cores + c, (b ^ (odd_bit if c % 2 else even_bit)) * cores + c)
        for b in range(blocks)
        for c in range(cores)
    ]
    return lax.ppermute(value, ("blk", "heads"), pairs)


def loop(count, body):
    if count <= 4:
        for i in range(count):
            body(i)
    else:
        lax.fori_loop(0, count, lambda i, carry: (body(i), carry)[1], 0)


def spread_rows(qheads, lanes):
    sub = lax.broadcasted_iota(jnp.int32, (qheads, lanes), 0)
    lane = lax.broadcasted_iota(jnp.int32, (qheads, lanes), 1)
    return sub == lane


def to_row(column, diagonal):
    return jnp.sum(jnp.where(diagonal, column, 0.0), axis=0, keepdims=True)


def to_column(row, diagonal):
    return jnp.sum(jnp.where(diagonal, row, 0.0), axis=1, keepdims=True)


def split(value):
    high = value.astype(jnp.bfloat16).astype(jnp.float32)
    return high, (value - high).astype(jnp.bfloat16).astype(jnp.float32)


def stat_block(top_row, total_row):
    top_high, top_low = split(top_row)
    total_high, total_low = split(total_row)
    blank = jnp.zeros((STAT_ROWS - 4, top_row.shape[1]), jnp.float32)
    return jnp.concatenate([top_high, top_low, total_high, total_low, blank], axis=0)


def suffix_rows(bulk_ref, start, slots, page_rows):
    return jnp.concatenate(
        [bulk_ref[start + s * 2 * page_rows : start + s * 2 * page_rows + page_rows] for s in range(slots)],
        axis=0,
    )


def attend(query, bulk_ref, bias, sizes):
    kv_heads, group, prefix_rows, slots, page_rows, scale = sizes
    rows = query.shape[0]
    qheads = kv_heads * group
    suffix_count = slots * page_rows
    key = bulk_ref[0:prefix_rows]
    value = bulk_ref[prefix_rows : 2 * prefix_rows]
    page_key = suffix_rows(bulk_ref, 2 * prefix_rows, slots, page_rows)
    page_value = suffix_rows(bulk_ref, 2 * prefix_rows + page_rows, slots, page_rows)
    contract = (((1,), (1,)), ((), ()))
    near = lax.dot_general(query, key, contract, preferred_element_type=jnp.float32)
    page = lax.dot_general(query, page_key, contract, preferred_element_type=jnp.float32)

    def own_head(width):
        row = lax.broadcasted_iota(jnp.int32, (rows, width), 0)
        column = lax.broadcasted_iota(jnp.int32, (rows, width), 1)
        return (row % qheads) // group == column % kv_heads

    near = jnp.where(own_head(prefix_rows), near, -jnp.inf)
    page = jnp.where(own_head(suffix_count), page, -jnp.inf) + bias
    top = jnp.maximum(
        jnp.max(near, axis=1, keepdims=True), jnp.max(page, axis=1, keepdims=True)
    )
    near = jnp.exp2((near - top) * scale)
    page = jnp.exp2((page - top) * scale)
    total = jnp.sum(near, axis=1, keepdims=True) + jnp.sum(page, axis=1, keepdims=True)
    mixed = jnp.dot(near.astype(jnp.bfloat16), value, preferred_element_type=jnp.float32)
    mixed = mixed + jnp.dot(
        page.astype(jnp.bfloat16), page_value, preferred_element_type=jnp.float32
    )
    return top, total, mixed


def chunk_bias(bias_ref, first, count, qheads):
    return jnp.concatenate(
        [
            jnp.broadcast_to(bias_ref[pl.ds(first + j, 1), :], (qheads, bias_ref.shape[1]))
            for j in range(count)
        ],
        axis=0,
    )


def bias_kernel(
    place_ref, owner_ref, slot_ref, len_ref, request_ref, near_ref, far_ref, *, rows_dev, page_len, kv_heads, blocks
):
    row_total = near_ref.shape[0]
    width = near_ref.shape[1]
    me, query_bit, key_bit = place_ref[0], place_ref[1], place_ref[2]
    all_rows = request_ref.shape[0]
    column = lax.broadcasted_iota(jnp.int32, (1, width), 1)

    def one(i):
        place = i // rows_dev
        device = me ^ jnp.where(place % 2 == 1, query_bit, 0) ^ ((place // 2) * 4)
        row = device * rows_dev + i % rows_dev
        request = request_ref[row]

        def count(j, later):
            return later + jnp.where((request_ref[j] == request) & (j > row), 1, 0)

        if all_rows <= 16:
            later = jnp.int32(0)
            for j in range(all_rows):
                later = count(j, later)
        else:
            later = lax.fori_loop(0, all_rows, count, jnp.int32(0))
        limit = len_ref[request] - later
        for holder, out_ref in ((me, near_ref), (me ^ key_bit, far_ref)):
            page = lax.rem(holder - owner_ref[request, 0] + blocks, blocks)
            shown = jnp.clip(limit - page * page_len, 0, page_len) * kv_heads
            first = slot_ref[request, page] * (page_len * kv_heads)
            out_ref[pl.ds(i, 1), :] = jnp.where(
                (column >= first) & (column < first + shown), 0.0, -jnp.inf
            )

    loop(row_total, one)


def near_kernel(first_ref, second_ref, bulk_ref, bias_ref, mixed_ref, top_ref, total_ref, *, sizes):
    half, qheads, head_dim = first_ref.shape
    chunk = min(CHUNK, half * 2)
    part = chunk // 2

    def one(i):
        base = i * part
        query = jnp.concatenate(
            [
                first_ref[pl.ds(base, part)].reshape(part * qheads, head_dim),
                second_ref[pl.ds(base, part)].reshape(part * qheads, head_dim),
            ],
            axis=0,
        )
        bias = jnp.concatenate(
            [
                chunk_bias(bias_ref, base, part, qheads),
                chunk_bias(bias_ref, half + base, part, qheads),
            ],
            axis=0,
        )
        top, total, mixed = attend(query, bulk_ref, bias, sizes)
        mixed_ref[i] = mixed
        top_ref[i] = jnp.broadcast_to(top, mixed.shape)
        total_ref[i] = jnp.broadcast_to(total, mixed.shape)

    loop(half // part, one)


def far_kernel(
    first_ref, second_ref, bulk_ref, bias_ref, mixed_ref, top_ref, total_ref,
    send_ref, keep_ref, stat_ref, *, sizes,
):
    half, qheads, head_dim = first_ref.shape
    scale = sizes[-1]
    chunk = min(CHUNK, half * 2)
    part = chunk // 2
    diagonal = spread_rows(qheads, head_dim)

    def one(i):
        base = i * part
        query = jnp.concatenate(
            [
                first_ref[pl.ds(base, part)].reshape(part * qheads, head_dim),
                second_ref[pl.ds(base, part)].reshape(part * qheads, head_dim),
            ],
            axis=0,
        )
        bias = jnp.concatenate(
            [
                chunk_bias(bias_ref, base, part, qheads),
                chunk_bias(bias_ref, half + base, part, qheads),
            ],
            axis=0,
        )
        top, total, mixed = attend(query, bulk_ref, bias, sizes)
        near_top = top_ref[i][:, :1]
        high, low = split(jnp.maximum(near_top, top))
        point = high + low
        near_scale = jnp.exp2((near_top - point) * scale)
        far_scale = jnp.exp2((top - point) * scale)
        total = total_ref[i][:, :1] * near_scale + total * far_scale
        mixed = (mixed_ref[i] * near_scale + mixed * far_scale) / total
        for j in range(part):
            rows = slice(j * qheads, (j + 1) * qheads)
            keep_ref[base + j] = mixed[rows]
            stat_ref[base + j, 0:1] = to_row(point[rows], diagonal)
            stat_ref[base + j, 1:2] = to_row(total[rows], diagonal)
            rows = slice((part + j) * qheads, (part + j + 1) * qheads)
            stats = stat_block(to_row(point[rows], diagonal), to_row(total[rows], diagonal))
            send_ref[base + j] = jnp.concatenate([mixed[rows], stats], axis=0).astype(jnp.bfloat16)

    loop(half // part, one)


def merge_rows(keep, top, total, parcel, qheads, diagonal, scale):
    stats = parcel[qheads:]
    other_top = stats[0:1] + stats[1:2]
    other_total = stats[2:3] + stats[3:4]
    point = jnp.maximum(top, other_top)
    own = total * jnp.exp2((top - point) * scale)
    other = other_total * jnp.exp2((other_top - point) * scale)
    total = own + other
    weight = to_column(other / total, diagonal)
    return keep + (parcel[:qheads] - keep) * weight, point, total


def merge_kernel(keep_in, stat_in, parcel_ref, send_ref, keep_ref, stat_ref, *, scale):
    count, qheads, head_dim = keep_in.shape
    diagonal = spread_rows(qheads, head_dim)
    half = count // 2

    def merged(i):
        return merge_rows(
            keep_in[i], stat_in[i, 0:1], stat_in[i, 1:2], parcel_ref[i].astype(jnp.float32),
            qheads, diagonal, scale,
        )

    def one(i):
        mixed, top, total = merged(half + i)
        send_ref[i] = jnp.concatenate([mixed, stat_block(top, total)], axis=0).astype(jnp.bfloat16)
        keep_ref[i], stat_ref[i, 0:1], stat_ref[i, 1:2] = merged(i)

    loop(half, one)


def last_kernel(keep_in, stat_in, parcel_ref, out_ref, *, scale):
    count, qheads, head_dim = keep_in.shape
    diagonal = spread_rows(qheads, head_dim)

    def one(i):
        mixed, _, _ = merge_rows(
            keep_in[i], stat_in[i, 0:1], stat_in[i, 1:2], parcel_ref[i].astype(jnp.float32),
            qheads, diagonal, scale,
        )
        out_ref[i] = mixed.astype(out_ref.dtype)

    loop(count, one)


def call(kernel, outs, operands, scalars=0, **static):
    return pl.pallas_call(
        functools.partial(kernel, **static),
        out_shape=outs,
        in_specs=[pl.BlockSpec(memory_space=pltpu.SMEM)] * scalars
        + [pl.BlockSpec(memory_space=pltpu.VMEM)] * (len(operands) - scalars),
        compiler_params=pltpu.CompilerParams(vmem_limit_bytes=VMEM_BYTES),
    )(*operands)


def on_device(
    queries, prefix_keys, prefix_values, suffix_pool, page_owner, page_slot, suffix_len, row_request
):
    blocks = lax.axis_size("blk")
    me = lax.axis_index("blk")
    odd_core = lax.axis_index("heads") % 2
    rows_dev, qheads, head_dim = queries.shape
    slots, _, page_len, kv_heads, _ = suffix_pool.shape
    prefix_rows = prefix_keys.shape[0] * kv_heads
    page_rows = page_len * kv_heads
    scale = math.log2(math.e) / math.sqrt(head_dim)
    sizes = (kv_heads, qheads // kv_heads, prefix_rows, slots, page_rows, scale)
    shared_bits = [1 << b for b in range(2, blocks.bit_length() - 1)]

    bulk = jnp.concatenate(
        [
            prefix_keys.reshape(prefix_rows, head_dim),
            prefix_values.reshape(prefix_rows, head_dim),
            suffix_pool.reshape(slots * 2 * page_rows, head_dim),
        ],
        axis=0,
    )
    far_bulk = exchange(bulk, 1, 2)
    first = queries
    second = exchange(first, 2, 1)
    for bit in shared_bits:
        first = jnp.concatenate([first, second], axis=0)
        second = exchange(first, bit, bit)
    half = first.shape[0]
    rows = 2 * half

    place = jnp.stack([me, 2 - odd_core, 1 + odd_core]).astype(jnp.int32)
    table = jax.ShapeDtypeStruct((rows, slots * page_rows), jnp.float32)
    near_bias, far_bias = call(
        bias_kernel, (table, table), (place, page_owner, page_slot, suffix_len, row_request), 5,
        rows_dev=rows_dev, page_len=page_len, kv_heads=kv_heads, blocks=blocks,
    )
    chunk = min(CHUNK, rows)
    block = jax.ShapeDtypeStruct((rows // chunk, chunk * qheads, head_dim), jnp.float32)
    near = call(
        near_kernel, (block, block, block), (first, second, bulk, near_bias), sizes=sizes
    )

    def parcel(count):
        return (
            jax.ShapeDtypeStruct((count, qheads + STAT_ROWS, head_dim), jnp.bfloat16),
            jax.ShapeDtypeStruct((count, qheads, head_dim), jnp.float32),
            jax.ShapeDtypeStruct((count, 8, head_dim), jnp.float32),
        )

    send, keep, stats = call(
        far_kernel, parcel(half), (first, second, far_bulk, far_bias, *near), sizes=sizes
    )
    for bit in reversed(shared_bits):
        arrived = exchange(send, bit, bit)
        half //= 2
        send, keep, stats = call(merge_kernel, parcel(half), (keep, stats, arrived), scale=scale)
    arrived = exchange(send, 2, 1)
    return call(
        last_kernel, jax.ShapeDtypeStruct(queries.shape, queries.dtype), (keep, stats, arrived),
        scale=scale,
    )


def solution(mesh):
    placed = (
        P(("groups", "blk"), "heads", None),
        P(("groups", "blk"), "heads", None),
        P(("groups", "blk"), "heads", None),
        P(("groups", "blk"), None, None, "heads", None),
        P("groups", None),
        P("groups", None),
        P("groups"),
        P("groups"),
    )
    return jax.shard_map(
        on_device,
        mesh=mesh,
        in_specs=placed,
        out_specs=P(("groups", "blk"), "heads", None),
        check_vma=False,
    )
```

```python
import functools
import math

import jax
import jax.numpy as jnp
from jax import lax
from jax.experimental import pallas as pl
from jax.experimental.pallas import tpu as pltpu
from jax.sharding import PartitionSpec as P

VMEM_BYTES = 40 * 1024 * 1024
STAT_ROWS = 16
CHUNK = 4


def exchange(value, even_bit, odd_bit):
    blocks = lax.axis_size("blk")
    cores = lax.axis_size("heads")
    pairs = [
        (b * cores + c, (b ^ (odd_bit if c % 2 else even_bit)) * cores + c)
        for b in range(blocks)
        for c in range(cores)
    ]
    return lax.ppermute(value, ("blk", "heads"), pairs)


def loop(count, body):
    if count <= 4:
        for i in range(count):
            body(i)
    else:
        lax.fori_loop(0, count, lambda i, carry: (body(i), carry)[1], 0)


def spread_rows(qheads, lanes):
    sub = lax.broadcasted_iota(jnp.int32, (qheads, lanes), 0)
    lane = lax.broadcasted_iota(jnp.int32, (qheads, lanes), 1)
    return sub == lane


def to_row(column, diagonal):
    return jnp.sum(jnp.where(diagonal, column, 0.0), axis=0, keepdims=True)


def to_column(row, diagonal):
    return jnp.sum(jnp.where(diagonal, row, 0.0), axis=1, keepdims=True)


def split(value):
    high = value.astype(jnp.bfloat16).astype(jnp.float32)
    return high, (value - high).astype(jnp.bfloat16).astype(jnp.float32)


def stat_block(top_row, total_row):
    top_high, top_low = split(top_row)
    total_high, total_low = split(total_row)
    blank = jnp.zeros((STAT_ROWS - 4, top_row.shape[1]), jnp.float32)
    return jnp.concatenate([top_high, top_low, total_high, total_low, blank], axis=0)


def suffix_rows(bulk_ref, start, slots, page_rows):
    return jnp.concatenate(
        [bulk_ref[start + s * 2 * page_rows : start + s * 2 * page_rows + page_rows] for s in range(slots)],
        axis=0,
    )


def attend(query, bulk_ref, bias, sizes):
    kv_heads, group, prefix_rows, slots, page_rows, scale = sizes
    rows = query.shape[0]
    qheads = kv_heads * group
    suffix_count = slots * page_rows
    key = bulk_ref[0:prefix_rows]
    value = bulk_ref[prefix_rows : 2 * prefix_rows]
    page_key = suffix_rows(bulk_ref, 2 * prefix_rows, slots, page_rows)
    page_value = suffix_rows(bulk_ref, 2 * prefix_rows + page_rows, slots, page_rows)
    contract = (((1,), (1,)), ((), ()))
    near = lax.dot_general(query, key, contract, preferred_element_type=jnp.float32)
    page = lax.dot_general(query, page_key, contract, preferred_element_type=jnp.float32)

    def own_head(width):
        row = lax.broadcasted_iota(jnp.int32, (rows, width), 0)
        column = lax.broadcasted_iota(jnp.int32, (rows, width), 1)
        return (row % qheads) // group == column % kv_heads

    near = jnp.where(own_head(prefix_rows), near, -jnp.inf)
    page = jnp.where(own_head(suffix_count), page, -jnp.inf) + bias
    top = jnp.maximum(
        jnp.max(near, axis=1, keepdims=True), jnp.max(page, axis=1, keepdims=True)
    )
    near = jnp.exp2((near - top) * scale)
    page = jnp.exp2((page - top) * scale)
    total = jnp.sum(near, axis=1, keepdims=True) + jnp.sum(page, axis=1, keepdims=True)
    mixed = jnp.dot(near.astype(jnp.bfloat16), value, preferred_element_type=jnp.float32)
    mixed = mixed + jnp.dot(
        page.astype(jnp.bfloat16), page_value, preferred_element_type=jnp.float32
    )
    return top, total, mixed


def chunk_bias(bias_ref, first, count, qheads):
    return jnp.concatenate(
        [
            jnp.broadcast_to(bias_ref[pl.ds(first + j, 1), :], (qheads, bias_ref.shape[1]))
            for j in range(count)
        ],
        axis=0,
    )


def pack_kernel(key_ref, value_ref, pool_ref, bulk_ref, sems):
    start = 0
    copies = []
    for i, source in enumerate((key_ref, value_ref, pool_ref)):
        rows = source.shape[0]
        copies.append(pltpu.make_async_copy(source, bulk_ref.at[start : start + rows], sems.at[i]))
        start += rows
    for copy in copies:
        copy.start()
    for copy in copies:
        copy.wait()


def pack(*sources):
    rows = sum(source.shape[0] for source in sources)
    return pl.pallas_call(
        pack_kernel,
        out_shape=jax.ShapeDtypeStruct((rows, sources[0].shape[1]), sources[0].dtype),
        in_specs=[pl.BlockSpec(memory_space=pltpu.HBM)] * len(sources),
        out_specs=pl.BlockSpec(memory_space=pltpu.VMEM),
        scratch_shapes=[pltpu.SemaphoreType.DMA((len(sources),))],
        compiler_params=pltpu.CompilerParams(vmem_limit_bytes=VMEM_BYTES),
    )(*(pltpu.with_memory_space_constraint(source, pltpu.HBM) for source in sources))


def bias_kernel(
    place_ref, owner_ref, slot_ref, len_ref, request_ref, near_ref, far_ref, *, rows_dev, page_len, kv_heads, blocks
):
    row_total = near_ref.shape[0]
    width = near_ref.shape[1]
    me, query_bit, key_bit = place_ref[0], place_ref[1], place_ref[2]
    all_rows = request_ref.shape[0]
    column = lax.broadcasted_iota(jnp.int32, (1, width), 1)

    def one(i):
        place = i // rows_dev
        device = me ^ jnp.where(place % 2 == 1, query_bit, 0) ^ ((place // 2) * 4)
        row = device * rows_dev + i % rows_dev
        request = request_ref[row]

        def count(j, later):
            return later + jnp.where((request_ref[j] == request) & (j > row), 1, 0)

        if all_rows <= 16:
            later = jnp.int32(0)
            for j in range(all_rows):
                later = count(j, later)
        else:
            later = lax.fori_loop(0, all_rows, count, jnp.int32(0))
        limit = len_ref[request] - later
        for holder, out_ref in ((me, near_ref), (me ^ key_bit, far_ref)):
            page = lax.rem(holder - owner_ref[request, 0] + blocks, blocks)
            shown = jnp.clip(limit - page * page_len, 0, page_len) * kv_heads
            first = slot_ref[request, page] * (page_len * kv_heads)
            out_ref[pl.ds(i, 1), :] = jnp.where(
                (column >= first) & (column < first + shown), 0.0, -jnp.inf
            )

    loop(row_total, one)


def chunks(query_ref):
    count, qheads, head_dim = query_ref.shape
    chunk = min(CHUNK, count)

    def load(i, bias_ref, offset):
        query = query_ref[pl.ds(i * chunk, chunk)].reshape(chunk * qheads, head_dim)
        return query, chunk_bias(bias_ref, offset + i * chunk, chunk, qheads)

    return chunk, count // chunk, load


def near_kernel(query_ref, bulk_ref, bias_ref, mixed_ref, top_ref, total_ref, *, offset, sizes):
    _, steps, load = chunks(query_ref)

    def one(i):
        query, bias = load(i, bias_ref, offset)
        top, total, mixed = attend(query, bulk_ref, bias, sizes)
        mixed_ref[i] = mixed
        top_ref[i] = jnp.broadcast_to(top, mixed.shape)
        total_ref[i] = jnp.broadcast_to(total, mixed.shape)

    loop(steps, one)


def far_kernel(
    query_ref, bulk_ref, bias_ref, mixed_ref, top_ref, total_ref, *out_refs, offset, sizes
):
    _, qheads, head_dim = query_ref.shape
    scale = sizes[-1]
    chunk, steps, load = chunks(query_ref)
    diagonal = spread_rows(qheads, head_dim)

    def one(i):
        query, bias = load(i, bias_ref, offset)
        top, total, mixed = attend(query, bulk_ref, bias, sizes)
        near_top = top_ref[i][:, :1]
        high, low = split(jnp.maximum(near_top, top))
        point = high + low
        near_scale = jnp.exp2((near_top - point) * scale)
        far_scale = jnp.exp2((top - point) * scale)
        total = total_ref[i][:, :1] * near_scale + total * far_scale
        mixed = (mixed_ref[i] * near_scale + mixed * far_scale) / total
        for j in range(chunk):
            rows = slice(j * qheads, (j + 1) * qheads)
            place = i * chunk + j
            point_row = to_row(point[rows], diagonal)
            total_row = to_row(total[rows], diagonal)
            if len(out_refs) == 1:
                (send_ref,) = out_refs
                stats = stat_block(point_row, total_row)
                send_ref[place] = jnp.concatenate([mixed[rows], stats], axis=0).astype(jnp.bfloat16)
            else:
                keep_ref, stat_ref = out_refs
                keep_ref[place] = mixed[rows]
                stat_ref[place, 0:1] = point_row
                stat_ref[place, 1:2] = total_row

    loop(steps, one)


def merge_rows(keep, top, total, parcel, qheads, diagonal, scale):
    stats = parcel[qheads:]
    other_top = stats[0:1] + stats[1:2]
    other_total = stats[2:3] + stats[3:4]
    point = jnp.maximum(top, other_top)
    own = total * jnp.exp2((top - point) * scale)
    other = other_total * jnp.exp2((other_top - point) * scale)
    total = own + other
    weight = to_column(other / total, diagonal)
    return keep + (parcel[:qheads] - keep) * weight, point, total


def merge_kernel(keep_in, stat_in, parcel_ref, send_ref, keep_ref, stat_ref, *, scale):
    count, qheads, head_dim = keep_in.shape
    diagonal = spread_rows(qheads, head_dim)
    half = count // 2

    def merged(i):
        return merge_rows(
            keep_in[i], stat_in[i, 0:1], stat_in[i, 1:2], parcel_ref[i].astype(jnp.float32),
            qheads, diagonal, scale,
        )

    def one(i):
        mixed, top, total = merged(half + i)
        send_ref[i] = jnp.concatenate([mixed, stat_block(top, total)], axis=0).astype(jnp.bfloat16)
        keep_ref[i], stat_ref[i, 0:1], stat_ref[i, 1:2] = merged(i)

    loop(half, one)


def last_kernel(keep_in, stat_in, parcel_ref, out_ref, *, scale):
    count, qheads, head_dim = keep_in.shape
    diagonal = spread_rows(qheads, head_dim)

    def one(i):
        mixed, _, _ = merge_rows(
            keep_in[i], stat_in[i, 0:1], stat_in[i, 1:2], parcel_ref[i].astype(jnp.float32),
            qheads, diagonal, scale,
        )
        out_ref[i] = mixed.astype(out_ref.dtype)

    loop(count, one)


def call(kernel, outs, operands, scalars=0, **static):
    return pl.pallas_call(
        functools.partial(kernel, **static),
        out_shape=outs,
        in_specs=[pl.BlockSpec(memory_space=pltpu.SMEM)] * scalars
        + [pl.BlockSpec(memory_space=pltpu.VMEM)] * (len(operands) - scalars),
        compiler_params=pltpu.CompilerParams(vmem_limit_bytes=VMEM_BYTES),
    )(*operands)


def on_device(
    queries, prefix_keys, prefix_values, suffix_pool, page_owner, page_slot, suffix_len, row_request
):
    blocks = lax.axis_size("blk")
    me = lax.axis_index("blk")
    odd_core = lax.axis_index("heads") % 2
    rows_dev, qheads, head_dim = queries.shape
    slots, _, page_len, kv_heads, _ = suffix_pool.shape
    prefix_rows = prefix_keys.shape[0] * kv_heads
    page_rows = page_len * kv_heads
    scale = math.log2(math.e) / math.sqrt(head_dim)
    sizes = (kv_heads, qheads // kv_heads, prefix_rows, slots, page_rows, scale)
    shared_bits = [1 << b for b in range(2, blocks.bit_length() - 1)]

    bulk = pack(
        prefix_keys.reshape(prefix_rows, head_dim),
        prefix_values.reshape(prefix_rows, head_dim),
        suffix_pool.reshape(slots * 2 * page_rows, head_dim),
    )
    far_bulk = exchange(bulk, 1, 2)
    first = queries
    second = exchange(first, 2, 1)
    for bit in shared_bits:
        first = jnp.concatenate([first, second], axis=0)
        second = exchange(first, bit, bit)
    half = first.shape[0]
    rows = 2 * half

    place = jnp.stack([me, 2 - odd_core, 1 + odd_core]).astype(jnp.int32)
    table = jax.ShapeDtypeStruct((rows, slots * page_rows), jnp.float32)
    near_bias, far_bias = call(
        bias_kernel, (table, table), (place, page_owner, page_slot, suffix_len, row_request), 5,
        rows_dev=rows_dev, page_len=page_len, kv_heads=kv_heads, blocks=blocks,
    )
    chunk = min(CHUNK, half)
    block = jax.ShapeDtypeStruct((half // chunk, chunk * qheads, head_dim), jnp.float32)
    near = [
        call(
            near_kernel, (block, block, block), (query, bulk, near_bias), offset=offset, sizes=sizes
        )
        for query, offset in ((first, 0), (second, half))
    ]

    def parcel(count):
        return (
            jax.ShapeDtypeStruct((count, qheads + STAT_ROWS, head_dim), jnp.bfloat16),
            jax.ShapeDtypeStruct((count, qheads, head_dim), jnp.float32),
            jax.ShapeDtypeStruct((count, 8, head_dim), jnp.float32),
        )

    outs = parcel(half)
    (send,) = call(
        far_kernel, outs[:1], (second, far_bulk, far_bias, *near[1]), offset=half, sizes=sizes
    )
    keep, stats = call(
        far_kernel, outs[1:], (first, far_bulk, far_bias, *near[0]), offset=0, sizes=sizes
    )
    for bit in reversed(shared_bits):
        arrived = exchange(send, bit, bit)
        half //= 2
        send, keep, stats = call(merge_kernel, parcel(half), (keep, stats, arrived), scale=scale)
    arrived = exchange(send, 2, 1)
    return call(
        last_kernel, jax.ShapeDtypeStruct(queries.shape, queries.dtype), (keep, stats, arrived),
        scale=scale,
    )


def solution(mesh):
    placed = (
        P(("groups", "blk"), "heads", None),
        P(("groups", "blk"), "heads", None),
        P(("groups", "blk"), "heads", None),
        P(("groups", "blk"), None, None, "heads", None),
        P("groups", None),
        P("groups", None),
        P("groups"),
        P("groups"),
    )
    return jax.shard_map(
        on_device,
        mesh=mesh,
        in_specs=placed,
        out_specs=P(("groups", "blk"), "heads", None),
        check_vma=False,
    )
```

```python
import functools
import math

import jax
import jax.numpy as jnp
from jax import lax
from jax.experimental import pallas as pl
from jax.experimental.pallas import tpu as pltpu
from jax.sharding import PartitionSpec as P

VMEM_BYTES = 40 * 1024 * 1024
STAT_ROWS = 16
CHUNK = 4
PACK_BYTES = 4 * 1024 * 1024


def exchange(value, even_bit, odd_bit):
    blocks = lax.axis_size("blk")
    cores = lax.axis_size("heads")
    pairs = [
        (b * cores + c, (b ^ (odd_bit if c % 2 else even_bit)) * cores + c)
        for b in range(blocks)
        for c in range(cores)
    ]
    return lax.ppermute(value, ("blk", "heads"), pairs)


def loop(count, body):
    if count <= 4:
        for i in range(count):
            body(i)
    else:
        lax.fori_loop(0, count, lambda i, carry: (body(i), carry)[1], 0)


def spread_rows(qheads, lanes):
    sub = lax.broadcasted_iota(jnp.int32, (qheads, lanes), 0)
    lane = lax.broadcasted_iota(jnp.int32, (qheads, lanes), 1)
    return sub == lane


def to_row(column, diagonal):
    return jnp.sum(jnp.where(diagonal, column, 0.0), axis=0, keepdims=True)


def to_column(row, diagonal):
    return jnp.sum(jnp.where(diagonal, row, 0.0), axis=1, keepdims=True)


def split(value):
    high = value.astype(jnp.bfloat16).astype(jnp.float32)
    return high, (value - high).astype(jnp.bfloat16).astype(jnp.float32)


def stat_block(top_row, total_row):
    top_high, top_low = split(top_row)
    total_high, total_low = split(total_row)
    blank = jnp.zeros((STAT_ROWS - 4, top_row.shape[1]), jnp.float32)
    return jnp.concatenate([top_high, top_low, total_high, total_low, blank], axis=0)


def suffix_rows(rest_ref, start, slots, page_rows):
    return jnp.concatenate(
        [rest_ref[start + s * 2 * page_rows : start + s * 2 * page_rows + page_rows] for s in range(slots)],
        axis=0,
    )


def attend(query, key_ref, rest_ref, bias, sizes):
    kv_heads, group, prefix_rows, slots, page_rows, scale = sizes
    rows = query.shape[0]
    qheads = kv_heads * group
    suffix_count = slots * page_rows
    key = key_ref[...]
    value = rest_ref[0:prefix_rows]
    page_key = suffix_rows(rest_ref, prefix_rows, slots, page_rows)
    page_value = suffix_rows(rest_ref, prefix_rows + page_rows, slots, page_rows)
    contract = (((1,), (1,)), ((), ()))
    near = lax.dot_general(query, key, contract, preferred_element_type=jnp.float32)
    page = lax.dot_general(query, page_key, contract, preferred_element_type=jnp.float32)

    def own_head(width):
        row = lax.broadcasted_iota(jnp.int32, (rows, width), 0)
        column = lax.broadcasted_iota(jnp.int32, (rows, width), 1)
        return (row % qheads) // group == column % kv_heads

    near = jnp.where(own_head(prefix_rows), near, -jnp.inf)
    page = jnp.where(own_head(suffix_count), page, -jnp.inf) + bias
    top = jnp.maximum(
        jnp.max(near, axis=1, keepdims=True), jnp.max(page, axis=1, keepdims=True)
    )
    near = jnp.exp2((near - top) * scale)
    page = jnp.exp2((page - top) * scale)
    total = jnp.sum(near, axis=1, keepdims=True) + jnp.sum(page, axis=1, keepdims=True)
    mixed = jnp.dot(near.astype(jnp.bfloat16), value, preferred_element_type=jnp.float32)
    mixed = mixed + jnp.dot(
        page.astype(jnp.bfloat16), page_value, preferred_element_type=jnp.float32
    )
    return top, total, mixed


def chunk_bias(bias_ref, first, count, qheads):
    return jnp.concatenate(
        [
            jnp.broadcast_to(bias_ref[pl.ds(first + j, 1), :], (qheads, bias_ref.shape[1]))
            for j in range(count)
        ],
        axis=0,
    )


def pack_kernel(*refs):
    *sources, rest_ref, sems = refs
    start = 0
    copies = []
    for i, source in enumerate(sources):
        rows = source.shape[0]
        copies.append(pltpu.make_async_copy(source, rest_ref.at[start : start + rows], sems.at[i]))
        start += rows
    for copy in copies:
        copy.start()
    for copy in copies:
        copy.wait()


def pack(*sources):
    rows = sum(source.shape[0] for source in sources)
    return pl.pallas_call(
        pack_kernel,
        out_shape=jax.ShapeDtypeStruct((rows, sources[0].shape[1]), sources[0].dtype),
        in_specs=[pl.BlockSpec(memory_space=pltpu.HBM)] * len(sources),
        out_specs=pl.BlockSpec(memory_space=pltpu.VMEM),
        scratch_shapes=[pltpu.SemaphoreType.DMA((len(sources),))],
        compiler_params=pltpu.CompilerParams(vmem_limit_bytes=VMEM_BYTES),
        cost_estimate=pl.CostEstimate(flops=0, bytes_accessed=PACK_BYTES, transcendentals=0),
    )(*(pltpu.with_memory_space_constraint(source, pltpu.HBM) for source in sources))


def bias_kernel(
    place_ref, owner_ref, slot_ref, len_ref, request_ref, near_ref, far_ref, *, rows_dev, page_len, kv_heads, blocks
):
    row_total = near_ref.shape[0]
    width = near_ref.shape[1]
    me, query_bit, key_bit = place_ref[0], place_ref[1], place_ref[2]
    all_rows = request_ref.shape[0]
    column = lax.broadcasted_iota(jnp.int32, (1, width), 1)

    def one(i):
        place = i // rows_dev
        device = me ^ jnp.where(place % 2 == 1, query_bit, 0) ^ ((place // 2) * 4)
        row = device * rows_dev + i % rows_dev
        request = request_ref[row]

        def count(j, later):
            return later + jnp.where((request_ref[j] == request) & (j > row), 1, 0)

        if all_rows <= 16:
            later = jnp.int32(0)
            for j in range(all_rows):
                later = count(j, later)
        else:
            later = lax.fori_loop(0, all_rows, count, jnp.int32(0))
        limit = len_ref[request] - later
        for holder, out_ref in ((me, near_ref), (me ^ key_bit, far_ref)):
            page = lax.rem(holder - owner_ref[request, 0] + blocks, blocks)
            shown = jnp.clip(limit - page * page_len, 0, page_len) * kv_heads
            first = slot_ref[request, page] * (page_len * kv_heads)
            out_ref[pl.ds(i, 1), :] = jnp.where(
                (column >= first) & (column < first + shown), 0.0, -jnp.inf
            )

    loop(row_total, one)


def chunks(query_ref):
    count, qheads, head_dim = query_ref.shape
    chunk = min(CHUNK, count)

    def load(i, bias_ref, offset):
        query = query_ref[pl.ds(i * chunk, chunk)].reshape(chunk * qheads, head_dim)
        return query, chunk_bias(bias_ref, offset + i * chunk, chunk, qheads)

    return chunk, count // chunk, load


def near_kernel(
    query_ref, key_ref, rest_ref, bias_ref, mixed_ref, top_ref, total_ref, *, offset, sizes
):
    _, steps, load = chunks(query_ref)

    def one(i):
        query, bias = load(i, bias_ref, offset)
        top, total, mixed = attend(query, key_ref, rest_ref, bias, sizes)
        mixed_ref[i] = mixed
        top_ref[i] = jnp.broadcast_to(top, mixed.shape)
        total_ref[i] = jnp.broadcast_to(total, mixed.shape)

    loop(steps, one)


def far_kernel(
    query_ref, key_ref, rest_ref, bias_ref, mixed_ref, top_ref, total_ref, *out_refs, offset, sizes
):
    _, qheads, head_dim = query_ref.shape
    scale = sizes[-1]
    chunk, steps, load = chunks(query_ref)
    diagonal = spread_rows(qheads, head_dim)

    def one(i):
        query, bias = load(i, bias_ref, offset)
        top, total, mixed = attend(query, key_ref, rest_ref, bias, sizes)
        near_top = top_ref[i][:, :1]
        high, low = split(jnp.maximum(near_top, top))
        point = high + low
        near_scale = jnp.exp2((near_top - point) * scale)
        far_scale = jnp.exp2((top - point) * scale)
        total = total_ref[i][:, :1] * near_scale + total * far_scale
        mixed = (mixed_ref[i] * near_scale + mixed * far_scale) / total
        for j in range(chunk):
            rows = slice(j * qheads, (j + 1) * qheads)
            place = i * chunk + j
            point_row = to_row(point[rows], diagonal)
            total_row = to_row(total[rows], diagonal)
            if len(out_refs) == 1:
                (send_ref,) = out_refs
                stats = stat_block(point_row, total_row)
                send_ref[place] = jnp.concatenate([mixed[rows], stats], axis=0).astype(jnp.bfloat16)
            else:
                keep_ref, stat_ref = out_refs
                keep_ref[place] = mixed[rows]
                stat_ref[place, 0:1] = point_row
                stat_ref[place, 1:2] = total_row

    loop(steps, one)


def merge_rows(keep, top, total, parcel, qheads, diagonal, scale):
    stats = parcel[qheads:]
    other_top = stats[0:1] + stats[1:2]
    other_total = stats[2:3] + stats[3:4]
    point = jnp.maximum(top, other_top)
    own = total * jnp.exp2((top - point) * scale)
    other = other_total * jnp.exp2((other_top - point) * scale)
    total = own + other
    weight = to_column(other / total, diagonal)
    return keep + (parcel[:qheads] - keep) * weight, point, total


def merge_kernel(keep_in, stat_in, parcel_ref, send_ref, keep_ref, stat_ref, *, scale):
    count, qheads, head_dim = keep_in.shape
    diagonal = spread_rows(qheads, head_dim)
    half = count // 2

    def merged(i):
        return merge_rows(
            keep_in[i], stat_in[i, 0:1], stat_in[i, 1:2], parcel_ref[i].astype(jnp.float32),
            qheads, diagonal, scale,
        )

    def one(i):
        mixed, top, total = merged(half + i)
        send_ref[i] = jnp.concatenate([mixed, stat_block(top, total)], axis=0).astype(jnp.bfloat16)
        keep_ref[i], stat_ref[i, 0:1], stat_ref[i, 1:2] = merged(i)

    loop(half, one)


def last_kernel(keep_in, stat_in, parcel_ref, out_ref, *, scale):
    count, qheads, head_dim = keep_in.shape
    diagonal = spread_rows(qheads, head_dim)

    def one(i):
        mixed, _, _ = merge_rows(
            keep_in[i], stat_in[i, 0:1], stat_in[i, 1:2], parcel_ref[i].astype(jnp.float32),
            qheads, diagonal, scale,
        )
        out_ref[i] = mixed.astype(out_ref.dtype)

    loop(count, one)


def call(kernel, outs, operands, scalars=0, **static):
    return pl.pallas_call(
        functools.partial(kernel, **static),
        out_shape=outs,
        in_specs=[pl.BlockSpec(memory_space=pltpu.SMEM)] * scalars
        + [pl.BlockSpec(memory_space=pltpu.VMEM)] * (len(operands) - scalars),
        compiler_params=pltpu.CompilerParams(vmem_limit_bytes=VMEM_BYTES),
    )(*operands)


def on_device(
    queries, prefix_keys, prefix_values, suffix_pool, page_owner, page_slot, suffix_len, row_request
):
    blocks = lax.axis_size("blk")
    me = lax.axis_index("blk")
    odd_core = lax.axis_index("heads") % 2
    rows_dev, qheads, head_dim = queries.shape
    slots, _, page_len, kv_heads, _ = suffix_pool.shape
    prefix_rows = prefix_keys.shape[0] * kv_heads
    page_rows = page_len * kv_heads
    scale = math.log2(math.e) / math.sqrt(head_dim)
    sizes = (kv_heads, qheads // kv_heads, prefix_rows, slots, page_rows, scale)
    shared_bits = [1 << b for b in range(2, blocks.bit_length() - 1)]

    keys = prefix_keys.reshape(prefix_rows, head_dim)
    rest = pack(
        prefix_values.reshape(prefix_rows, head_dim),
        suffix_pool.reshape(slots * 2 * page_rows, head_dim),
    )
    far_keys = exchange(keys, 1, 2)
    first = queries
    second = exchange(first, 2, 1)
    far_rest = exchange(rest, 1, 2)
    for bit in shared_bits:
        first = jnp.concatenate([first, second], axis=0)
        second = exchange(first, bit, bit)
    half = first.shape[0]
    rows = 2 * half

    place = jnp.stack([me, 2 - odd_core, 1 + odd_core]).astype(jnp.int32)
    table = jax.ShapeDtypeStruct((rows, slots * page_rows), jnp.float32)
    near_bias, far_bias = call(
        bias_kernel, (table, table), (place, page_owner, page_slot, suffix_len, row_request), 5,
        rows_dev=rows_dev, page_len=page_len, kv_heads=kv_heads, blocks=blocks,
    )
    chunk = min(CHUNK, half)
    block = jax.ShapeDtypeStruct((half // chunk, chunk * qheads, head_dim), jnp.float32)
    near = [
        call(
            near_kernel, (block, block, block), (query, pack(keys), rest, near_bias), offset=offset, sizes=sizes
        )
        for query, offset in ((first, 0), (second, half))
    ]

    def parcel(count):
        return (
            jax.ShapeDtypeStruct((count, qheads + STAT_ROWS, head_dim), jnp.bfloat16),
            jax.ShapeDtypeStruct((count, qheads, head_dim), jnp.float32),
            jax.ShapeDtypeStruct((count, 8, head_dim), jnp.float32),
        )

    outs = parcel(half)
    (send,) = call(
        far_kernel, outs[:1], (second, far_keys, far_rest, far_bias, *near[1]), offset=half, sizes=sizes
    )
    keep, stats = call(
        far_kernel, outs[1:], (first, far_keys, far_rest, far_bias, *near[0]), offset=0, sizes=sizes
    )
    for bit in reversed(shared_bits):
        arrived = exchange(send, bit, bit)
        half //= 2
        send, keep, stats = call(merge_kernel, parcel(half), (keep, stats, arrived), scale=scale)
    arrived = exchange(send, 2, 1)
    return call(
        last_kernel, jax.ShapeDtypeStruct(queries.shape, queries.dtype), (keep, stats, arrived),
        scale=scale,
    )


def solution(mesh):
    placed = (
        P(("groups", "blk"), "heads", None),
        P(("groups", "blk"), "heads", None),
        P(("groups", "blk"), "heads", None),
        P(("groups", "blk"), None, None, "heads", None),
        P("groups", None),
        P("groups", None),
        P("groups"),
        P("groups"),
    )
    return jax.shard_map(
        on_device,
        mesh=mesh,
        in_specs=placed,
        out_specs=P(("groups", "blk"), "heads", None),
        check_vma=False,
    )
```

```python
import functools
import math

import jax
import jax.numpy as jnp
from jax import lax
from jax.experimental import pallas as pl
from jax.experimental.pallas import tpu as pltpu
from jax.sharding import PartitionSpec as P

VMEM_BYTES = 40 * 1024 * 1024
STAT_ROWS = 16
CHUNK = 4
PACK_BYTES = 4 * 1024 * 1024


def exchange(value, even_bit, odd_bit, turn=0):
    blocks = lax.axis_size("blk")
    cores = lax.axis_size("heads")
    pairs = []
    for b in range(blocks):
        for c in range(cores):
            goal = c ^ turn
            pairs.append((b * cores + c, (b ^ (odd_bit if goal % 2 else even_bit)) * cores + goal))
    return lax.ppermute(value, ("blk", "heads"), pairs)


def loop(count, body):
    if count <= 4:
        for i in range(count):
            body(i)
    else:
        lax.fori_loop(0, count, lambda i, carry: (body(i), carry)[1], 0)


def spread_rows(qheads, lanes):
    sub = lax.broadcasted_iota(jnp.int32, (qheads, lanes), 0)
    lane = lax.broadcasted_iota(jnp.int32, (qheads, lanes), 1)
    return sub == lane


def to_row(column, diagonal):
    return jnp.sum(jnp.where(diagonal, column, 0.0), axis=0, keepdims=True)


def to_column(row, diagonal):
    return jnp.sum(jnp.where(diagonal, row, 0.0), axis=1, keepdims=True)


def split(value):
    high = value.astype(jnp.bfloat16).astype(jnp.float32)
    return high, (value - high).astype(jnp.bfloat16).astype(jnp.float32)


def stat_block(top_row, total_row):
    top_high, top_low = split(top_row)
    total_high, total_low = split(total_row)
    blank = jnp.zeros((STAT_ROWS - 4, top_row.shape[1]), jnp.float32)
    return jnp.concatenate([top_high, top_low, total_high, total_low, blank], axis=0)


def suffix_rows(rest_ref, start, slots, page_rows):
    return jnp.concatenate(
        [rest_ref[start + s * 2 * page_rows : start + s * 2 * page_rows + page_rows] for s in range(slots)],
        axis=0,
    )


def attend(query, key_ref, rest_ref, bias, sizes):
    kv_heads, group, prefix_rows, slots, page_rows, scale = sizes
    rows = query.shape[0]
    qheads = kv_heads * group
    suffix_count = slots * page_rows
    key = key_ref[...]
    value = rest_ref[0:prefix_rows]
    page_key = suffix_rows(rest_ref, prefix_rows, slots, page_rows)
    page_value = suffix_rows(rest_ref, prefix_rows + page_rows, slots, page_rows)
    contract = (((1,), (1,)), ((), ()))
    near = lax.dot_general(query, key, contract, preferred_element_type=jnp.float32)
    page = lax.dot_general(query, page_key, contract, preferred_element_type=jnp.float32)

    def own_head(width):
        row = lax.broadcasted_iota(jnp.int32, (rows, width), 0)
        column = lax.broadcasted_iota(jnp.int32, (rows, width), 1)
        return (row % qheads) // group == column % kv_heads

    near = jnp.where(own_head(prefix_rows), near, -jnp.inf)
    page = jnp.where(own_head(suffix_count), page, -jnp.inf) + bias
    top = jnp.maximum(
        jnp.max(near, axis=1, keepdims=True), jnp.max(page, axis=1, keepdims=True)
    )
    near = jnp.exp2((near - top) * scale)
    page = jnp.exp2((page - top) * scale)
    total = jnp.sum(near, axis=1, keepdims=True) + jnp.sum(page, axis=1, keepdims=True)
    mixed = jnp.dot(near.astype(jnp.bfloat16), value, preferred_element_type=jnp.float32)
    mixed = mixed + jnp.dot(
        page.astype(jnp.bfloat16), page_value, preferred_element_type=jnp.float32
    )
    return top, total, mixed


def chunk_bias(bias_ref, first, count, qheads):
    return jnp.concatenate(
        [
            jnp.broadcast_to(bias_ref[pl.ds(first + j, 1), :], (qheads, bias_ref.shape[1]))
            for j in range(count)
        ],
        axis=0,
    )


def pack_kernel(*refs):
    *sources, rest_ref, sems = refs
    start = 0
    copies = []
    for i, source in enumerate(sources):
        rows = source.shape[0]
        copies.append(pltpu.make_async_copy(source, rest_ref.at[start : start + rows], sems.at[i]))
        start += rows
    for copy in copies:
        copy.start()
    for copy in copies:
        copy.wait()


def pack(*sources):
    rows = sum(source.shape[0] for source in sources)
    return pl.pallas_call(
        pack_kernel,
        out_shape=jax.ShapeDtypeStruct((rows, sources[0].shape[1]), sources[0].dtype),
        in_specs=[pl.BlockSpec(memory_space=pltpu.HBM)] * len(sources),
        out_specs=pl.BlockSpec(memory_space=pltpu.VMEM),
        scratch_shapes=[pltpu.SemaphoreType.DMA((len(sources),))],
        compiler_params=pltpu.CompilerParams(vmem_limit_bytes=VMEM_BYTES),
        cost_estimate=pl.CostEstimate(flops=0, bytes_accessed=PACK_BYTES, transcendentals=0),
    )(*(pltpu.with_memory_space_constraint(source, pltpu.HBM) for source in sources))


def bias_kernel(
    place_ref, owner_ref, slot_ref, len_ref, request_ref, near_ref, far_ref, *, rows_dev, page_len, kv_heads, blocks
):
    row_total = near_ref.shape[0]
    width = near_ref.shape[1]
    me, query_bit, key_bit = place_ref[0], place_ref[1], place_ref[2]
    all_rows = request_ref.shape[0]
    column = lax.broadcasted_iota(jnp.int32, (1, width), 1)

    def one(i):
        place = i // rows_dev
        device = me ^ jnp.where(place % 2 == 1, query_bit, 0) ^ ((place // 2) * 4)
        row = device * rows_dev + i % rows_dev
        request = request_ref[row]

        def count(j, later):
            return later + jnp.where((request_ref[j] == request) & (j > row), 1, 0)

        if all_rows <= 16:
            later = jnp.int32(0)
            for j in range(all_rows):
                later = count(j, later)
        else:
            later = lax.fori_loop(0, all_rows, count, jnp.int32(0))
        limit = len_ref[request] - later
        for holder, out_ref in ((me, near_ref), (me ^ key_bit, far_ref)):
            page = lax.rem(holder - owner_ref[request, 0] + blocks, blocks)
            shown = jnp.clip(limit - page * page_len, 0, page_len) * kv_heads
            first = slot_ref[request, page] * (page_len * kv_heads)
            out_ref[pl.ds(i, 1), :] = jnp.where(
                (column >= first) & (column < first + shown), 0.0, -jnp.inf
            )

    loop(row_total, one)


def chunks(first_ref, second_ref, bias_ref):
    half, qheads, head_dim = first_ref.shape
    part = min(CHUNK // 2, half)

    def load(i):
        query = jnp.concatenate(
            [
                ref[pl.ds(i * part, part)].reshape(part * qheads, head_dim)
                for ref in (first_ref, second_ref)
            ],
            axis=0,
        )
        bias = jnp.concatenate(
            [
                chunk_bias(bias_ref, i * part, part, qheads),
                chunk_bias(bias_ref, half + i * part, part, qheads),
            ],
            axis=0,
        )
        return query, bias

    return part, half // part, load


def near_kernel(
    first_ref, second_ref, key_ref, rest_ref, bias_ref, mixed_ref, top_ref, total_ref, *, sizes
):
    _, steps, load = chunks(first_ref, second_ref, bias_ref)

    def one(i):
        query, bias = load(i)
        top, total, mixed = attend(query, key_ref, rest_ref, bias, sizes)
        mixed_ref[i] = mixed
        top_ref[i] = jnp.broadcast_to(top, mixed.shape)
        total_ref[i] = jnp.broadcast_to(total, mixed.shape)

    loop(steps, one)


def far_kernel(
    first_ref, second_ref, key_ref, rest_ref, bias_ref, mixed_ref, top_ref, total_ref,
    send_ref, keep_ref, *, sizes,
):
    _, qheads, head_dim = first_ref.shape
    scale = sizes[-1]
    part, steps, load = chunks(first_ref, second_ref, bias_ref)
    diagonal = spread_rows(qheads, head_dim)

    def one(i):
        query, bias = load(i)
        top, total, mixed = attend(query, key_ref, rest_ref, bias, sizes)
        near_top = top_ref[i][:, :1]
        high, low = split(jnp.maximum(near_top, top))
        point = high + low
        near_scale = jnp.exp2((near_top - point) * scale)
        far_scale = jnp.exp2((top - point) * scale)
        total = total_ref[i][:, :1] * near_scale + total * far_scale
        mixed = (mixed_ref[i] * near_scale + mixed * far_scale) / total
        for j in range(2 * part):
            rows = slice(j * qheads, (j + 1) * qheads)
            place = i * part + j % part
            out_ref = keep_ref if j < part else send_ref
            out_ref[place] = write(
                mixed[rows], to_row(point[rows], diagonal), to_row(total[rows], diagonal),
                out_ref.dtype,
            )

    loop(steps, one)


def read(parcel):
    parcel = parcel.astype(jnp.float32)
    qheads = parcel.shape[0] - STAT_ROWS
    stats = parcel[qheads:]
    return parcel[:qheads], stats[0:1] + stats[1:2], stats[2:3] + stats[3:4]


def write(mixed, top, total, dtype):
    return jnp.concatenate([mixed, stat_block(top, total)], axis=0).astype(dtype)


def merged(keep_ref, parcel_ref, i, diagonal, scale):
    keep, top, total = read(keep_ref[i])
    other, other_top, other_total = read(parcel_ref[i])
    point = jnp.maximum(top, other_top)
    own_weight = total * jnp.exp2((top - point) * scale)
    other_weight = other_total * jnp.exp2((other_top - point) * scale)
    total = own_weight + other_weight
    return keep + (other - keep) * to_column(other_weight / total, diagonal), point, total


def merge_kernel(parcel_ref, keep_in, send_ref, keep_ref, *, scale):
    count, rows, head_dim = keep_in.shape
    diagonal = spread_rows(rows - STAT_ROWS, head_dim)
    half = count // 2

    def one(i):
        send_ref[i] = write(*merged(keep_in, parcel_ref, half + i, diagonal, scale), send_ref.dtype)
        keep_ref[i] = write(*merged(keep_in, parcel_ref, i, diagonal, scale), keep_ref.dtype)

    loop(half, one)


def last_kernel(parcel_ref, keep_in, out_ref, *, scale):
    count, rows, head_dim = keep_in.shape
    diagonal = spread_rows(rows - STAT_ROWS, head_dim)

    def one(i):
        mixed, _, _ = merged(keep_in, parcel_ref, i, diagonal, scale)
        out_ref[i] = mixed.astype(out_ref.dtype)

    loop(count, one)


def call(kernel, outs, operands, scalars=0, **static):
    return pl.pallas_call(
        functools.partial(kernel, **static),
        out_shape=outs,
        in_specs=[pl.BlockSpec(memory_space=pltpu.SMEM)] * scalars
        + [pl.BlockSpec(memory_space=pltpu.VMEM)] * (len(operands) - scalars),
        compiler_params=pltpu.CompilerParams(vmem_limit_bytes=VMEM_BYTES),
    )(*operands)


def on_device(
    queries, prefix_keys, prefix_values, suffix_pool, page_owner, page_slot, suffix_len, row_request
):
    blocks = lax.axis_size("blk")
    me = lax.axis_index("blk")
    odd_core = lax.axis_index("heads") % 2
    rows_dev, qheads, head_dim = queries.shape
    slots, _, page_len, kv_heads, _ = suffix_pool.shape
    prefix_rows = prefix_keys.shape[0] * kv_heads
    page_rows = page_len * kv_heads
    scale = math.log2(math.e) / math.sqrt(head_dim)
    sizes = (kv_heads, qheads // kv_heads, prefix_rows, slots, page_rows, scale)
    shared_bits = [1 << b for b in range(2, blocks.bit_length() - 1)]

    keys = prefix_keys.reshape(prefix_rows, head_dim)
    rest = pack(
        prefix_values.reshape(prefix_rows, head_dim),
        suffix_pool.reshape(slots * 2 * page_rows, head_dim),
    )
    far_keys = exchange(keys, 1, 2)
    first = queries
    second = exchange(first, 2, 1)
    far_rest = exchange(rest, 1, 2)
    for bit in shared_bits:
        first = jnp.concatenate([first, second], axis=0)
        second = exchange(first, bit, bit)
    half = first.shape[0]
    rows = 2 * half

    place = jnp.stack([me, 2 - odd_core, 1 + odd_core]).astype(jnp.int32)
    table = jax.ShapeDtypeStruct((rows, slots * page_rows), jnp.float32)
    near_bias, far_bias = call(
        bias_kernel, (table, table), (place, page_owner, page_slot, suffix_len, row_request), 5,
        rows_dev=rows_dev, page_len=page_len, kv_heads=kv_heads, blocks=blocks,
    )
    part = min(CHUNK // 2, half)
    block = jax.ShapeDtypeStruct((half // part, 2 * part * qheads, head_dim), jnp.float32)
    near = call(
        near_kernel, (block, block, block), (first, second, pack(keys), rest, near_bias), sizes=sizes
    )

    def parcels(count):
        shape = (count, qheads + STAT_ROWS, head_dim)
        return jax.ShapeDtypeStruct(shape, jnp.bfloat16), jax.ShapeDtypeStruct(shape, jnp.float32)

    send, keep = call(
        far_kernel, parcels(half), (first, second, far_keys, far_rest, far_bias, *near), sizes=sizes
    )
    cross = 1 if shared_bits and lax.axis_size("heads") % 2 == 0 else 0
    turn = cross
    for bit in reversed(shared_bits):
        arrived = exchange(send, bit, bit, turn)
        if turn:
            keep = exchange(keep, 0, 0, turn)
        half //= 2
        send, keep = call(merge_kernel, parcels(half), (arrived, keep), scale=scale)
        turn = 0
    arrived = exchange(send, 2, 1, cross)
    if cross:
        keep = exchange(keep, 0, 0, cross)
    return call(
        last_kernel, jax.ShapeDtypeStruct(queries.shape, queries.dtype), (arrived, keep), scale=scale
    )


def solution(mesh):
    placed = (
        P(("groups", "blk"), "heads", None),
        P(("groups", "blk"), "heads", None),
        P(("groups", "blk"), "heads", None),
        P(("groups", "blk"), None, None, "heads", None),
        P("groups", None),
        P("groups", None),
        P("groups"),
        P("groups"),
    )
    return jax.shard_map(
        on_device,
        mesh=mesh,
        in_specs=placed,
        out_specs=P(("groups", "blk"), "heads", None),
        check_vma=False,
    )
```

```python
import functools
import math

import jax
import jax.numpy as jnp
from jax import lax
from jax.experimental import pallas as pl
from jax.experimental.pallas import tpu as pltpu
from jax.sharding import PartitionSpec as P

VMEM_BYTES = 40 * 1024 * 1024
STAT_ROWS = 16
CHUNK = 4
PACK_BYTES = 4 * 1024 * 1024


def exchange(value, even_bit, odd_bit, turn=0):
    blocks = lax.axis_size("blk")
    cores = lax.axis_size("heads")
    pairs = []
    for b in range(blocks):
        for c in range(cores):
            goal = c ^ turn
            pairs.append((b * cores + c, (b ^ (odd_bit if goal % 2 else even_bit)) * cores + goal))
    return lax.ppermute(value, ("blk", "heads"), pairs)


def loop(count, body):
    if count <= 4:
        for i in range(count):
            body(i)
    else:
        lax.fori_loop(0, count, lambda i, carry: (body(i), carry)[1], 0)


def spread_rows(qheads, lanes):
    sub = lax.broadcasted_iota(jnp.int32, (qheads, lanes), 0)
    lane = lax.broadcasted_iota(jnp.int32, (qheads, lanes), 1)
    return sub == lane


def to_row(column, diagonal):
    return jnp.sum(jnp.where(diagonal, column, 0.0), axis=0, keepdims=True)


def to_column(row, diagonal):
    return jnp.sum(jnp.where(diagonal, row, 0.0), axis=1, keepdims=True)


def split(value):
    high = value.astype(jnp.bfloat16).astype(jnp.float32)
    return high, (value - high).astype(jnp.bfloat16).astype(jnp.float32)


def stat_block(top_row, total_row):
    top_high, top_low = split(top_row)
    total_high, total_low = split(total_row)
    blank = jnp.zeros((STAT_ROWS - 4, top_row.shape[1]), jnp.float32)
    return jnp.concatenate([top_high, top_low, total_high, total_low, blank], axis=0)


def suffix_rows(rest_ref, start, slots, page_rows):
    return jnp.concatenate(
        [rest_ref[start + s * 2 * page_rows : start + s * 2 * page_rows + page_rows] for s in range(slots)],
        axis=0,
    )


def attend(query, key_ref, rest_ref, bias, sizes):
    kv_heads, group, prefix_rows, slots, page_rows, scale = sizes
    rows = query.shape[0]
    qheads = kv_heads * group
    suffix_count = slots * page_rows
    key = key_ref[...]
    value = rest_ref[0:prefix_rows]
    page_key = suffix_rows(rest_ref, prefix_rows, slots, page_rows)
    page_value = suffix_rows(rest_ref, prefix_rows + page_rows, slots, page_rows)
    contract = (((1,), (1,)), ((), ()))
    near = lax.dot_general(query, key, contract, preferred_element_type=jnp.float32)
    page = lax.dot_general(query, page_key, contract, preferred_element_type=jnp.float32)

    def own_head(width):
        row = lax.broadcasted_iota(jnp.int32, (rows, width), 0)
        column = lax.broadcasted_iota(jnp.int32, (rows, width), 1)
        return (row % qheads) // group == column % kv_heads

    near = jnp.where(own_head(prefix_rows), near, -jnp.inf)
    page = jnp.where(own_head(suffix_count), page, -jnp.inf) + bias
    top = jnp.maximum(
        jnp.max(near, axis=1, keepdims=True), jnp.max(page, axis=1, keepdims=True)
    )
    near = jnp.exp2((near - top) * scale)
    page = jnp.exp2((page - top) * scale)
    total = jnp.sum(near, axis=1, keepdims=True) + jnp.sum(page, axis=1, keepdims=True)
    mixed = jnp.dot(near.astype(jnp.bfloat16), value, preferred_element_type=jnp.float32)
    mixed = mixed + jnp.dot(
        page.astype(jnp.bfloat16), page_value, preferred_element_type=jnp.float32
    )
    return top, total, mixed


def chunk_bias(bias_ref, first, count, qheads):
    return jnp.concatenate(
        [
            jnp.broadcast_to(bias_ref[pl.ds(first + j, 1), :], (qheads, bias_ref.shape[1]))
            for j in range(count)
        ],
        axis=0,
    )


def pack_kernel(*refs):
    *sources, rest_ref, sems = refs
    start = 0
    copies = []
    for i, source in enumerate(sources):
        rows = source.shape[0]
        copies.append(pltpu.make_async_copy(source, rest_ref.at[start : start + rows], sems.at[i]))
        start += rows
    for copy in copies:
        copy.start()
    for copy in copies:
        copy.wait()


def pack(*sources):
    rows = sum(source.shape[0] for source in sources)
    return pl.pallas_call(
        pack_kernel,
        out_shape=jax.ShapeDtypeStruct((rows, sources[0].shape[1]), sources[0].dtype),
        in_specs=[pl.BlockSpec(memory_space=pltpu.HBM)] * len(sources),
        out_specs=pl.BlockSpec(memory_space=pltpu.VMEM),
        scratch_shapes=[pltpu.SemaphoreType.DMA((len(sources),))],
        compiler_params=pltpu.CompilerParams(vmem_limit_bytes=VMEM_BYTES),
        cost_estimate=pl.CostEstimate(flops=0, bytes_accessed=PACK_BYTES, transcendentals=0),
    )(*(pltpu.with_memory_space_constraint(source, pltpu.HBM) for source in sources))


def bias_kernel(
    place_ref, owner_ref, slot_ref, len_ref, request_ref, near_ref, far_ref, *, rows_dev, page_len, kv_heads, blocks
):
    row_total = near_ref.shape[0]
    width = near_ref.shape[1]
    me, query_bit, key_bit = place_ref[0], place_ref[1], place_ref[2]
    all_rows = request_ref.shape[0]
    column = lax.broadcasted_iota(jnp.int32, (1, width), 1)

    def one(i):
        place = i // rows_dev
        device = me ^ jnp.where(place % 2 == 1, query_bit, 0) ^ ((place // 2) * 4)
        row = device * rows_dev + i % rows_dev
        request = request_ref[row]

        def count(j, later):
            return later + jnp.where((request_ref[j] == request) & (j > row), 1, 0)

        if all_rows <= 16:
            later = jnp.int32(0)
            for j in range(all_rows):
                later = count(j, later)
        else:
            later = lax.fori_loop(0, all_rows, count, jnp.int32(0))
        limit = len_ref[request] - later
        for holder, out_ref in ((me, near_ref), (me ^ key_bit, far_ref)):
            page = lax.rem(holder - owner_ref[request, 0] + blocks, blocks)
            shown = jnp.clip(limit - page * page_len, 0, page_len) * kv_heads
            first = slot_ref[request, page] * (page_len * kv_heads)
            out_ref[pl.ds(i, 1), :] = jnp.where(
                (column >= first) & (column < first + shown), 0.0, -jnp.inf
            )

    loop(row_total, one)


def chunks(first_ref, second_ref, bias_ref):
    half, qheads, head_dim = first_ref.shape
    part = min(CHUNK // 2, half)

    def load(i):
        query = jnp.concatenate(
            [
                ref[pl.ds(i * part, part)].reshape(part * qheads, head_dim)
                for ref in (first_ref, second_ref)
            ],
            axis=0,
        )
        bias = jnp.concatenate(
            [
                chunk_bias(bias_ref, i * part, part, qheads),
                chunk_bias(bias_ref, half + i * part, part, qheads),
            ],
            axis=0,
        )
        return query, bias

    return part, half // part, load


def near_kernel(
    first_ref, second_ref, key_ref, rest_ref, bias_ref, mixed_ref, top_ref, total_ref, *, sizes
):
    _, steps, load = chunks(first_ref, second_ref, bias_ref)

    def one(i):
        query, bias = load(i)
        top, total, mixed = attend(query, key_ref, rest_ref, bias, sizes)
        mixed_ref[i] = mixed
        top_ref[i] = jnp.broadcast_to(top, mixed.shape)
        total_ref[i] = jnp.broadcast_to(total, mixed.shape)

    loop(steps, one)


def far_kernel(
    first_ref, second_ref, key_ref, rest_ref, bias_ref, mixed_ref, top_ref, total_ref,
    send_ref, keep_ref, *, sizes,
):
    _, qheads, head_dim = first_ref.shape
    scale = sizes[-1]
    part, steps, load = chunks(first_ref, second_ref, bias_ref)
    diagonal = spread_rows(qheads, head_dim)

    def one(i):
        query, bias = load(i)
        top, total, mixed = attend(query, key_ref, rest_ref, bias, sizes)
        near_top = top_ref[i][:, :1]
        high, low = split(jnp.maximum(near_top, top))
        point = high + low
        near_scale = jnp.exp2((near_top - point) * scale)
        far_scale = jnp.exp2((top - point) * scale)
        total = total_ref[i][:, :1] * near_scale + total * far_scale
        mixed = (mixed_ref[i] * near_scale + mixed * far_scale) / total
        for j in range(2 * part):
            rows = slice(j * qheads, (j + 1) * qheads)
            place = i * part + j % part
            out_ref = keep_ref if j < part else send_ref
            out_ref[place] = write(
                mixed[rows], to_row(point[rows], diagonal), to_row(total[rows], diagonal),
                out_ref.dtype,
            )

    loop(steps, one)


def read(parcel):
    parcel = parcel.astype(jnp.float32)
    qheads = parcel.shape[0] - STAT_ROWS
    stats = parcel[qheads:]
    return parcel[:qheads], stats[0:1] + stats[1:2], stats[2:3] + stats[3:4]


def write(mixed, top, total, dtype):
    return jnp.concatenate([mixed, stat_block(top, total)], axis=0).astype(dtype)


def merged(keep_ref, parcel_ref, i, diagonal, scale):
    keep, top, total = read(keep_ref[i])
    other, other_top, other_total = read(parcel_ref[i])
    point = jnp.maximum(top, other_top)
    own_weight = total * jnp.exp2((top - point) * scale)
    other_weight = other_total * jnp.exp2((other_top - point) * scale)
    total = own_weight + other_weight
    return keep + (other - keep) * to_column(other_weight / total, diagonal), point, total


def merge_kernel(parcel_ref, keep_in, send_ref, keep_ref, *, scale):
    count, rows, head_dim = keep_in.shape
    diagonal = spread_rows(rows - STAT_ROWS, head_dim)
    half = count // 2

    def one(i):
        send_ref[i] = write(*merged(keep_in, parcel_ref, half + i, diagonal, scale), send_ref.dtype)
        keep_ref[i] = write(*merged(keep_in, parcel_ref, i, diagonal, scale), keep_ref.dtype)

    loop(half, one)


def last_kernel(parcel_ref, keep_in, out_ref, *, scale):
    count, rows, head_dim = keep_in.shape
    diagonal = spread_rows(rows - STAT_ROWS, head_dim)

    def one(i):
        mixed, _, _ = merged(keep_in, parcel_ref, i, diagonal, scale)
        out_ref[i] = mixed.astype(out_ref.dtype)

    loop(count, one)


def call(kernel, outs, operands, scalars=0, **static):
    return pl.pallas_call(
        functools.partial(kernel, **static),
        out_shape=outs,
        in_specs=[pl.BlockSpec(memory_space=pltpu.SMEM)] * scalars
        + [pl.BlockSpec(memory_space=pltpu.VMEM)] * (len(operands) - scalars),
        compiler_params=pltpu.CompilerParams(vmem_limit_bytes=VMEM_BYTES),
    )(*operands)


def on_device(
    queries, prefix_keys, prefix_values, suffix_pool, page_owner, page_slot, suffix_len, row_request
):
    blocks = lax.axis_size("blk")
    me = lax.axis_index("blk")
    odd_core = lax.axis_index("heads") % 2
    rows_dev, qheads, head_dim = queries.shape
    slots, _, page_len, kv_heads, _ = suffix_pool.shape
    prefix_rows = prefix_keys.shape[0] * kv_heads
    page_rows = page_len * kv_heads
    scale = math.log2(math.e) / math.sqrt(head_dim)
    sizes = (kv_heads, qheads // kv_heads, prefix_rows, slots, page_rows, scale)
    shared_bits = [1 << b for b in range(2, blocks.bit_length() - 1)]

    keys = prefix_keys.reshape(prefix_rows, head_dim)
    rest = pack(
        prefix_values.reshape(prefix_rows, head_dim),
        suffix_pool.reshape(slots * 2 * page_rows, head_dim),
    )
    far_keys = exchange(keys, 1, 2)
    first = queries
    second = exchange(first, 2, 1)
    far_rest = exchange(rest, 1, 2)
    for bit in shared_bits:
        first = jnp.concatenate([first, second], axis=0)
        second = exchange(first, bit, bit)
    half = first.shape[0]
    rows = 2 * half

    place = jnp.stack([me, 2 - odd_core, 1 + odd_core]).astype(jnp.int32)
    table = jax.ShapeDtypeStruct((rows, slots * page_rows), jnp.float32)
    near_bias, far_bias = call(
        bias_kernel, (table, table), (place, page_owner, page_slot, suffix_len, row_request), 5,
        rows_dev=rows_dev, page_len=page_len, kv_heads=kv_heads, blocks=blocks,
    )
    part = min(CHUNK // 2, half)
    block = jax.ShapeDtypeStruct((half // part, 2 * part * qheads, head_dim), jnp.float32)
    near = call(
        near_kernel, (block, block, block), (first, second, pack(keys), rest, near_bias), sizes=sizes
    )

    def parcels(count):
        shape = (count, qheads + STAT_ROWS, head_dim)
        return jax.ShapeDtypeStruct(shape, jnp.bfloat16), jax.ShapeDtypeStruct(shape, jnp.bfloat16)

    send, keep = call(
        far_kernel, parcels(half), (first, second, far_keys, far_rest, far_bias, *near), sizes=sizes
    )
    cross = 1 if shared_bits and lax.axis_size("heads") % 2 == 0 else 0
    turn = cross
    for bit in reversed(shared_bits):
        arrived = exchange(send, bit, bit, turn)
        if turn:
            keep = exchange(keep, 0, 0, turn)
        half //= 2
        send, keep = call(merge_kernel, parcels(half), (arrived, keep), scale=scale)
        turn = 0
    arrived = exchange(send, 2, 1, cross)
    if cross:
        keep = exchange(keep, 0, 0, cross)
    return call(
        last_kernel, jax.ShapeDtypeStruct(queries.shape, queries.dtype), (arrived, keep), scale=scale
    )


def solution(mesh):
    placed = (
        P(("groups", "blk"), "heads", None),
        P(("groups", "blk"), "heads", None),
        P(("groups", "blk"), "heads", None),
        P(("groups", "blk"), None, None, "heads", None),
        P("groups", None),
        P("groups", None),
        P("groups"),
        P("groups"),
    )
    return jax.shard_map(
        on_device,
        mesh=mesh,
        in_specs=placed,
        out_specs=P(("groups", "blk"), "heads", None),
        check_vma=False,
    )
```

```python
import functools
import math

import jax
import jax.numpy as jnp
from jax import lax
from jax.experimental import pallas as pl
from jax.experimental.pallas import tpu as pltpu
from jax.sharding import PartitionSpec as P

VMEM_BYTES = 40 * 1024 * 1024
STAT_ROWS = 16
CHUNK = 4
PACK_BYTES = 4 * 1024 * 1024


def exchange(value, even_bit, odd_bit, turn=0):
    blocks = lax.axis_size("blk")
    cores = lax.axis_size("heads")
    pairs = []
    for b in range(blocks):
        for c in range(cores):
            goal = c ^ turn
            pairs.append((b * cores + c, (b ^ (odd_bit if goal % 2 else even_bit)) * cores + goal))
    return lax.ppermute(value, ("blk", "heads"), pairs)


def loop(count, body):
    if count <= 4:
        for i in range(count):
            body(i)
    else:
        lax.fori_loop(0, count, lambda i, carry: (body(i), carry)[1], 0)


def spread_rows(qheads, lanes):
    sub = lax.broadcasted_iota(jnp.int32, (qheads, lanes), 0)
    lane = lax.broadcasted_iota(jnp.int32, (qheads, lanes), 1)
    return sub == lane


def to_row(column, diagonal):
    return jnp.sum(jnp.where(diagonal, column, 0.0), axis=0, keepdims=True)


def to_column(row, diagonal):
    return jnp.sum(jnp.where(diagonal, row, 0.0), axis=1, keepdims=True)


def split(value):
    high = value.astype(jnp.bfloat16).astype(jnp.float32)
    return high, (value - high).astype(jnp.bfloat16).astype(jnp.float32)


def stat_block(top_row, total_row):
    top_high, top_low = split(top_row)
    total_high, total_low = split(total_row)
    blank = jnp.zeros((STAT_ROWS - 4, top_row.shape[1]), jnp.float32)
    return jnp.concatenate([top_high, top_low, total_high, total_low, blank], axis=0)


def suffix_rows(rest_ref, start, slots, page_rows):
    return jnp.concatenate(
        [rest_ref[start + s * 2 * page_rows : start + s * 2 * page_rows + page_rows] for s in range(slots)],
        axis=0,
    )


def attend(query, sides, sizes):
    kv_heads, group, slots, page_rows, scale = sizes
    rows = query.shape[0]
    qheads = kv_heads * group

    def own_head(width):
        row = lax.broadcasted_iota(jnp.int32, (rows, width), 0)
        column = lax.broadcasted_iota(jnp.int32, (rows, width), 1)
        return (row % qheads) // group == column % kv_heads

    def scores(key):
        product = lax.dot_general(
            query, key, (((1,), (1,)), ((), ())), preferred_element_type=jnp.float32
        )
        return jnp.where(own_head(key.shape[0]), product, -jnp.inf)

    parts = []
    for key_ref, rest_ref, bias in sides:
        prefix_rows = key_ref.shape[0]
        page_key = suffix_rows(rest_ref, prefix_rows, slots, page_rows)
        page_value = suffix_rows(rest_ref, prefix_rows + page_rows, slots, page_rows)
        parts.append((scores(key_ref[...]), rest_ref[0:prefix_rows]))
        parts.append((scores(page_key) + bias, page_value))
    top = functools.reduce(jnp.maximum, [jnp.max(score, axis=1, keepdims=True) for score, _ in parts])
    high, low = split(top)
    point = high + low
    total = mixed = 0.0
    for score, value in parts:
        weight = jnp.exp2((score - point) * scale)
        total = total + jnp.sum(weight, axis=1, keepdims=True)
        mixed = mixed + jnp.dot(
            weight.astype(jnp.bfloat16), value, preferred_element_type=jnp.float32
        )
    return point, total, mixed / total


def chunk_bias(bias_ref, first, count, qheads):
    return jnp.concatenate(
        [
            jnp.broadcast_to(bias_ref[pl.ds(first + j, 1), :], (qheads, bias_ref.shape[1]))
            for j in range(count)
        ],
        axis=0,
    )


def pack_kernel(*refs):
    *sources, rest_ref, sems = refs
    start = 0
    copies = []
    for i, source in enumerate(sources):
        rows = source.shape[0]
        copies.append(pltpu.make_async_copy(source, rest_ref.at[start : start + rows], sems.at[i]))
        start += rows
    for copy in copies:
        copy.start()
    for copy in copies:
        copy.wait()


def pack(*sources):
    rows = sum(source.shape[0] for source in sources)
    return pl.pallas_call(
        pack_kernel,
        out_shape=jax.ShapeDtypeStruct((rows, sources[0].shape[1]), sources[0].dtype),
        in_specs=[pl.BlockSpec(memory_space=pltpu.HBM)] * len(sources),
        out_specs=pl.BlockSpec(memory_space=pltpu.VMEM),
        scratch_shapes=[pltpu.SemaphoreType.DMA((len(sources),))],
        compiler_params=pltpu.CompilerParams(vmem_limit_bytes=VMEM_BYTES),
        cost_estimate=pl.CostEstimate(flops=0, bytes_accessed=PACK_BYTES, transcendentals=0),
    )(*(pltpu.with_memory_space_constraint(source, pltpu.HBM) for source in sources))


def bias_kernel(
    place_ref, owner_ref, slot_ref, len_ref, request_ref, near_ref, far_ref, *, rows_dev, page_len, kv_heads, blocks
):
    row_total = near_ref.shape[0]
    width = near_ref.shape[1]
    me, query_bit, key_bit = place_ref[0], place_ref[1], place_ref[2]
    all_rows = request_ref.shape[0]
    half = row_total // rows_dev // 2
    column = lax.broadcasted_iota(jnp.int32, (1, width), 1)

    def one(i):
        place = i // rows_dev
        device = me ^ jnp.where(place >= half, query_bit, 0) ^ ((place % half) * 4)
        row = device * rows_dev + i % rows_dev
        request = request_ref[row]

        def count(j, later):
            return later + jnp.where((request_ref[j] == request) & (j > row), 1, 0)

        if all_rows <= 16:
            later = jnp.int32(0)
            for j in range(all_rows):
                later = count(j, later)
        else:
            later = lax.fori_loop(0, all_rows, count, jnp.int32(0))
        limit = len_ref[request] - later
        for holder, out_ref in ((me, near_ref), (me ^ key_bit, far_ref)):
            page = lax.rem(holder - owner_ref[request, 0] + blocks, blocks)
            shown = jnp.clip(limit - page * page_len, 0, page_len) * kv_heads
            first = slot_ref[request, page] * (page_len * kv_heads)
            out_ref[pl.ds(i, 1), :] = jnp.where(
                (column >= first) & (column < first + shown), 0.0, -jnp.inf
            )

    loop(row_total, one)


def attend_kernel(
    first_ref, second_ref, near_key_ref, near_rest_ref, near_bias_ref,
    far_key_ref, far_rest_ref, far_bias_ref, send_ref, keep_ref, *, sizes,
):
    half, qheads, head_dim = first_ref.shape
    part = min(CHUNK // 2, half)
    diagonal = spread_rows(qheads, head_dim)

    def one(i):
        query = jnp.concatenate(
            [
                ref[pl.ds(i * part, part)].reshape(part * qheads, head_dim)
                for ref in (first_ref, second_ref)
            ],
            axis=0,
        )

        def bias(ref):
            return jnp.concatenate(
                [
                    chunk_bias(ref, i * part, part, qheads),
                    chunk_bias(ref, half + i * part, part, qheads),
                ],
                axis=0,
            )

        sides = (
            (near_key_ref, near_rest_ref, bias(near_bias_ref)),
            (far_key_ref, far_rest_ref, bias(far_bias_ref)),
        )
        point, total, mixed = attend(query, sides, sizes)
        for j in range(2 * part):
            rows = slice(j * qheads, (j + 1) * qheads)
            out_ref = keep_ref if j < part else send_ref
            out_ref[i * part + j % part] = write(
                mixed[rows], to_row(point[rows], diagonal), to_row(total[rows], diagonal),
                out_ref.dtype,
            )

    loop(half // part, one)


def read(parcel):
    parcel = parcel.astype(jnp.float32)
    qheads = parcel.shape[0] - STAT_ROWS
    stats = parcel[qheads:]
    return parcel[:qheads], stats[0:1] + stats[1:2], stats[2:3] + stats[3:4]


def write(mixed, top, total, dtype):
    return jnp.concatenate([mixed, stat_block(top, total)], axis=0).astype(dtype)


def merged(keep_ref, parcel_ref, i, diagonal, scale):
    keep, top, total = read(keep_ref[i])
    other, other_top, other_total = read(parcel_ref[i])
    point = jnp.maximum(top, other_top)
    own_weight = total * jnp.exp2((top - point) * scale)
    other_weight = other_total * jnp.exp2((other_top - point) * scale)
    total = own_weight + other_weight
    return keep + (other - keep) * to_column(other_weight / total, diagonal), point, total


def merge_kernel(parcel_ref, keep_in, send_ref, keep_ref, *, scale):
    count, rows, head_dim = keep_in.shape
    diagonal = spread_rows(rows - STAT_ROWS, head_dim)
    half = count // 2

    def one(i):
        send_ref[i] = write(*merged(keep_in, parcel_ref, half + i, diagonal, scale), send_ref.dtype)
        keep_ref[i] = write(*merged(keep_in, parcel_ref, i, diagonal, scale), keep_ref.dtype)

    loop(half, one)


def last_kernel(parcel_ref, keep_in, out_ref, *, scale):
    count, rows, head_dim = keep_in.shape
    diagonal = spread_rows(rows - STAT_ROWS, head_dim)

    def one(i):
        mixed, _, _ = merged(keep_in, parcel_ref, i, diagonal, scale)
        out_ref[i] = mixed.astype(out_ref.dtype)

    loop(count, one)


def call(kernel, outs, operands, scalars=0, **static):
    return pl.pallas_call(
        functools.partial(kernel, **static),
        out_shape=outs,
        in_specs=[pl.BlockSpec(memory_space=pltpu.SMEM)] * scalars
        + [pl.BlockSpec(memory_space=pltpu.VMEM)] * (len(operands) - scalars),
        compiler_params=pltpu.CompilerParams(vmem_limit_bytes=VMEM_BYTES),
    )(*operands)


def on_device(
    queries, prefix_keys, prefix_values, suffix_pool, page_owner, page_slot, suffix_len, row_request
):
    blocks = lax.axis_size("blk")
    me = lax.axis_index("blk")
    odd_core = lax.axis_index("heads") % 2
    rows_dev, qheads, head_dim = queries.shape
    slots, _, page_len, kv_heads, _ = suffix_pool.shape
    prefix_rows = prefix_keys.shape[0] * kv_heads
    page_rows = page_len * kv_heads
    scale = math.log2(math.e) / math.sqrt(head_dim)
    sizes = (kv_heads, qheads // kv_heads, slots, page_rows, scale)
    shared_bits = [1 << b for b in range(2, blocks.bit_length() - 1)]

    keys = prefix_keys.reshape(prefix_rows, head_dim)
    rest = pack(
        prefix_values.reshape(prefix_rows, head_dim),
        suffix_pool.reshape(slots * 2 * page_rows, head_dim),
    )
    far_keys = exchange(keys, 1, 2)
    far_rest = exchange(rest, 1, 2)
    first = queries
    for bit in shared_bits:
        first = jnp.concatenate([first, exchange(first, bit, bit)], axis=0)
    second = exchange(first, 2, 1)
    half = first.shape[0]
    rows = 2 * half

    place = jnp.stack([me, 2 - odd_core, 1 + odd_core]).astype(jnp.int32)
    table = jax.ShapeDtypeStruct((rows, slots * page_rows), jnp.float32)
    near_bias, far_bias = call(
        bias_kernel, (table, table), (place, page_owner, page_slot, suffix_len, row_request), 5,
        rows_dev=rows_dev, page_len=page_len, kv_heads=kv_heads, blocks=blocks,
    )
    def parcels(count):
        shape = (count, qheads + STAT_ROWS, head_dim)
        return jax.ShapeDtypeStruct(shape, jnp.bfloat16), jax.ShapeDtypeStruct(shape, jnp.bfloat16)

    send, keep = call(
        attend_kernel, parcels(half),
        (first, second, keys, rest, near_bias, far_keys, far_rest, far_bias), sizes=sizes,
    )
    cross = 1 if shared_bits and lax.axis_size("heads") % 2 == 0 else 0
    arrived = exchange(send, 1, 2, 1) if cross else exchange(send, 2, 1)
    turn = cross
    for bit in reversed(shared_bits):
        if turn:
            keep = exchange(keep, 0, 0, turn)
        half //= 2
        send, keep = call(merge_kernel, parcels(half), (arrived, keep), scale=scale)
        turn = cross if bit == shared_bits[0] else 0
        arrived = exchange(send, bit, bit, turn)
    if cross:
        keep = exchange(keep, 0, 0, cross)
    return call(
        last_kernel, jax.ShapeDtypeStruct(queries.shape, queries.dtype), (arrived, keep), scale=scale
    )


def solution(mesh):
    placed = (
        P(("groups", "blk"), "heads", None),
        P(("groups", "blk"), "heads", None),
        P(("groups", "blk"), "heads", None),
        P(("groups", "blk"), None, None, "heads", None),
        P("groups", None),
        P("groups", None),
        P("groups"),
        P("groups"),
    )
    return jax.shard_map(
        on_device,
        mesh=mesh,
        in_specs=placed,
        out_specs=P(("groups", "blk"), "heads", None),
        check_vma=False,
    )
```

```python
import functools
import math

import jax
import jax.numpy as jnp
from jax import lax
from jax.experimental import pallas as pl
from jax.experimental.pallas import tpu as pltpu
from jax.sharding import PartitionSpec as P

VMEM_BYTES = 32 * 1024 * 1024
STAT_ROWS = 16
CHUNK = 4
PACK_BYTES = 4 * 1024 * 1024


def exchange(value, even_bit, odd_bit, turn=0):
    blocks = lax.axis_size("blk")
    cores = lax.axis_size("heads")
    pairs = []
    for b in range(blocks):
        for c in range(cores):
            goal = c ^ turn
            pairs.append((b * cores + c, (b ^ (odd_bit if goal % 2 else even_bit)) * cores + goal))
    return lax.ppermute(value, ("blk", "heads"), pairs)


def loop(count, body):
    if count <= 4:
        for i in range(count):
            body(i)
    else:
        lax.fori_loop(0, count, lambda i, carry: (body(i), carry)[1], 0)


def spread_rows(qheads, lanes):
    sub = lax.broadcasted_iota(jnp.int32, (qheads, lanes), 0)
    lane = lax.broadcasted_iota(jnp.int32, (qheads, lanes), 1)
    return sub == lane


def to_row(column, diagonal):
    return jnp.sum(jnp.where(diagonal, column, 0.0), axis=0, keepdims=True)


def to_column(row, diagonal):
    return jnp.sum(jnp.where(diagonal, row, 0.0), axis=1, keepdims=True)


def split(value):
    high = value.astype(jnp.bfloat16).astype(jnp.float32)
    return high, (value - high).astype(jnp.bfloat16).astype(jnp.float32)


def stat_block(top_row, total_row):
    top_high, top_low = split(top_row)
    total_high, total_low = split(total_row)
    blank = jnp.zeros((STAT_ROWS - 4, top_row.shape[1]), jnp.float32)
    return jnp.concatenate([top_high, top_low, total_high, total_low, blank], axis=0)


def suffix_rows(rest_ref, start, slots, page_rows):
    return jnp.concatenate(
        [rest_ref[start + s * 2 * page_rows : start + s * 2 * page_rows + page_rows] for s in range(slots)],
        axis=0,
    )


def attend(query, sides, sizes):
    kv_heads, group, slots, page_rows, scale = sizes
    rows = query.shape[0]
    qheads = kv_heads * group

    def own_head(width):
        row = lax.broadcasted_iota(jnp.int32, (rows, width), 0)
        column = lax.broadcasted_iota(jnp.int32, (rows, width), 1)
        return (row % qheads) // group == column % kv_heads

    def scores(key):
        product = lax.dot_general(
            query, key, (((1,), (1,)), ((), ())), preferred_element_type=jnp.float32
        )
        return jnp.where(own_head(key.shape[0]), product, -jnp.inf)

    parts = []
    for key_ref, bias, value_ref in sides:
        prefix_rows = key_ref.shape[0] - 2 * slots * page_rows
        page_key = suffix_rows(key_ref, prefix_rows, slots, page_rows)
        page_value = suffix_rows(key_ref, prefix_rows + page_rows, slots, page_rows)
        parts.append((scores(key_ref[0:prefix_rows]), value_ref))
        parts.append((scores(page_key) + bias, page_value))
    top = functools.reduce(jnp.maximum, [jnp.max(score, axis=1, keepdims=True) for score, _ in parts])
    high, low = split(top)
    point = high + low
    total = mixed = 0.0
    late = None
    for score, value in parts:
        weight = jnp.exp2((score - point) * scale)
        total = total + jnp.sum(weight, axis=1, keepdims=True)
        weight = weight.astype(jnp.bfloat16)
        if value is None:
            late = weight
        else:
            mixed = mixed + jnp.dot(weight, value[...], preferred_element_type=jnp.float32)
    return point, total, mixed, late


def chunk_bias(bias_ref, first, count, qheads):
    return jnp.concatenate(
        [
            jnp.broadcast_to(bias_ref[pl.ds(first + j, 1), :], (qheads, bias_ref.shape[1]))
            for j in range(count)
        ],
        axis=0,
    )


def pack_kernel(*refs):
    *sources, rest_ref, sems = refs
    start = 0
    copies = []
    for i, source in enumerate(sources):
        rows = source.shape[0]
        copies.append(pltpu.make_async_copy(source, rest_ref.at[start : start + rows], sems.at[i]))
        start += rows
    for copy in copies:
        copy.start()
    for copy in copies:
        copy.wait()


def pack(*sources):
    rows = sum(source.shape[0] for source in sources)
    return pl.pallas_call(
        pack_kernel,
        out_shape=jax.ShapeDtypeStruct((rows, sources[0].shape[1]), sources[0].dtype),
        in_specs=[pl.BlockSpec(memory_space=pltpu.HBM)] * len(sources),
        out_specs=pl.BlockSpec(memory_space=pltpu.VMEM),
        scratch_shapes=[pltpu.SemaphoreType.DMA((len(sources),))],
        compiler_params=pltpu.CompilerParams(vmem_limit_bytes=VMEM_BYTES),
        cost_estimate=pl.CostEstimate(flops=0, bytes_accessed=PACK_BYTES, transcendentals=0),
    )(*(pltpu.with_memory_space_constraint(source, pltpu.HBM) for source in sources))


def bias_kernel(
    place_ref, owner_ref, slot_ref, len_ref, request_ref, near_ref, far_ref, *, rows_dev, page_len, kv_heads, blocks
):
    row_total = near_ref.shape[0]
    width = near_ref.shape[1]
    me, query_bit, key_bit = place_ref[0], place_ref[1], place_ref[2]
    all_rows = request_ref.shape[0]
    half = row_total // rows_dev // 2
    column = lax.broadcasted_iota(jnp.int32, (1, width), 1)

    def one(i):
        place = i // rows_dev
        device = me ^ jnp.where(place >= half, query_bit, 0) ^ ((place % half) * 4)
        row = device * rows_dev + i % rows_dev
        request = request_ref[row]

        def count(j, later):
            return later + jnp.where((request_ref[j] == request) & (j > row), 1, 0)

        if all_rows <= 16:
            later = jnp.int32(0)
            for j in range(all_rows):
                later = count(j, later)
        else:
            later = lax.fori_loop(0, all_rows, count, jnp.int32(0))
        limit = len_ref[request] - later
        for holder, out_ref in ((me, near_ref), (me ^ key_bit, far_ref)):
            page = lax.rem(holder - owner_ref[request, 0] + blocks, blocks)
            shown = jnp.clip(limit - page * page_len, 0, page_len) * kv_heads
            first = slot_ref[request, page] * (page_len * kv_heads)
            out_ref[pl.ds(i, 1), :] = jnp.where(
                (column >= first) & (column < first + shown), 0.0, -jnp.inf
            )

    loop(row_total, one)


def weigh_kernel(
    first_ref, second_ref, near_ref, near_value_ref, near_bias_ref, far_ref, far_bias_ref,
    late_ref, mixed_ref, point_ref, total_ref, *, sizes,
):
    half, qheads, head_dim = first_ref.shape
    part = min(CHUNK // 2, half)

    def one(i):
        query = jnp.concatenate(
            [
                ref[pl.ds(i * part, part)].reshape(part * qheads, head_dim)
                for ref in (first_ref, second_ref)
            ],
            axis=0,
        )

        def bias(ref):
            return jnp.concatenate(
                [
                    chunk_bias(ref, i * part, part, qheads),
                    chunk_bias(ref, half + i * part, part, qheads),
                ],
                axis=0,
            )

        sides = (
            (near_ref, bias(near_bias_ref), near_value_ref),
            (far_ref, bias(far_bias_ref), None),
        )
        point, total, mixed, late_ref[i] = attend(query, sides, sizes)
        mixed_ref[i] = mixed
        point_ref[i] = jnp.broadcast_to(point, mixed.shape)
        total_ref[i] = jnp.broadcast_to(total, mixed.shape)

    loop(half // part, one)


def finish_kernel(late_ref, mixed_ref, point_ref, total_ref, far_value_ref, send_ref, keep_ref):
    steps, rows, head_dim = mixed_ref.shape
    qheads = send_ref.shape[1] - STAT_ROWS
    part = rows // qheads // 2
    diagonal = spread_rows(qheads, head_dim)

    def one(i):
        mixed = mixed_ref[i] + jnp.dot(
            late_ref[i], far_value_ref[...], preferred_element_type=jnp.float32
        )
        mixed = mixed / total_ref[i]
        for j in range(2 * part):
            rows = slice(j * qheads, (j + 1) * qheads)
            out_ref = keep_ref if j < part else send_ref
            out_ref[i * part + j % part] = write(
                mixed[rows],
                to_row(point_ref[i, rows], diagonal),
                to_row(total_ref[i, rows], diagonal),
                out_ref.dtype,
            )

    loop(steps, one)


def read(parcel):
    parcel = parcel.astype(jnp.float32)
    qheads = parcel.shape[0] - STAT_ROWS
    stats = parcel[qheads:]
    return parcel[:qheads], stats[0:1] + stats[1:2], stats[2:3] + stats[3:4]


def write(mixed, top, total, dtype):
    return jnp.concatenate([mixed, stat_block(top, total)], axis=0).astype(dtype)


def merged(keep_ref, parcel_ref, i, diagonal, scale):
    keep, top, total = read(keep_ref[i])
    other, other_top, other_total = read(parcel_ref[i])
    point = jnp.maximum(top, other_top)
    own_weight = total * jnp.exp2((top - point) * scale)
    other_weight = other_total * jnp.exp2((other_top - point) * scale)
    total = own_weight + other_weight
    return keep + (other - keep) * to_column(other_weight / total, diagonal), point, total


def merge_kernel(parcel_ref, keep_in, send_ref, keep_ref, *, scale):
    count, rows, head_dim = keep_in.shape
    diagonal = spread_rows(rows - STAT_ROWS, head_dim)
    half = count // 2

    def one(i):
        send_ref[i] = write(*merged(keep_in, parcel_ref, half + i, diagonal, scale), send_ref.dtype)
        keep_ref[i] = write(*merged(keep_in, parcel_ref, i, diagonal, scale), keep_ref.dtype)

    loop(half, one)


def last_kernel(parcel_ref, keep_in, out_ref, *, scale):
    count, rows, head_dim = keep_in.shape
    diagonal = spread_rows(rows - STAT_ROWS, head_dim)

    def one(i):
        mixed, _, _ = merged(keep_in, parcel_ref, i, diagonal, scale)
        out_ref[i] = mixed.astype(out_ref.dtype)

    loop(count, one)


def call(kernel, outs, operands, scalars=0, **static):
    return pl.pallas_call(
        functools.partial(kernel, **static),
        out_shape=outs,
        in_specs=[pl.BlockSpec(memory_space=pltpu.SMEM)] * scalars
        + [pl.BlockSpec(memory_space=pltpu.VMEM)] * (len(operands) - scalars),
        compiler_params=pltpu.CompilerParams(vmem_limit_bytes=VMEM_BYTES),
    )(*operands)


def on_device(
    queries, prefix_keys, prefix_values, suffix_pool, page_owner, page_slot, suffix_len, row_request
):
    blocks = lax.axis_size("blk")
    me = lax.axis_index("blk")
    odd_core = lax.axis_index("heads") % 2
    rows_dev, qheads, head_dim = queries.shape
    slots, _, page_len, kv_heads, _ = suffix_pool.shape
    prefix_rows = prefix_keys.shape[0] * kv_heads
    page_rows = page_len * kv_heads
    scale = math.log2(math.e) / math.sqrt(head_dim)
    sizes = (kv_heads, qheads // kv_heads, slots, page_rows, scale)
    shared_bits = [1 << b for b in range(2, blocks.bit_length() - 1)]

    values = prefix_values.reshape(prefix_rows, head_dim)
    near = pack(
        prefix_keys.reshape(prefix_rows, head_dim),
        suffix_pool.reshape(slots * 2 * page_rows, head_dim),
    )
    far = exchange(near, 1, 2)
    far_values = exchange(values, 1, 2)
    first = queries
    for bit in shared_bits:
        first = jnp.concatenate([first, exchange(first, bit, bit)], axis=0)
    second = exchange(first, 2, 1)
    half = first.shape[0]
    rows = 2 * half

    place = jnp.stack([me, 2 - odd_core, 1 + odd_core]).astype(jnp.int32)
    table = jax.ShapeDtypeStruct((rows, slots * page_rows), jnp.float32)
    near_bias, far_bias = call(
        bias_kernel, (table, table), (place, page_owner, page_slot, suffix_len, row_request), 5,
        rows_dev=rows_dev, page_len=page_len, kv_heads=kv_heads, blocks=blocks,
    )
    def parcels(count):
        shape = (count, qheads + STAT_ROWS, head_dim)
        return jax.ShapeDtypeStruct(shape, jnp.bfloat16), jax.ShapeDtypeStruct(shape, jnp.bfloat16)

    part = min(CHUNK // 2, half)
    shape = (half // part, 2 * part * qheads)
    late = jax.ShapeDtypeStruct((*shape, prefix_rows), jnp.bfloat16)
    block = jax.ShapeDtypeStruct((*shape, head_dim), jnp.float32)
    weighed = call(
        weigh_kernel, (late, block, block, block),
        (first, second, near, values, near_bias, far, far_bias), sizes=sizes,
    )
    send, keep = call(finish_kernel, parcels(half), (*weighed, far_values))
    cross = 1 if shared_bits and lax.axis_size("heads") % 2 == 0 else 0
    arrived = exchange(send, 1, 2, 1) if cross else exchange(send, 2, 1)
    turn = cross
    for bit in reversed(shared_bits):
        if turn:
            keep = exchange(keep, 0, 0, turn)
        half //= 2
        send, keep = call(merge_kernel, parcels(half), (arrived, keep), scale=scale)
        turn = cross if bit == shared_bits[0] else 0
        arrived = exchange(send, bit, bit, turn)
    if cross:
        keep = exchange(keep, 0, 0, cross)
    return call(
        last_kernel, jax.ShapeDtypeStruct(queries.shape, queries.dtype), (arrived, keep), scale=scale
    )


def solution(mesh):
    placed = (
        P(("groups", "blk"), "heads", None),
        P(("groups", "blk"), "heads", None),
        P(("groups", "blk"), "heads", None),
        P(("groups", "blk"), None, None, "heads", None),
        P("groups", None),
        P("groups", None),
        P("groups"),
        P("groups"),
    )
    return jax.shard_map(
        on_device,
        mesh=mesh,
        in_specs=placed,
        out_specs=P(("groups", "blk"), "heads", None),
        check_vma=False,
    )
```

```python
import functools
import math

import jax
import jax.numpy as jnp
from jax import lax
from jax.experimental import pallas as pl
from jax.experimental.pallas import tpu as pltpu
from jax.sharding import PartitionSpec as P

VMEM_BYTES = 32 * 1024 * 1024
STAT_ROWS = 16


def exchange(value, even_bit, odd_bit, turn=0):
    blocks = lax.axis_size("blk")
    cores = lax.axis_size("heads")
    pairs = []
    for b in range(blocks):
        for c in range(cores):
            goal = c ^ turn
            pairs.append((b * cores + c, (b ^ (odd_bit if goal % 2 else even_bit)) * cores + goal))
    return lax.ppermute(value, ("blk", "heads"), pairs)


def loop(count, body):
    if count <= 4:
        for i in range(count):
            body(i)
    else:
        lax.fori_loop(0, count, lambda i, carry: (body(i), carry)[1], 0)


def spread_rows(qheads, lanes):
    sub = lax.broadcasted_iota(jnp.int32, (qheads, lanes), 0)
    lane = lax.broadcasted_iota(jnp.int32, (qheads, lanes), 1)
    return sub == lane


def to_row(column, diagonal):
    return jnp.sum(jnp.where(diagonal, column, 0.0), axis=0, keepdims=True)


def to_column(row, diagonal):
    return jnp.sum(jnp.where(diagonal, row, 0.0), axis=1, keepdims=True)


def split(value):
    high = value.astype(jnp.bfloat16).astype(jnp.float32)
    return high, (value - high).astype(jnp.bfloat16).astype(jnp.float32)


def stat_block(top_row, total_row):
    top_high, top_low = split(top_row)
    total_high, total_low = split(total_row)
    blank = jnp.zeros((STAT_ROWS - 4, top_row.shape[1]), jnp.float32)
    return jnp.concatenate([top_high, top_low, total_high, total_low, blank], axis=0)


def suffix_rows(rest_ref, start, slots, page_rows):
    return jnp.concatenate(
        [rest_ref[start + s * 2 * page_rows : start + s * 2 * page_rows + page_rows] for s in range(slots)],
        axis=0,
    )


def attend(query, sides, sizes):
    kv_heads, group, slots, page_rows, scale = sizes
    rows = query.shape[0]
    qheads = kv_heads * group

    def own_head(width):
        row = lax.broadcasted_iota(jnp.int32, (rows, width), 0)
        column = lax.broadcasted_iota(jnp.int32, (rows, width), 1)
        return (row % qheads) // group == column % kv_heads

    def scores(key):
        product = lax.dot_general(
            query, key, (((1,), (1,)), ((), ())), preferred_element_type=jnp.float32
        )
        return jnp.where(own_head(key.shape[0]), product, -jnp.inf)

    parts = []
    for key_ref, pool_ref, bias, value_ref in sides:
        page_key = suffix_rows(pool_ref, 0, slots, page_rows)
        page_value = suffix_rows(pool_ref, page_rows, slots, page_rows)
        parts.append((scores(key_ref[...]), value_ref))
        parts.append((scores(page_key) + bias, page_value))
    top = functools.reduce(jnp.maximum, [jnp.max(score, axis=1, keepdims=True) for score, _ in parts])
    high, low = split(top)
    point = high + low
    total = mixed = 0.0
    late = None
    for score, value in parts:
        weight = jnp.exp2((score - point) * scale)
        total = total + jnp.sum(weight, axis=1, keepdims=True)
        weight = weight.astype(jnp.bfloat16)
        if value is None:
            late = weight
        else:
            mixed = mixed + jnp.dot(weight, value[...], preferred_element_type=jnp.float32)
    return point, total, mixed, late


def chunk_bias(bias_ref, first, count, qheads):
    return jnp.concatenate(
        [
            jnp.broadcast_to(bias_ref[pl.ds(first + j, 1), :], (qheads, bias_ref.shape[1]))
            for j in range(count)
        ],
        axis=0,
    )


def fetch_kernel(
    queries_ref, owner_hbm, slot_hbm, len_hbm, request_hbm, *refs, rows_dev, page_len, kv_heads, sources
):
    del queries_ref
    goals = refs[sources : 2 * sources]
    near_ref, far_ref, owner_ref, slot_ref, len_ref, request_ref, sems = refs[2 * sources :]
    pairs = [
        (owner_hbm, owner_ref),
        (slot_hbm, slot_ref),
        (len_hbm, len_ref),
        (request_hbm, request_ref),
        *zip(refs[:sources], goals),
    ]
    copies = [pltpu.make_async_copy(*pair, sems.at[i]) for i, pair in enumerate(pairs)]
    for copy in copies:
        copy.start()
    for copy in copies[:4]:
        copy.wait()
    blocks = lax.axis_size("blk")
    me = lax.axis_index("blk")
    odd_core = lax.axis_index("heads") % 2
    query_bit, key_bit = 2 - odd_core, 1 + odd_core
    width = near_ref.shape[1]
    all_rows = request_ref.shape[0]
    column = lax.broadcasted_iota(jnp.int32, (1, width), 1)

    def one(i):
        place = i // rows_dev
        device = me ^ jnp.where(place % 2 == 1, query_bit, 0) ^ ((place // 2) * 4)
        row = device * rows_dev + i % rows_dev
        request = request_ref[row]

        def count(j, later):
            return later + jnp.where((request_ref[j] == request) & (j > row), 1, 0)

        if all_rows <= 16:
            later = jnp.int32(0)
            for j in range(all_rows):
                later = count(j, later)
        else:
            later = lax.fori_loop(0, all_rows, count, jnp.int32(0))
        limit = len_ref[request] - later
        for holder, out_ref in ((me, near_ref), (me ^ key_bit, far_ref)):
            page = lax.rem(holder - owner_ref[request, 0] + blocks, blocks)
            shown = jnp.clip(limit - page * page_len, 0, page_len) * kv_heads
            first = slot_ref[request, page] * (page_len * kv_heads)
            out_ref[pl.ds(i, 1), :] = jnp.where(
                (column >= first) & (column < first + shown), 0.0, -jnp.inf
            )

    loop(near_ref.shape[0], one)
    for copy in copies[4:]:
        copy.wait()


def attend(query, sides, sizes):
    kv_heads, group, slots, page_rows, scale = sizes
    rows = query.shape[0]
    qheads = kv_heads * group

    def own_head(width):
        row = lax.broadcasted_iota(jnp.int32, (rows, width), 0)
        column = lax.broadcasted_iota(jnp.int32, (rows, width), 1)
        return (row % qheads) // group == column % kv_heads

    def scores(key):
        product = lax.dot_general(
            query, key, (((1,), (1,)), ((), ())), preferred_element_type=jnp.float32
        )
        return jnp.where(own_head(key.shape[0]), product, -jnp.inf)

    parts = []
    for key_ref, pool_ref, bias, value_ref in sides:
        page_key = suffix_rows(pool_ref, 0, slots, page_rows)
        page_value = suffix_rows(pool_ref, page_rows, slots, page_rows)
        parts.append((scores(key_ref[...]), value_ref))
        parts.append((scores(page_key) + bias, page_value))
    top = functools.reduce(jnp.maximum, [jnp.max(score, axis=1, keepdims=True) for score, _ in parts])
    high, low = split(top)
    point = high + low
    total = mixed = 0.0
    late = None
    for score, value in parts:
        weight = jnp.exp2((score - point) * scale)
        total = total + jnp.sum(weight, axis=1, keepdims=True)
        weight = weight.astype(jnp.bfloat16)
        if value is None:
            late = weight
        else:
            mixed = mixed + jnp.dot(weight, value[...], preferred_element_type=jnp.float32)
    return point, total, mixed, late


def chunk_bias(bias_ref, first, count, qheads):
    return jnp.concatenate(
        [
            jnp.broadcast_to(bias_ref[pl.ds(first + j, 1), :], (qheads, bias_ref.shape[1]))
            for j in range(count)
        ],
        axis=0,
    )


def weigh_kernel(
    first_ref, second_ref, near_ref, near_pool_ref, near_value_ref, near_bias_ref, far_ref, far_pool_ref, far_bias_ref,
    late_ref, mixed_ref, point_ref, total_ref, *, sizes,
):
    half, qheads, head_dim = first_ref.shape
    part = point_ref.shape[1] // qheads // 2

    def one(i):
        query = jnp.concatenate(
            [
                ref[pl.ds(i * part, part)].reshape(part * qheads, head_dim)
                for ref in (first_ref, second_ref)
            ],
            axis=0,
        )

        def bias(ref):
            return jnp.concatenate(
                [
                    chunk_bias(ref, i * part, part, qheads),
                    chunk_bias(ref, half + i * part, part, qheads),
                ],
                axis=0,
            )

        sides = (
            (near_ref, near_pool_ref, bias(near_bias_ref), near_value_ref),
            (far_ref, far_pool_ref, bias(far_bias_ref), None),
        )
        point, total, mixed, late_ref[i] = attend(query, sides, sizes)
        mixed_ref[i] = mixed
        point_ref[i] = jnp.broadcast_to(point, mixed.shape)
        total_ref[i] = jnp.broadcast_to(total, mixed.shape)

    loop(half // part, one)


def finish_kernel(
    late_ref, mixed_ref, point_ref, total_ref, far_value_ref, send_ref, keep_ref, *, rows_dev
):
    steps, rows, head_dim = mixed_ref.shape
    qheads = send_ref.shape[1] - STAT_ROWS
    part = rows // qheads // 2
    diagonal = spread_rows(qheads, head_dim)

    def one(i):
        mixed = mixed_ref[i] + jnp.dot(
            late_ref[i], far_value_ref[...], preferred_element_type=jnp.float32
        )
        mixed = mixed / total_ref[i]
        for j in range(2 * part):
            rows = slice(j * qheads, (j + 1) * qheads)
            own, inner = divmod(j % part, rows_dev)
            out_ref = send_ref if own else keep_ref
            out_ref[j // part * (keep_ref.shape[0] // 2) + i * rows_dev + inner] = write(
                mixed[rows],
                to_row(point_ref[i, rows], diagonal),
                to_row(total_ref[i, rows], diagonal),
                out_ref.dtype,
            )

    loop(steps, one)


def read(parcel):
    parcel = parcel.astype(jnp.float32)
    qheads = parcel.shape[0] - STAT_ROWS
    stats = parcel[qheads:]
    return parcel[:qheads], stats[0:1] + stats[1:2], stats[2:3] + stats[3:4]


def write(mixed, top, total, dtype):
    return jnp.concatenate([mixed, stat_block(top, total)], axis=0).astype(dtype)


def merged(keep_ref, parcel_ref, i, diagonal, scale):
    keep, top, total = read(keep_ref[i])
    other, other_top, other_total = read(parcel_ref[i])
    point = jnp.maximum(top, other_top)
    own_weight = total * jnp.exp2((top - point) * scale)
    other_weight = other_total * jnp.exp2((other_top - point) * scale)
    total = own_weight + other_weight
    return keep + (other - keep) * to_column(other_weight / total, diagonal), point, total


def merge_kernel(parcel_ref, keep_in, send_ref, keep_ref, *, scale):
    count, rows, head_dim = keep_in.shape
    diagonal = spread_rows(rows - STAT_ROWS, head_dim)
    half = count // 2

    def one(i):
        send_ref[i] = write(*merged(keep_in, parcel_ref, half + i, diagonal, scale), send_ref.dtype)
        keep_ref[i] = write(*merged(keep_in, parcel_ref, i, diagonal, scale), keep_ref.dtype)

    loop(half, one)


def last_kernel(parcel_ref, keep_in, out_ref, *, scale):
    count, rows, head_dim = keep_in.shape
    diagonal = spread_rows(rows - STAT_ROWS, head_dim)

    def one(i):
        mixed, _, _ = merged(keep_in, parcel_ref, i, diagonal, scale)
        out_ref[i] = mixed.astype(out_ref.dtype)

    loop(count, one)


def call(kernel, outs, operands, scalars=0, **static):
    return pl.pallas_call(
        functools.partial(kernel, **static),
        out_shape=outs,
        in_specs=[pl.BlockSpec(memory_space=pltpu.SMEM)] * scalars
        + [pl.BlockSpec(memory_space=pltpu.VMEM)] * (len(operands) - scalars),
        compiler_params=pltpu.CompilerParams(vmem_limit_bytes=VMEM_BYTES),
    )(*operands)


def on_device(
    queries, prefix_keys, prefix_values, suffix_pool, page_owner, page_slot, suffix_len, row_request
):
    blocks = lax.axis_size("blk")
    me = lax.axis_index("blk")
    odd_core = lax.axis_index("heads") % 2
    rows_dev, qheads, head_dim = queries.shape
    slots, _, page_len, kv_heads, _ = suffix_pool.shape
    prefix_rows = prefix_keys.shape[0] * kv_heads
    page_rows = page_len * kv_heads
    scale = math.log2(math.e) / math.sqrt(head_dim)
    sizes = (kv_heads, qheads // kv_heads, slots, page_rows, scale)
    shared_bits = [1 << b for b in range(2, blocks.bit_length() - 1)]

    values = prefix_values.reshape(prefix_rows, head_dim)
    keys = prefix_keys.reshape(prefix_rows, head_dim)
    pool = suffix_pool.reshape(slots * 2 * page_rows, head_dim)
    far = exchange(keys, 1, 2)
    far_values = exchange(values, 1, 2)
    far_pool = exchange(pool, 1, 2)
    first = queries
    second = exchange(first, 2, 1)
    for bit in shared_bits:
        first = jnp.concatenate([first, second], axis=0)
        second = exchange(first, bit, bit)
    half = first.shape[0]

    tables = (page_owner, page_slot, suffix_len, row_request)
    arrays = (keys, values, pool)
    mask = jax.ShapeDtypeStruct((2 * half, slots * page_rows), jnp.float32)
    near_keys, near_values, near_pool, near_mask, far_mask = pl.pallas_call(
        functools.partial(
            fetch_kernel,
            rows_dev=rows_dev, page_len=page_len, kv_heads=kv_heads, sources=len(arrays),
        ),
        out_shape=[jax.ShapeDtypeStruct(array.shape, array.dtype) for array in arrays] + [mask] * 2,
        in_specs=[pl.BlockSpec(memory_space=pltpu.VMEM)]
        + [pl.BlockSpec(memory_space=pltpu.HBM)] * (len(tables) + len(arrays)),
        out_specs=[pl.BlockSpec(memory_space=pltpu.VMEM)] * (len(arrays) + 2),
        scratch_shapes=[pltpu.SMEM(table.shape, table.dtype) for table in tables]
        + [pltpu.SemaphoreType.DMA((len(tables) + len(arrays),))],
        compiler_params=pltpu.CompilerParams(vmem_limit_bytes=VMEM_BYTES),
    )(
        first,
        *(pltpu.with_memory_space_constraint(operand, pltpu.HBM) for operand in tables + arrays),
    )

    def parcels(count):
        shape = (count, qheads + STAT_ROWS, head_dim)
        return jax.ShapeDtypeStruct(shape, jnp.bfloat16), jax.ShapeDtypeStruct(shape, jnp.bfloat16)

    part = 2 * rows_dev
    shape = (half // part, 2 * part * qheads)
    late = jax.ShapeDtypeStruct((*shape, prefix_rows), jnp.bfloat16)
    block = jax.ShapeDtypeStruct((*shape, head_dim), jnp.float32)
    weighed = call(
        weigh_kernel, (late, block, block, block),
        (
            first, second, near_keys, near_pool, near_values, near_mask, far, far_pool, far_mask,
        ),
        sizes=sizes,
    )
    send, keep = call(
        finish_kernel, parcels(half), (*weighed, far_values), rows_dev=rows_dev
    )
    cross = 1 if shared_bits and lax.axis_size("heads") % 2 == 0 else 0
    arrived = exchange(send, 1, 2, 1) if cross else exchange(send, 2, 1)
    turn = cross
    for bit in reversed(shared_bits):
        if turn:
            keep = exchange(keep, 0, 0, turn)
        half //= 2
        send, keep = call(merge_kernel, parcels(half), (arrived, keep), scale=scale)
        turn = cross if bit == shared_bits[0] else 0
        arrived = exchange(send, bit, bit, turn)
    if cross:
        keep = exchange(keep, 0, 0, cross)
    return call(
        last_kernel, jax.ShapeDtypeStruct(queries.shape, queries.dtype), (arrived, keep), scale=scale
    )


def solution(mesh):
    placed = (
        P(("groups", "blk"), "heads", None),
        P(("groups", "blk"), "heads", None),
        P(("groups", "blk"), "heads", None),
        P(("groups", "blk"), None, None, "heads", None),
        P("groups", None),
        P("groups", None),
        P("groups"),
        P("groups"),
    )
    return jax.shard_map(
        on_device,
        mesh=mesh,
        in_specs=placed,
        out_specs=P(("groups", "blk"), "heads", None),
        check_vma=False,
    )
```

```python
import functools
import math

import jax
import jax.numpy as jnp
from jax import lax
from jax.experimental import pallas as pl
from jax.experimental.pallas import tpu as pltpu
from jax.sharding import PartitionSpec as P

VMEM_BYTES = 32 * 1024 * 1024
STAT_ROWS = 16


def exchange(value, even_bit, odd_bit, turn=0):
    blocks = lax.axis_size("blk")
    cores = lax.axis_size("heads")
    pairs = []
    for b in range(blocks):
        for c in range(cores):
            goal = c ^ turn
            pairs.append((b * cores + c, (b ^ (odd_bit if goal % 2 else even_bit)) * cores + goal))
    return lax.ppermute(value, ("blk", "heads"), pairs)


def loop(count, body):
    if count <= 4:
        for i in range(count):
            body(i)
    else:
        lax.fori_loop(0, count, lambda i, carry: (body(i), carry)[1], 0)


def spread_rows(qheads, lanes):
    sub = lax.broadcasted_iota(jnp.int32, (qheads, lanes), 0)
    lane = lax.broadcasted_iota(jnp.int32, (qheads, lanes), 1)
    return sub == lane


def to_row(column, diagonal):
    return jnp.sum(jnp.where(diagonal, column, 0.0), axis=0, keepdims=True)


def to_column(row, diagonal):
    return jnp.sum(jnp.where(diagonal, row, 0.0), axis=1, keepdims=True)


def split(value):
    high = value.astype(jnp.bfloat16).astype(jnp.float32)
    return high, (value - high).astype(jnp.bfloat16).astype(jnp.float32)


def stat_block(top_row, total_row):
    top_high, top_low = split(top_row)
    total_high, total_low = split(total_row)
    blank = jnp.zeros((STAT_ROWS - 4, top_row.shape[1]), jnp.float32)
    return jnp.concatenate([top_high, top_low, total_high, total_low, blank], axis=0)


def suffix_rows(rest_ref, start, slots, page_rows):
    return jnp.concatenate(
        [rest_ref[start + s * 2 * page_rows : start + s * 2 * page_rows + page_rows] for s in range(slots)],
        axis=0,
    )


def fetch_kernel(
    queries_ref, owner_hbm, slot_hbm, len_hbm, request_hbm, *refs, rows_dev, page_len, kv_heads, sources
):
    del queries_ref
    goals = refs[sources : 2 * sources]
    near_ref, far_ref, owner_ref, slot_ref, len_ref, request_ref, sems = refs[2 * sources :]
    pairs = [
        (owner_hbm, owner_ref),
        (slot_hbm, slot_ref),
        (len_hbm, len_ref),
        (request_hbm, request_ref),
        *zip(refs[:sources], goals),
    ]
    copies = [pltpu.make_async_copy(*pair, sems.at[i]) for i, pair in enumerate(pairs)]
    for copy in copies:
        copy.start()
    for copy in copies[:4]:
        copy.wait()
    blocks = lax.axis_size("blk")
    me = lax.axis_index("blk")
    odd_core = lax.axis_index("heads") % 2
    query_bit, key_bit = 2 - odd_core, 1 + odd_core
    width = near_ref.shape[1]
    all_rows = request_ref.shape[0]
    column = lax.broadcasted_iota(jnp.int32, (1, width), 1)

    def one(i):
        place = i // rows_dev
        device = me ^ jnp.where(place % 2 == 1, query_bit, 0) ^ ((place // 2) * 4)
        row = device * rows_dev + i % rows_dev
        request = request_ref[row]

        def count(j, later):
            return later + jnp.where((request_ref[j] == request) & (j > row), 1, 0)

        if all_rows <= 16:
            later = jnp.int32(0)
            for j in range(all_rows):
                later = count(j, later)
        else:
            later = lax.fori_loop(0, all_rows, count, jnp.int32(0))
        limit = len_ref[request] - later
        for holder, out_ref in ((me, near_ref), (me ^ key_bit, far_ref)):
            page = lax.rem(holder - owner_ref[request, 0] + blocks, blocks)
            shown = jnp.clip(limit - page * page_len, 0, page_len) * kv_heads
            first = slot_ref[request, page] * (page_len * kv_heads)
            out_ref[pl.ds(i, 1), :] = jnp.where(
                (column >= first) & (column < first + shown), 0.0, -jnp.inf
            )

    loop(near_ref.shape[0], one)
    for copy in copies[4:]:
        copy.wait()


def attend(query, sides, sizes):
    kv_heads, group, slots, page_rows, scale = sizes
    rows = query.shape[0]
    qheads = kv_heads * group

    def own_head(width):
        row = lax.broadcasted_iota(jnp.int32, (rows, width), 0)
        column = lax.broadcasted_iota(jnp.int32, (rows, width), 1)
        return (row % qheads) // group == column % kv_heads

    def scores(key):
        product = lax.dot_general(
            query, key, (((1,), (1,)), ((), ())), preferred_element_type=jnp.float32
        )
        return jnp.where(own_head(key.shape[0]), product, -jnp.inf)

    parts = []
    for key_ref, value_ref, pool_ref, mask in sides:
        page_key = suffix_rows(pool_ref, 0, slots, page_rows)
        page_value = suffix_rows(pool_ref, page_rows, slots, page_rows)
        parts.append((scores(key_ref[...]), value_ref[...]))
        parts.append((scores(page_key) + mask, page_value))
    top = functools.reduce(jnp.maximum, [jnp.max(score, axis=1, keepdims=True) for score, _ in parts])
    high, low = split(top)
    point = high + low
    total = mixed = 0.0
    for score, value in parts:
        weight = jnp.exp2((score - point) * scale)
        total = total + jnp.sum(weight, axis=1, keepdims=True)
        mixed = mixed + jnp.dot(
            weight.astype(jnp.bfloat16), value, preferred_element_type=jnp.float32
        )
    return point, total, mixed / total


def chunk_bias(bias_ref, first, count, qheads):
    return jnp.concatenate(
        [
            jnp.broadcast_to(bias_ref[pl.ds(first + j, 1), :], (qheads, bias_ref.shape[1]))
            for j in range(count)
        ],
        axis=0,
    )


def attend_kernel(first_ref, second_ref, *refs, rows_dev, sizes):
    *side_refs, send_ref, keep_ref = refs
    half, qheads, head_dim = first_ref.shape
    part = 2 * rows_dev
    diagonal = spread_rows(qheads, head_dim)

    def one(i):
        query = jnp.concatenate(
            [
                ref[pl.ds(i * part, part)].reshape(part * qheads, head_dim)
                for ref in (first_ref, second_ref)
            ],
            axis=0,
        )

        def mask(ref):
            return jnp.concatenate(
                [
                    chunk_bias(ref, i * part, part, qheads),
                    chunk_bias(ref, half + i * part, part, qheads),
                ],
                axis=0,
            )

        sides = [(*side_refs[j : j + 3], mask(side_refs[j + 3])) for j in (0, 4)]
        point, total, mixed = attend(query, sides, sizes)
        for j in range(2 * part):
            rows = slice(j * qheads, (j + 1) * qheads)
            own, inner = divmod(j % part, rows_dev)
            out_ref = send_ref if own else keep_ref
            out_ref[j // part * (half // 2) + i * rows_dev + inner] = write(
                mixed[rows], to_row(point[rows], diagonal), to_row(total[rows], diagonal),
                out_ref.dtype,
            )

    loop(half // part, one)


def read(parcel):
    parcel = parcel.astype(jnp.float32)
    qheads = parcel.shape[0] - STAT_ROWS
    stats = parcel[qheads:]
    return parcel[:qheads], stats[0:1] + stats[1:2], stats[2:3] + stats[3:4]


def write(mixed, top, total, dtype):
    return jnp.concatenate([mixed, stat_block(top, total)], axis=0).astype(dtype)


def merged(keep_ref, parcel_ref, i, diagonal, scale):
    keep, top, total = read(keep_ref[i])
    other, other_top, other_total = read(parcel_ref[i])
    point = jnp.maximum(top, other_top)
    own_weight = total * jnp.exp2((top - point) * scale)
    other_weight = other_total * jnp.exp2((other_top - point) * scale)
    total = own_weight + other_weight
    return keep + (other - keep) * to_column(other_weight / total, diagonal), point, total


def merge_kernel(parcel_ref, keep_in, send_ref, keep_ref, *, scale):
    count, rows, head_dim = keep_in.shape
    diagonal = spread_rows(rows - STAT_ROWS, head_dim)
    half = count // 2

    def one(i):
        send_ref[i] = write(*merged(keep_in, parcel_ref, half + i, diagonal, scale), send_ref.dtype)
        keep_ref[i] = write(*merged(keep_in, parcel_ref, i, diagonal, scale), keep_ref.dtype)

    loop(half, one)


def last_kernel(parcel_ref, keep_in, out_ref, *, scale):
    count, rows, head_dim = keep_in.shape
    diagonal = spread_rows(rows - STAT_ROWS, head_dim)

    def one(i):
        mixed, _, _ = merged(keep_in, parcel_ref, i, diagonal, scale)
        out_ref[i] = mixed.astype(out_ref.dtype)

    loop(count, one)


def call(kernel, outs, operands, **static):
    return pl.pallas_call(
        functools.partial(kernel, **static),
        out_shape=outs,
        in_specs=[pl.BlockSpec(memory_space=pltpu.VMEM)] * len(operands),
        compiler_params=pltpu.CompilerParams(vmem_limit_bytes=VMEM_BYTES),
    )(*operands)


def on_device(
    queries, prefix_keys, prefix_values, suffix_pool, page_owner, page_slot, suffix_len, row_request
):
    blocks = lax.axis_size("blk")
    me = lax.axis_index("blk")
    odd_core = lax.axis_index("heads") % 2
    rows_dev, qheads, head_dim = queries.shape
    slots, _, page_len, kv_heads, _ = suffix_pool.shape
    prefix_rows = prefix_keys.shape[0] * kv_heads
    page_rows = page_len * kv_heads
    scale = math.log2(math.e) / math.sqrt(head_dim)
    sizes = (kv_heads, qheads // kv_heads, slots, page_rows, scale)
    shared_bits = [1 << b for b in range(2, blocks.bit_length() - 1)]

    values = prefix_values.reshape(prefix_rows, head_dim)
    keys = prefix_keys.reshape(prefix_rows, head_dim)
    pool = suffix_pool.reshape(slots * 2 * page_rows, head_dim)
    far_keys = exchange(keys, 1, 2)
    far_values = exchange(values, 1, 2)
    far_pool = exchange(pool, 1, 2)
    first = queries
    second = exchange(first, 2, 1)
    for bit in shared_bits:
        first = jnp.concatenate([first, second], axis=0)
        second = exchange(first, bit, bit)
    half = first.shape[0]

    tables = (page_owner, page_slot, suffix_len, row_request)
    arrays = (keys, values, pool)
    mask = jax.ShapeDtypeStruct((2 * half, slots * page_rows), jnp.float32)
    near_keys, near_values, near_pool, near_mask, far_mask = pl.pallas_call(
        functools.partial(
            fetch_kernel,
            rows_dev=rows_dev, page_len=page_len, kv_heads=kv_heads, sources=len(arrays),
        ),
        out_shape=[jax.ShapeDtypeStruct(array.shape, array.dtype) for array in arrays] + [mask] * 2,
        in_specs=[pl.BlockSpec(memory_space=pltpu.VMEM)]
        + [pl.BlockSpec(memory_space=pltpu.HBM)] * (len(tables) + len(arrays)),
        out_specs=[pl.BlockSpec(memory_space=pltpu.VMEM)] * (len(arrays) + 2),
        scratch_shapes=[pltpu.SMEM(table.shape, table.dtype) for table in tables]
        + [pltpu.SemaphoreType.DMA((len(tables) + len(arrays),))],
        compiler_params=pltpu.CompilerParams(vmem_limit_bytes=VMEM_BYTES),
    )(
        first,
        *(pltpu.with_memory_space_constraint(operand, pltpu.HBM) for operand in tables + arrays),
    )

    def parcels(count):
        shape = (count, qheads + STAT_ROWS, head_dim)
        return jax.ShapeDtypeStruct(shape, jnp.bfloat16), jax.ShapeDtypeStruct(shape, jnp.bfloat16)

    send, keep = call(
        attend_kernel, parcels(half),
        (
            first, second, near_keys, near_values, near_pool, near_mask,
            far_keys, far_values, far_pool, far_mask,
        ),
        rows_dev=rows_dev, sizes=sizes,
    )
    cross = 1 if shared_bits and lax.axis_size("heads") % 2 == 0 else 0
    arrived = exchange(send, 1, 2, 1) if cross else exchange(send, 2, 1)
    turn = cross
    for bit in reversed(shared_bits):
        if turn:
            keep = exchange(keep, 0, 0, turn)
        half //= 2
        send, keep = call(merge_kernel, parcels(half), (arrived, keep), scale=scale)
        turn = cross if bit == shared_bits[0] else 0
        arrived = exchange(send, bit, bit, turn)
    if cross:
        keep = exchange(keep, 0, 0, cross)
    return call(
        last_kernel, jax.ShapeDtypeStruct(queries.shape, queries.dtype), (arrived, keep), scale=scale
    )


def solution(mesh):
    placed = (
        P(("groups", "blk"), "heads", None),
        P(("groups", "blk"), "heads", None),
        P(("groups", "blk"), "heads", None),
        P(("groups", "blk"), None, None, "heads", None),
        P("groups", None),
        P("groups", None),
        P("groups"),
        P("groups"),
    )
    return jax.shard_map(
        on_device,
        mesh=mesh,
        in_specs=placed,
        out_specs=P(("groups", "blk"), "heads", None),
        check_vma=False,
    )
```

```python
import functools
import math

import jax
import jax.numpy as jnp
from jax import lax
from jax.experimental import pallas as pl
from jax.experimental.pallas import tpu as pltpu
from jax.sharding import PartitionSpec as P

VMEM_BYTES = 32 * 1024 * 1024
STAT_ROWS = 16


def exchange(value, even_bit, odd_bit, turn=0):
    blocks = lax.axis_size("blk")
    cores = lax.axis_size("heads")
    pairs = []
    for b in range(blocks):
        for c in range(cores):
            goal = c ^ turn
            pairs.append((b * cores + c, (b ^ (odd_bit if goal % 2 else even_bit)) * cores + goal))
    return lax.ppermute(value, ("blk", "heads"), pairs)


def loop(count, body):
    if count <= 4:
        for i in range(count):
            body(i)
    else:
        lax.fori_loop(0, count, lambda i, carry: (body(i), carry)[1], 0)


def spread_rows(qheads, lanes):
    sub = lax.broadcasted_iota(jnp.int32, (qheads, lanes), 0)
    lane = lax.broadcasted_iota(jnp.int32, (qheads, lanes), 1)
    return sub == lane


def to_row(column, diagonal):
    return jnp.sum(jnp.where(diagonal, column, 0.0), axis=0, keepdims=True)


def to_column(row, diagonal):
    return jnp.sum(jnp.where(diagonal, row, 0.0), axis=1, keepdims=True)


def split(value):
    high = value.astype(jnp.bfloat16).astype(jnp.float32)
    return high, (value - high).astype(jnp.bfloat16).astype(jnp.float32)


def stat_block(top_row, total_row):
    top_high, top_low = split(top_row)
    total_high, total_low = split(total_row)
    blank = jnp.zeros((STAT_ROWS - 4, top_row.shape[1]), jnp.float32)
    return jnp.concatenate([top_high, top_low, total_high, total_low, blank], axis=0)


def suffix_rows(pool_ref, start, slots, page_rows, width):
    rows = [
        pool_ref[start + s * 2 * page_rows : start + s * 2 * page_rows + page_rows]
        for s in range(slots)
    ]
    if width > slots * page_rows:
        rows.append(jnp.zeros((width - slots * page_rows, pool_ref.shape[1]), pool_ref.dtype))
    return jnp.concatenate(rows, axis=0)


def fold(function, values, lanes):
    tiles = [
        value[:, at : at + lanes] for value in values for at in range(0, value.shape[1], lanes)
    ]
    return functools.reduce(function, tiles)


def sort_heads(source, wide_ref, goal_ref):
    heads, tokens, _ = goal_ref.shape
    wide_ref[...] = source[...].astype(jnp.float32)
    for g in range(heads):
        goal_ref[g] = wide_ref[pl.ds(g, tokens, stride=heads), :].astype(goal_ref.dtype)


def fetch_kernel(
    queries_ref, far_key_ref, far_value_ref,
    owner_hbm, slot_hbm, len_hbm, request_hbm, key_hbm, value_hbm, pool_hbm,
    far_key_out, far_value_out, key_out, value_out, pool_out, near_ref, far_ref,
    owner_ref, slot_ref, len_ref, request_ref, key_ref, value_ref, wide_ref, sems,
    *, rows_dev, page_len, kv_heads,
):
    del queries_ref
    pairs = [
        (owner_hbm, owner_ref),
        (slot_hbm, slot_ref),
        (len_hbm, len_ref),
        (request_hbm, request_ref),
        (key_hbm, key_ref),
        (value_hbm, value_ref),
        (pool_hbm, pool_out),
    ]
    copies = [pltpu.make_async_copy(*pair, sems.at[i]) for i, pair in enumerate(pairs)]
    for copy in copies:
        copy.start()
    sort_heads(far_key_ref, wide_ref.at[0], far_key_out)
    sort_heads(far_value_ref, wide_ref.at[1], far_value_out)
    for copy in copies[:4]:
        copy.wait()
    blocks = lax.axis_size("blk")
    me = lax.axis_index("blk")
    odd_core = lax.axis_index("heads") % 2
    query_bit, key_bit = 2 - odd_core, 1 + odd_core
    width = near_ref.shape[1]
    all_rows = request_ref.shape[0]
    column = lax.broadcasted_iota(jnp.int32, (1, width), 1)

    def one(i):
        place = i // rows_dev
        device = me ^ jnp.where(place % 2 == 1, query_bit, 0) ^ ((place // 2) * 4)
        row = device * rows_dev + i % rows_dev
        request = request_ref[row]

        def count(j, later):
            return later + jnp.where((request_ref[j] == request) & (j > row), 1, 0)

        if all_rows <= 16:
            later = jnp.int32(0)
            for j in range(all_rows):
                later = count(j, later)
        else:
            later = lax.fori_loop(0, all_rows, count, jnp.int32(0))
        limit = len_ref[request] - later
        for holder, out_ref in ((me, near_ref), (me ^ key_bit, far_ref)):
            page = lax.rem(holder - owner_ref[request, 0] + blocks, blocks)
            shown = jnp.clip(limit - page * page_len, 0, page_len) * kv_heads
            first = slot_ref[request, page] * (page_len * kv_heads)
            out_ref[pl.ds(i, 1), :] = jnp.where(
                (column >= first) & (column < first + shown), 0.0, -jnp.inf
            )

    loop(near_ref.shape[0], one)
    for copy in copies[4:]:
        copy.wait()
    sort_heads(key_ref, wide_ref.at[2], key_out)
    sort_heads(value_ref, wide_ref.at[3], value_out)


def attend(query, sides, sizes):
    kv_heads, slots, page_rows, scale = sizes
    rows, head_dim = query.shape
    share = rows // kv_heads

    def product(left, right):
        return lax.dot_general(
            left, right, (((1,), (1,)), ((), ())), preferred_element_type=jnp.float32
        )

    def own_head(width):
        row = lax.broadcasted_iota(jnp.int32, (rows, width), 0)
        column = lax.broadcasted_iota(jnp.int32, (rows, width), 1)
        return row // share == column % kv_heads

    def by_head(function):
        return jnp.concatenate(
            [function(g, slice(g * share, (g + 1) * share)) for g in range(kv_heads)], axis=0
        )

    parts = []
    for key_ref, value_ref, pool_ref, mask in sides:
        width = mask.shape[1]
        page_key = suffix_rows(pool_ref, 0, slots, page_rows, width)
        page_value = suffix_rows(pool_ref, page_rows, slots, page_rows, width)
        parts.append((by_head(lambda g, at, ref=key_ref: product(query[at], ref[g])), value_ref, None))
        page = jnp.where(own_head(width), product(query, page_key), -jnp.inf) + mask
        parts.append((page, None, page_value))
    top = jnp.max(
        fold(jnp.maximum, [part[0] for part in parts], head_dim), axis=1, keepdims=True
    )
    high, low = split(top)
    point = high + low
    weights = [jnp.exp2((part[0] - point) * scale) for part in parts]
    total = jnp.sum(fold(jnp.add, weights, head_dim), axis=1, keepdims=True)
    mixed = 0.0
    for weight, (_, value_ref, page_value) in zip(weights, parts):
        weight = weight.astype(jnp.bfloat16)
        if page_value is None:
            mixed = mixed + by_head(
                lambda g, at, left=weight, ref=value_ref: jnp.dot(
                    left[at], ref[g], preferred_element_type=jnp.float32
                )
            )
        else:
            mixed = mixed + jnp.dot(weight, page_value, preferred_element_type=jnp.float32)
    return point, total, mixed / total


def attend_kernel(first_ref, second_ref, *refs, rows_dev, sizes):
    *side_refs, send_ref, keep_ref = refs
    half, qheads, head_dim = first_ref.shape
    part = 2 * rows_dev
    diagonal = spread_rows(qheads, head_dim)

    kv_heads = sizes[0]
    group = qheads // kv_heads

    def one(i):
        taken = [(ref, i * part + j) for ref in (first_ref, second_ref) for j in range(part)]
        wide = [ref[place].astype(jnp.float32) for ref, place in taken]
        query = jnp.concatenate(
            [row[g * group : (g + 1) * group] for g in range(kv_heads) for row in wide], axis=0
        ).astype(first_ref.dtype)

        def mask(ref):
            rows = [ref[pl.ds(i * part + j, 1), :] for j in range(part)]
            rows += [ref[pl.ds(half + i * part + j, 1), :] for j in range(part)]
            block = jnp.concatenate(
                [jnp.broadcast_to(row, (group, row.shape[1])) for row in rows], axis=0
            )
            return jnp.concatenate([block] * kv_heads, axis=0)

        sides = [(*side_refs[j : j + 3], mask(side_refs[j + 3])) for j in (0, 4)]
        point, total, mixed = attend(query, sides, sizes)

        def of_row(value, j):
            share = 2 * part * group
            return jnp.concatenate(
                [
                    value[g * share + j * group : g * share + (j + 1) * group]
                    for g in range(kv_heads)
                ],
                axis=0,
            )

        for j in range(2 * part):
            own, inner = divmod(j % part, rows_dev)
            out_ref = send_ref if own else keep_ref
            out_ref[j // part * (half // 2) + i * rows_dev + inner] = write(
                of_row(mixed, j),
                to_row(of_row(point, j), diagonal), to_row(of_row(total, j), diagonal),
                out_ref.dtype,
            )

    loop(half // part, one)


def read(parcel):
    parcel = parcel.astype(jnp.float32)
    qheads = parcel.shape[0] - STAT_ROWS
    stats = parcel[qheads:]
    return parcel[:qheads], stats[0:1] + stats[1:2], stats[2:3] + stats[3:4]


def write(mixed, top, total, dtype):
    return jnp.concatenate([mixed, stat_block(top, total)], axis=0).astype(dtype)


def merged(keep_ref, parcel_ref, i, diagonal, scale):
    keep, top, total = read(keep_ref[i])
    other, other_top, other_total = read(parcel_ref[i])
    point = jnp.maximum(top, other_top)
    own_weight = total * jnp.exp2((top - point) * scale)
    other_weight = other_total * jnp.exp2((other_top - point) * scale)
    total = own_weight + other_weight
    return keep + (other - keep) * to_column(other_weight / total, diagonal), point, total


def merge_kernel(parcel_ref, keep_in, send_ref, keep_ref, *, scale):
    count, rows, head_dim = keep_in.shape
    diagonal = spread_rows(rows - STAT_ROWS, head_dim)
    half = count // 2

    def one(i):
        send_ref[i] = write(*merged(keep_in, parcel_ref, half + i, diagonal, scale), send_ref.dtype)
        keep_ref[i] = write(*merged(keep_in, parcel_ref, i, diagonal, scale), keep_ref.dtype)

    loop(half, one)


def last_kernel(parcel_ref, keep_in, out_ref, *, scale):
    count, rows, head_dim = keep_in.shape
    diagonal = spread_rows(rows - STAT_ROWS, head_dim)

    def one(i):
        mixed, _, _ = merged(keep_in, parcel_ref, i, diagonal, scale)
        out_ref[i] = mixed.astype(out_ref.dtype)

    loop(count, one)


def call(kernel, outs, operands, **static):
    return pl.pallas_call(
        functools.partial(kernel, **static),
        out_shape=outs,
        in_specs=[pl.BlockSpec(memory_space=pltpu.VMEM)] * len(operands),
        compiler_params=pltpu.CompilerParams(vmem_limit_bytes=VMEM_BYTES),
    )(*operands)


def on_device(
    queries, prefix_keys, prefix_values, suffix_pool, page_owner, page_slot, suffix_len, row_request
):
    blocks = lax.axis_size("blk")
    me = lax.axis_index("blk")
    odd_core = lax.axis_index("heads") % 2
    rows_dev, qheads, head_dim = queries.shape
    slots, _, page_len, kv_heads, _ = suffix_pool.shape
    prefix_rows = prefix_keys.shape[0] * kv_heads
    page_rows = page_len * kv_heads
    scale = math.log2(math.e) / math.sqrt(head_dim)
    sizes = (kv_heads, slots, page_rows, scale)
    shared_bits = [1 << b for b in range(2, blocks.bit_length() - 1)]

    values = prefix_values.reshape(prefix_rows, head_dim)
    keys = prefix_keys.reshape(prefix_rows, head_dim)
    pool = suffix_pool.reshape(slots * 2 * page_rows, head_dim)
    far_keys = exchange(keys, 1, 2)
    far_values = exchange(values, 1, 2)
    far_pool = exchange(pool, 1, 2)
    first = queries
    second = exchange(first, 2, 1)
    for bit in shared_bits:
        first = jnp.concatenate([first, second], axis=0)
        second = exchange(first, bit, bit)
    half = first.shape[0]

    tables = (page_owner, page_slot, suffix_len, row_request)
    arrays = (keys, values, pool)
    width = -(-slots * page_rows // head_dim) * head_dim
    mask = jax.ShapeDtypeStruct((2 * half, width), jnp.float32)
    sorted_shape = (kv_heads, prefix_rows // kv_heads, head_dim)
    sorted_heads = jax.ShapeDtypeStruct(sorted_shape, keys.dtype)
    far_keys, far_values, near_keys, near_values, near_pool, near_mask, far_mask = pl.pallas_call(
        functools.partial(
            fetch_kernel, rows_dev=rows_dev, page_len=page_len, kv_heads=kv_heads
        ),
        out_shape=[sorted_heads] * 4 + [jax.ShapeDtypeStruct(pool.shape, pool.dtype)] + [mask] * 2,
        in_specs=[pl.BlockSpec(memory_space=pltpu.VMEM)] * 3
        + [pl.BlockSpec(memory_space=pltpu.HBM)] * (len(tables) + len(arrays)),
        out_specs=[pl.BlockSpec(memory_space=pltpu.VMEM)] * 7,
        scratch_shapes=[pltpu.SMEM(table.shape, table.dtype) for table in tables]
        + [pltpu.VMEM(keys.shape, keys.dtype)] * 2
        + [
            pltpu.VMEM((4, *keys.shape), jnp.float32),
            pltpu.SemaphoreType.DMA((len(tables) + len(arrays),)),
        ],
        compiler_params=pltpu.CompilerParams(vmem_limit_bytes=VMEM_BYTES),
    )(
        first, far_keys, far_values,
        *(pltpu.with_memory_space_constraint(operand, pltpu.HBM) for operand in tables + arrays),
    )

    def parcels(count):
        shape = (count, qheads + STAT_ROWS, head_dim)
        return jax.ShapeDtypeStruct(shape, jnp.bfloat16), jax.ShapeDtypeStruct(shape, jnp.bfloat16)

    send, keep = call(
        attend_kernel, parcels(half),
        (
            first, second, near_keys, near_values, near_pool, near_mask,
            far_keys, far_values, far_pool, far_mask,
        ),
        rows_dev=rows_dev, sizes=sizes,
    )
    cross = 1 if shared_bits and lax.axis_size("heads") % 2 == 0 else 0
    arrived = exchange(send, 1, 2, 1) if cross else exchange(send, 2, 1)
    turn = cross
    for bit in reversed(shared_bits):
        if turn:
            keep = exchange(keep, 0, 0, turn)
        half //= 2
        send, keep = call(merge_kernel, parcels(half), (arrived, keep), scale=scale)
        turn = cross if bit == shared_bits[0] else 0
        arrived = exchange(send, bit, bit, turn)
    if cross:
        keep = exchange(keep, 0, 0, cross)
    return call(
        last_kernel, jax.ShapeDtypeStruct(queries.shape, queries.dtype), (arrived, keep), scale=scale
    )


def solution(mesh):
    placed = (
        P(("groups", "blk"), "heads", None),
        P(("groups", "blk"), "heads", None),
        P(("groups", "blk"), "heads", None),
        P(("groups", "blk"), None, None, "heads", None),
        P("groups", None),
        P("groups", None),
        P("groups"),
        P("groups"),
    )
    return jax.shard_map(
        on_device,
        mesh=mesh,
        in_specs=placed,
        out_specs=P(("groups", "blk"), "heads", None),
        check_vma=False,
    )
```

```python
import functools
import math

import jax
import jax.numpy as jnp
from jax import lax
from jax.experimental import pallas as pl
from jax.experimental.pallas import tpu as pltpu
from jax.sharding import PartitionSpec as P

VMEM_BYTES = 32 * 1024 * 1024
STAT_ROWS = 16


def exchange(value, even_bit, odd_bit, turn=0):
    blocks = lax.axis_size("blk")
    cores = lax.axis_size("heads")
    pairs = []
    for b in range(blocks):
        for c in range(cores):
            goal = c ^ turn
            pairs.append((b * cores + c, (b ^ (odd_bit if goal % 2 else even_bit)) * cores + goal))
    return lax.ppermute(value, ("blk", "heads"), pairs)


def loop(count, body):
    if count <= 4:
        for i in range(count):
            body(i)
    else:
        lax.fori_loop(0, count, lambda i, carry: (body(i), carry)[1], 0)


def spread_rows(qheads, lanes):
    sub = lax.broadcasted_iota(jnp.int32, (qheads, lanes), 0)
    lane = lax.broadcasted_iota(jnp.int32, (qheads, lanes), 1)
    return sub == lane


def to_row(column, diagonal):
    return jnp.sum(jnp.where(diagonal, column, 0.0), axis=0, keepdims=True)


def to_column(row, diagonal):
    return jnp.sum(jnp.where(diagonal, row, 0.0), axis=1, keepdims=True)


def split(value, pieces):
    found = []
    for _ in range(pieces):
        found.append(value.astype(jnp.bfloat16).astype(jnp.float32))
        value = value - found[-1]
    return found


def stat_block(top_row, total_row):
    rows = split(top_row, 3) + split(total_row, 2)
    blank = jnp.zeros((STAT_ROWS - len(rows), top_row.shape[1]), jnp.float32)
    return jnp.concatenate([*rows, blank], axis=0)


def suffix_rows(pool_refs, start, page_rows):
    return jnp.concatenate(
        [
            pool_ref[at + start : at + start + page_rows]
            for pool_ref in pool_refs
            for at in range(0, pool_ref.shape[0], 2 * page_rows)
        ],
        axis=0,
    )


def fold(function, values, lanes):
    tiles = [
        value[:, at : at + lanes] for value in values for at in range(0, value.shape[1], lanes)
    ]
    return functools.reduce(function, tiles)


def sort_heads(source, wide_ref, goal_ref):
    heads, tokens, _ = goal_ref.shape
    wide_ref[...] = source[...].astype(jnp.float32)
    for g in range(heads):
        goal_ref[g] = wide_ref[pl.ds(g, tokens, stride=heads), :].astype(goal_ref.dtype)


def fetch_kernel(
    queries_ref, far_key_ref, far_value_ref,
    owner_hbm, slot_hbm, len_hbm, request_hbm, key_hbm, value_hbm, pool_hbm,
    far_key_out, far_value_out, key_out, value_out, pool_out, mask_ref,
    owner_ref, slot_ref, len_ref, request_ref, key_ref, value_ref, wide_ref, sems,
    *, rows_dev, page_len, kv_heads,
):
    del queries_ref
    pairs = [
        (owner_hbm, owner_ref),
        (slot_hbm, slot_ref),
        (len_hbm, len_ref),
        (request_hbm, request_ref),
        (key_hbm, key_ref),
        (value_hbm, value_ref),
        (pool_hbm, pool_out),
    ]
    copies = [pltpu.make_async_copy(*pair, sems.at[i]) for i, pair in enumerate(pairs)]
    for copy in copies:
        copy.start()
    sort_heads(far_key_ref, wide_ref.at[0], far_key_out)
    sort_heads(far_value_ref, wide_ref.at[1], far_value_out)
    for copy in copies[:4]:
        copy.wait()
    blocks = lax.axis_size("blk")
    me = lax.axis_index("blk")
    odd_core = lax.axis_index("heads") % 2
    query_bit, key_bit = 2 - odd_core, 1 + odd_core
    width = mask_ref.shape[1]
    all_rows = request_ref.shape[0]
    column = lax.broadcasted_iota(jnp.int32, (1, width), 1)

    def one(i):
        place = i // rows_dev
        device = me ^ jnp.where(place % 2 == 1, query_bit, 0) ^ ((place // 2) * 4)
        row = device * rows_dev + i % rows_dev
        request = request_ref[row]

        def count(j, later):
            return later + jnp.where((request_ref[j] == request) & (j > row), 1, 0)

        if all_rows <= 16:
            later = jnp.int32(0)
            for j in range(all_rows):
                later = count(j, later)
        else:
            later = lax.fori_loop(0, all_rows, count, jnp.int32(0))
        limit = len_ref[request] - later
        visible = column < 0
        for holder, start in ((me, 0), (me ^ key_bit, width // 2)):
            page = lax.rem(holder - owner_ref[request, 0] + blocks, blocks)
            shown = jnp.clip(limit - page * page_len, 0, page_len) * kv_heads
            first = start + slot_ref[request, page] * (page_len * kv_heads)
            visible = visible | ((column >= first) & (column < first + shown))
        mask_ref[pl.ds(i, 1), :] = jnp.where(visible, 0.0, -jnp.inf)

    loop(mask_ref.shape[0], one)
    for copy in copies[4:]:
        copy.wait()
    sort_heads(key_ref, wide_ref.at[2], key_out)
    sort_heads(value_ref, wide_ref.at[3], value_out)


def attend(query, sides, pool_refs, mask, sizes):
    kv_heads, page_rows, scale = sizes
    rows, head_dim = query.shape
    share = rows // kv_heads

    def product(left, right):
        return lax.dot_general(
            left, right, (((1,), (1,)), ((), ())), preferred_element_type=jnp.float32
        )

    def own_head(width):
        row = lax.broadcasted_iota(jnp.int32, (rows, width), 0)
        column = lax.broadcasted_iota(jnp.int32, (rows, width), 1)
        return row // share == column % kv_heads

    def by_head(function):
        return jnp.concatenate(
            [function(g, slice(g * share, (g + 1) * share)) for g in range(kv_heads)], axis=0
        )

    parts = [
        (by_head(lambda g, at, ref=key_ref: product(query[at], ref[g])), value_ref, None)
        for key_ref, value_ref in sides
    ]
    page = product(query, suffix_rows(pool_refs, 0, page_rows))
    page = jnp.where(own_head(page.shape[1]), page, -jnp.inf) + mask
    parts.append((page, None, suffix_rows(pool_refs, page_rows, page_rows)))
    top = jnp.max(
        fold(jnp.maximum, [part[0] for part in parts], head_dim), axis=1, keepdims=True
    )
    weights = [jnp.exp2((part[0] - top) * scale) for part in parts]
    total = jnp.sum(fold(jnp.add, weights, head_dim), axis=1, keepdims=True)
    mixed = 0.0
    for weight, (_, value_ref, page_value) in zip(weights, parts):
        weight = weight.astype(jnp.bfloat16)
        if page_value is None:
            mixed = mixed + by_head(
                lambda g, at, left=weight, ref=value_ref: jnp.dot(
                    left[at], ref[g], preferred_element_type=jnp.float32
                )
            )
        else:
            mixed = mixed + jnp.dot(weight, page_value, preferred_element_type=jnp.float32)
    return top, total, mixed * (1.0 / total)


def attend_kernel(
    first_ref, second_ref, near_key_ref, near_value_ref, near_pool_ref,
    far_key_ref, far_value_ref, far_pool_ref, mask_ref, send_ref, keep_ref, *, rows_dev, sizes
):
    half, qheads, head_dim = first_ref.shape
    part = 2 * rows_dev
    diagonal = spread_rows(qheads, head_dim)

    kv_heads = sizes[0]
    group = qheads // kv_heads

    def one(i):
        taken = [(ref, i * part + j) for ref in (first_ref, second_ref) for j in range(part)]
        wide = [ref[place].astype(jnp.float32) for ref, place in taken]
        query = jnp.concatenate(
            [row[g * group : (g + 1) * group] for g in range(kv_heads) for row in wide], axis=0
        ).astype(first_ref.dtype)

        places = [i * part + j for j in range(part)] + [half + i * part + j for j in range(part)]
        masks = [mask_ref[pl.ds(place, 1), :] for place in places]
        block = jnp.concatenate(
            [jnp.broadcast_to(row, (group, row.shape[1])) for row in masks], axis=0
        )
        point, total, mixed = attend(
            query, ((near_key_ref, near_value_ref), (far_key_ref, far_value_ref)),
            (near_pool_ref, far_pool_ref), jnp.concatenate([block] * kv_heads, axis=0), sizes,
        )

        def of_row(value, j):
            share = 2 * part * group
            return jnp.concatenate(
                [
                    value[g * share + j * group : g * share + (j + 1) * group]
                    for g in range(kv_heads)
                ],
                axis=0,
            )

        for j in range(2 * part):
            own, inner = divmod(j % part, rows_dev)
            out_ref = send_ref if own else keep_ref
            out_ref[j // part * (half // 2) + i * rows_dev + inner] = write(
                of_row(mixed, j),
                to_row(of_row(point, j), diagonal), to_row(of_row(total, j), diagonal),
                out_ref.dtype,
            )

    loop(half // part, one)


def read(parcel):
    parcel = parcel.astype(jnp.float32)
    qheads = parcel.shape[0] - STAT_ROWS
    stats = parcel[qheads:]
    return parcel[:qheads], stats[0:1] + stats[1:2] + stats[2:3], stats[3:4] + stats[4:5]


def write(mixed, top, total, dtype):
    return jnp.concatenate([mixed, stat_block(top, total)], axis=0).astype(dtype)


def merged(keep_ref, parcel_ref, i, diagonal, scale):
    keep, top, total = read(keep_ref[i])
    other, other_top, other_total = read(parcel_ref[i])
    point = jnp.maximum(top, other_top)
    own_weight = total * jnp.exp2((top - point) * scale)
    other_weight = other_total * jnp.exp2((other_top - point) * scale)
    total = own_weight + other_weight
    return keep + (other - keep) * to_column(other_weight / total, diagonal), point, total


def merge_kernel(parcel_ref, keep_in, send_ref, keep_ref, *, scale):
    count, rows, head_dim = keep_in.shape
    diagonal = spread_rows(rows - STAT_ROWS, head_dim)
    half = count // 2

    def one(i):
        send_ref[i] = write(*merged(keep_in, parcel_ref, half + i, diagonal, scale), send_ref.dtype)
        keep_ref[i] = write(*merged(keep_in, parcel_ref, i, diagonal, scale), keep_ref.dtype)

    loop(half, one)


def last_kernel(parcel_ref, keep_in, out_ref, *, scale):
    count, rows, head_dim = keep_in.shape
    diagonal = spread_rows(rows - STAT_ROWS, head_dim)

    def one(i):
        mixed, _, _ = merged(keep_in, parcel_ref, i, diagonal, scale)
        out_ref[i] = mixed.astype(out_ref.dtype)

    loop(count, one)


def call(kernel, outs, operands, **static):
    return pl.pallas_call(
        functools.partial(kernel, **static),
        out_shape=outs,
        in_specs=[pl.BlockSpec(memory_space=pltpu.VMEM)] * len(operands),
        compiler_params=pltpu.CompilerParams(vmem_limit_bytes=VMEM_BYTES),
    )(*operands)


def on_device(
    queries, prefix_keys, prefix_values, suffix_pool, page_owner, page_slot, suffix_len, row_request
):
    blocks = lax.axis_size("blk")
    me = lax.axis_index("blk")
    odd_core = lax.axis_index("heads") % 2
    rows_dev, qheads, head_dim = queries.shape
    slots, _, page_len, kv_heads, _ = suffix_pool.shape
    prefix_rows = prefix_keys.shape[0] * kv_heads
    page_rows = page_len * kv_heads
    scale = math.log2(math.e) / math.sqrt(head_dim)
    sizes = (kv_heads, page_rows, scale)
    shared_bits = [1 << b for b in range(2, blocks.bit_length() - 1)]

    values = prefix_values.reshape(prefix_rows, head_dim)
    keys = prefix_keys.reshape(prefix_rows, head_dim)
    pool = suffix_pool.reshape(slots * 2 * page_rows, head_dim)
    far_keys = exchange(keys, 1, 2)
    far_values = exchange(values, 1, 2)
    far_pool = exchange(pool, 1, 2)
    first = queries
    second = exchange(first, 2, 1)
    for bit in shared_bits:
        first = jnp.concatenate([first, second], axis=0)
        second = exchange(first, bit, bit)
    half = first.shape[0]

    tables = (page_owner, page_slot, suffix_len, row_request)
    arrays = (keys, values, pool)
    mask = jax.ShapeDtypeStruct((2 * half, pool.shape[0]), jnp.float32)
    sorted_shape = (kv_heads, prefix_rows // kv_heads, head_dim)
    sorted_heads = jax.ShapeDtypeStruct(sorted_shape, keys.dtype)
    far_keys, far_values, near_keys, near_values, near_pool, near_and_far = pl.pallas_call(
        functools.partial(
            fetch_kernel, rows_dev=rows_dev, page_len=page_len, kv_heads=kv_heads
        ),
        out_shape=[sorted_heads] * 4 + [jax.ShapeDtypeStruct(pool.shape, pool.dtype), mask],
        in_specs=[pl.BlockSpec(memory_space=pltpu.VMEM)] * 3
        + [pl.BlockSpec(memory_space=pltpu.HBM)] * (len(tables) + len(arrays)),
        out_specs=[pl.BlockSpec(memory_space=pltpu.VMEM)] * 6,
        scratch_shapes=[pltpu.SMEM(table.shape, table.dtype) for table in tables]
        + [pltpu.VMEM(keys.shape, keys.dtype)] * 2
        + [
            pltpu.VMEM((4, *keys.shape), jnp.float32),
            pltpu.SemaphoreType.DMA((len(tables) + len(arrays),)),
        ],
        compiler_params=pltpu.CompilerParams(vmem_limit_bytes=VMEM_BYTES),
    )(
        first, far_keys, far_values,
        *(pltpu.with_memory_space_constraint(operand, pltpu.HBM) for operand in tables + arrays),
    )

    def parcels(count):
        shape = (count, qheads + STAT_ROWS, head_dim)
        return jax.ShapeDtypeStruct(shape, jnp.bfloat16), jax.ShapeDtypeStruct(shape, jnp.bfloat16)

    send, keep = call(
        attend_kernel, parcels(half),
        (
            first, second, near_keys, near_values, near_pool,
            far_keys, far_values, far_pool, near_and_far,
        ),
        rows_dev=rows_dev, sizes=sizes,
    )
    cross = 1 if shared_bits and lax.axis_size("heads") % 2 == 0 else 0
    arrived = exchange(send, 1, 2, 1) if cross else exchange(send, 2, 1)
    turn = cross
    for bit in reversed(shared_bits):
        if turn:
            keep = exchange(keep, 0, 0, turn)
        half //= 2
        send, keep = call(merge_kernel, parcels(half), (arrived, keep), scale=scale)
        turn = cross if bit == shared_bits[0] else 0
        arrived = exchange(send, bit, bit, turn)
    if cross:
        keep = exchange(keep, 0, 0, cross)
    return call(
        last_kernel, jax.ShapeDtypeStruct(queries.shape, queries.dtype), (arrived, keep), scale=scale
    )


def solution(mesh):
    placed = (
        P(("groups", "blk"), "heads", None),
        P(("groups", "blk"), "heads", None),
        P(("groups", "blk"), "heads", None),
        P(("groups", "blk"), None, None, "heads", None),
        P("groups", None),
        P("groups", None),
        P("groups"),
        P("groups"),
    )
    return jax.shard_map(
        on_device,
        mesh=mesh,
        in_specs=placed,
        out_specs=P(("groups", "blk"), "heads", None),
        check_vma=False,
    )
```

```python
import functools
import math

import jax
import jax.numpy as jnp
from jax import lax
from jax.experimental import pallas as pl
from jax.experimental.pallas import tpu as pltpu
from jax.sharding import PartitionSpec as P

VMEM_BYTES = 32 * 1024 * 1024
STAT_ROWS = 16


def exchange(value, even_bit, odd_bit, turn=0):
    blocks = lax.axis_size("blk")
    cores = lax.axis_size("heads")
    pairs = []
    for b in range(blocks):
        for c in range(cores):
            goal = c ^ turn
            pairs.append((b * cores + c, (b ^ (odd_bit if goal % 2 else even_bit)) * cores + goal))
    return lax.ppermute(value, ("blk", "heads"), pairs)


def loop(count, body):
    if count <= 4:
        for i in range(count):
            body(i)
    else:
        lax.fori_loop(0, count, lambda i, carry: (body(i), carry)[1], 0)


def spread_rows(qheads, lanes):
    sub = lax.broadcasted_iota(jnp.int32, (qheads, lanes), 0)
    lane = lax.broadcasted_iota(jnp.int32, (qheads, lanes), 1)
    return sub == lane


def to_row(column, diagonal):
    return jnp.sum(jnp.where(diagonal, column, 0.0), axis=0, keepdims=True)


def to_column(row, diagonal):
    return jnp.sum(jnp.where(diagonal, row, 0.0), axis=1, keepdims=True)


def split(value, pieces):
    found = []
    for _ in range(pieces):
        found.append(value.astype(jnp.bfloat16).astype(jnp.float32))
        value = value - found[-1]
    return found


def stat_block(top_row, total_row):
    rows = split(top_row, 3) + split(total_row, 2)
    blank = jnp.zeros((STAT_ROWS - len(rows), top_row.shape[1]), jnp.float32)
    return jnp.concatenate([*rows, blank], axis=0)


def suffix_rows(pool_refs, start, page_rows):
    return jnp.concatenate(
        [
            pool_ref[at + start : at + start + page_rows]
            for pool_ref in pool_refs
            for at in range(0, pool_ref.shape[0], 2 * page_rows)
        ],
        axis=0,
    )


def fold(function, values, lanes):
    tiles = [
        value[:, at : at + lanes] for value in values for at in range(0, value.shape[1], lanes)
    ]
    return functools.reduce(function, tiles)


def sort_heads(source, wide_ref, goal_ref):
    heads, tokens, _ = goal_ref.shape
    wide_ref[...] = source[...].astype(jnp.float32)
    for g in range(heads):
        goal_ref[g] = wide_ref[pl.ds(g, tokens, stride=heads), :].astype(goal_ref.dtype)


def sort_kernel(key_ref, value_ref, mask_ref, key_out, value_out, wide_ref):
    del mask_ref
    sort_heads(key_ref, wide_ref.at[0], key_out)
    sort_heads(value_ref, wide_ref.at[1], value_out)


def fetch_kernel(
    queries_ref,
    owner_hbm, slot_hbm, len_hbm, request_hbm, key_hbm, value_hbm, pool_hbm,
    key_out, value_out, pool_out, mask_ref,
    owner_ref, slot_ref, len_ref, request_ref, key_ref, value_ref, wide_ref, sems,
    *, rows_dev, page_len, kv_heads,
):
    del queries_ref
    pairs = [
        (owner_hbm, owner_ref),
        (slot_hbm, slot_ref),
        (len_hbm, len_ref),
        (request_hbm, request_ref),
        (key_hbm, key_ref),
        (value_hbm, value_ref),
        (pool_hbm, pool_out),
    ]
    copies = [pltpu.make_async_copy(*pair, sems.at[i]) for i, pair in enumerate(pairs)]
    for copy in copies:
        copy.start()
    for copy in copies[:4]:
        copy.wait()
    blocks = lax.axis_size("blk")
    me = lax.axis_index("blk")
    odd_core = lax.axis_index("heads") % 2
    query_bit, key_bit = 2 - odd_core, 1 + odd_core
    width = mask_ref.shape[1]
    all_rows = request_ref.shape[0]
    column = lax.broadcasted_iota(jnp.int32, (1, width), 1)

    def one(i):
        place = i // rows_dev
        device = me ^ jnp.where(place % 2 == 1, query_bit, 0) ^ ((place // 2) * 4)
        row = device * rows_dev + i % rows_dev
        request = request_ref[row]

        def count(j, later):
            return later + jnp.where((request_ref[j] == request) & (j > row), 1, 0)

        if all_rows <= 16:
            later = jnp.int32(0)
            for j in range(all_rows):
                later = count(j, later)
        else:
            later = lax.fori_loop(0, all_rows, count, jnp.int32(0))
        limit = len_ref[request] - later
        visible = column < 0
        for holder, start in ((me, 0), (me ^ key_bit, width // 2)):
            page = lax.rem(holder - owner_ref[request, 0] + blocks, blocks)
            shown = jnp.clip(limit - page * page_len, 0, page_len) * kv_heads
            first = start + slot_ref[request, page] * (page_len * kv_heads)
            visible = visible | ((column >= first) & (column < first + shown))
        mask_ref[pl.ds(i, 1), :] = jnp.where(visible, 0.0, -jnp.inf)

    loop(mask_ref.shape[0], one)
    for copy in copies[4:]:
        copy.wait()
    sort_heads(key_ref, wide_ref.at[0], key_out)
    sort_heads(value_ref, wide_ref.at[1], value_out)


def attend(query, sides, pool_refs, mask, sizes):
    kv_heads, page_rows, scale = sizes
    rows, head_dim = query.shape
    share = rows // kv_heads

    def product(left, right):
        return lax.dot_general(
            left, right, (((1,), (1,)), ((), ())), preferred_element_type=jnp.float32
        )

    def own_head(width):
        row = lax.broadcasted_iota(jnp.int32, (rows, width), 0)
        column = lax.broadcasted_iota(jnp.int32, (rows, width), 1)
        return row // share == column % kv_heads

    def by_head(function):
        return jnp.concatenate(
            [function(g, slice(g * share, (g + 1) * share)) for g in range(kv_heads)], axis=0
        )

    parts = [
        (by_head(lambda g, at, ref=key_ref: product(query[at], ref[g])), value_ref, None)
        for key_ref, value_ref in sides
    ]
    page = product(query, suffix_rows(pool_refs, 0, page_rows))
    page = jnp.where(own_head(page.shape[1]), page, -jnp.inf) + mask
    parts.append((page, None, suffix_rows(pool_refs, page_rows, page_rows)))
    top = jnp.max(
        fold(jnp.maximum, [part[0] for part in parts], head_dim), axis=1, keepdims=True
    )
    weights = [jnp.exp2((part[0] - top) * scale) for part in parts]
    total = jnp.sum(fold(jnp.add, weights, head_dim), axis=1, keepdims=True)
    mixed = 0.0
    for weight, (_, value_ref, page_value) in zip(weights, parts):
        weight = weight.astype(jnp.bfloat16)
        if page_value is None:
            mixed = mixed + by_head(
                lambda g, at, left=weight, ref=value_ref: jnp.dot(
                    left[at], ref[g], preferred_element_type=jnp.float32
                )
            )
        else:
            mixed = mixed + jnp.dot(weight, page_value, preferred_element_type=jnp.float32)
    return top, total, mixed * (1.0 / total)


def attend_kernel(
    first_ref, second_ref, near_key_ref, near_value_ref, near_pool_ref,
    far_key_ref, far_value_ref, far_pool_ref, mask_ref, send_ref, keep_ref, *, rows_dev, sizes
):
    half, qheads, head_dim = first_ref.shape
    part = 2 * rows_dev
    diagonal = spread_rows(qheads, head_dim)

    kv_heads = sizes[0]
    group = qheads // kv_heads

    def one(i):
        taken = [(ref, i * part + j) for ref in (first_ref, second_ref) for j in range(part)]
        wide = [ref[place].astype(jnp.float32) for ref, place in taken]
        query = jnp.concatenate(
            [row[g * group : (g + 1) * group] for g in range(kv_heads) for row in wide], axis=0
        ).astype(first_ref.dtype)

        places = [i * part + j for j in range(part)] + [half + i * part + j for j in range(part)]
        masks = [mask_ref[pl.ds(place, 1), :] for place in places]
        block = jnp.concatenate(
            [jnp.broadcast_to(row, (group, row.shape[1])) for row in masks], axis=0
        )
        point, total, mixed = attend(
            query, ((near_key_ref, near_value_ref), (far_key_ref, far_value_ref)),
            (near_pool_ref, far_pool_ref), jnp.concatenate([block] * kv_heads, axis=0), sizes,
        )

        def of_row(value, j):
            share = 2 * part * group
            return jnp.concatenate(
                [
                    value[g * share + j * group : g * share + (j + 1) * group]
                    for g in range(kv_heads)
                ],
                axis=0,
            )

        for j in range(2 * part):
            own, inner = divmod(j % part, rows_dev)
            out_ref = send_ref if own else keep_ref
            out_ref[j // part * (half // 2) + i * rows_dev + inner] = write(
                of_row(mixed, j),
                to_row(of_row(point, j), diagonal), to_row(of_row(total, j), diagonal),
                out_ref.dtype,
            )

    loop(half // part, one)


def read(parcel):
    parcel = parcel.astype(jnp.float32)
    qheads = parcel.shape[0] - STAT_ROWS
    stats = parcel[qheads:]
    return parcel[:qheads], stats[0:1] + stats[1:2] + stats[2:3], stats[3:4] + stats[4:5]


def write(mixed, top, total, dtype):
    return jnp.concatenate([mixed, stat_block(top, total)], axis=0).astype(dtype)


def merged(keep_ref, parcel_ref, i, diagonal, scale):
    keep, top, total = read(keep_ref[i])
    other, other_top, other_total = read(parcel_ref[i])
    point = jnp.maximum(top, other_top)
    own_weight = total * jnp.exp2((top - point) * scale)
    other_weight = other_total * jnp.exp2((other_top - point) * scale)
    total = own_weight + other_weight
    return keep + (other - keep) * to_column(other_weight / total, diagonal), point, total


def merge_kernel(parcel_ref, keep_in, send_ref, keep_ref, *, scale):
    count, rows, head_dim = keep_in.shape
    diagonal = spread_rows(rows - STAT_ROWS, head_dim)
    half = count // 2

    def one(i):
        send_ref[i] = write(*merged(keep_in, parcel_ref, half + i, diagonal, scale), send_ref.dtype)
        keep_ref[i] = write(*merged(keep_in, parcel_ref, i, diagonal, scale), keep_ref.dtype)

    loop(half, one)


def last_kernel(parcel_ref, keep_in, out_ref, *, scale):
    count, rows, head_dim = keep_in.shape
    diagonal = spread_rows(rows - STAT_ROWS, head_dim)

    def one(i):
        mixed, _, _ = merged(keep_in, parcel_ref, i, diagonal, scale)
        out_ref[i] = mixed.astype(out_ref.dtype)

    loop(count, one)


def call(kernel, outs, operands, scratch=(), **static):
    return pl.pallas_call(
        functools.partial(kernel, **static),
        out_shape=outs,
        in_specs=[pl.BlockSpec(memory_space=pltpu.VMEM)] * len(operands),
        scratch_shapes=scratch,
        compiler_params=pltpu.CompilerParams(vmem_limit_bytes=VMEM_BYTES),
    )(*operands)


def on_device(
    queries, prefix_keys, prefix_values, suffix_pool, page_owner, page_slot, suffix_len, row_request
):
    blocks = lax.axis_size("blk")
    me = lax.axis_index("blk")
    odd_core = lax.axis_index("heads") % 2
    rows_dev, qheads, head_dim = queries.shape
    slots, _, page_len, kv_heads, _ = suffix_pool.shape
    prefix_rows = prefix_keys.shape[0] * kv_heads
    page_rows = page_len * kv_heads
    scale = math.log2(math.e) / math.sqrt(head_dim)
    sizes = (kv_heads, page_rows, scale)
    shared_bits = [1 << b for b in range(2, blocks.bit_length() - 1)]

    values = prefix_values.reshape(prefix_rows, head_dim)
    keys = prefix_keys.reshape(prefix_rows, head_dim)
    pool = suffix_pool.reshape(slots * 2 * page_rows, head_dim)
    far_keys = exchange(keys, 1, 2)
    far_values = exchange(values, 1, 2)
    far_pool = exchange(pool, 1, 2)
    first = queries
    second = exchange(first, 2, 1)
    for bit in shared_bits:
        first = jnp.concatenate([first, second], axis=0)
        second = exchange(first, bit, bit)
    half = first.shape[0]

    tables = (page_owner, page_slot, suffix_len, row_request)
    arrays = (keys, values, pool)
    mask = jax.ShapeDtypeStruct((2 * half, pool.shape[0]), jnp.float32)
    sorted_shape = (kv_heads, prefix_rows // kv_heads, head_dim)
    sorted_heads = jax.ShapeDtypeStruct(sorted_shape, keys.dtype)
    near_keys, near_values, near_pool, near_and_far = pl.pallas_call(
        functools.partial(
            fetch_kernel, rows_dev=rows_dev, page_len=page_len, kv_heads=kv_heads
        ),
        out_shape=[sorted_heads] * 2 + [jax.ShapeDtypeStruct(pool.shape, pool.dtype), mask],
        in_specs=[pl.BlockSpec(memory_space=pltpu.VMEM)]
        + [pl.BlockSpec(memory_space=pltpu.HBM)] * (len(tables) + len(arrays)),
        out_specs=[pl.BlockSpec(memory_space=pltpu.VMEM)] * 4,
        scratch_shapes=[pltpu.SMEM(table.shape, table.dtype) for table in tables]
        + [pltpu.VMEM(keys.shape, keys.dtype)] * 2
        + [
            pltpu.VMEM((2, *keys.shape), jnp.float32),
            pltpu.SemaphoreType.DMA((len(tables) + len(arrays),)),
        ],
        compiler_params=pltpu.CompilerParams(vmem_limit_bytes=VMEM_BYTES),
    )(
        first,
        *(pltpu.with_memory_space_constraint(operand, pltpu.HBM) for operand in tables + arrays),
    )

    far_keys, far_values = call(
        sort_kernel, (sorted_heads, sorted_heads), (far_keys, far_values, near_and_far),
        scratch=[pltpu.VMEM((2, *keys.shape), jnp.float32)],
    )

    def parcels(count):
        shape = (count, qheads + STAT_ROWS, head_dim)
        return jax.ShapeDtypeStruct(shape, jnp.bfloat16), jax.ShapeDtypeStruct(shape, jnp.bfloat16)

    send, keep = call(
        attend_kernel, parcels(half),
        (
            first, second, near_keys, near_values, near_pool,
            far_keys, far_values, far_pool, near_and_far,
        ),
        rows_dev=rows_dev, sizes=sizes,
    )
    cross = 1 if shared_bits and lax.axis_size("heads") % 2 == 0 else 0
    arrived = exchange(send, 1, 2, 1) if cross else exchange(send, 2, 1)
    turn = cross
    for bit in reversed(shared_bits):
        if turn:
            keep = exchange(keep, 0, 0, turn)
        half //= 2
        send, keep = call(merge_kernel, parcels(half), (arrived, keep), scale=scale)
        turn = cross if bit == shared_bits[0] else 0
        arrived = exchange(send, bit, bit, turn)
    if cross:
        keep = exchange(keep, 0, 0, cross)
    return call(
        last_kernel, jax.ShapeDtypeStruct(queries.shape, queries.dtype), (arrived, keep), scale=scale
    )


def solution(mesh):
    placed = (
        P(("groups", "blk"), "heads", None),
        P(("groups", "blk"), "heads", None),
        P(("groups", "blk"), "heads", None),
        P(("groups", "blk"), None, None, "heads", None),
        P("groups", None),
        P("groups", None),
        P("groups"),
        P("groups"),
    )
    return jax.shard_map(
        on_device,
        mesh=mesh,
        in_specs=placed,
        out_specs=P(("groups", "blk"), "heads", None),
        check_vma=False,
    )
```

```python
import functools
import math

import jax
import jax.numpy as jnp
from jax import lax
from jax.experimental import pallas as pl
from jax.experimental.pallas import tpu as pltpu
from jax.sharding import PartitionSpec as P

VMEM_BYTES = 32 * 1024 * 1024
STAT_ROWS = 16


def exchange(value, even_bit, odd_bit, turn=0):
    blocks = lax.axis_size("blk")
    cores = lax.axis_size("heads")
    pairs = []
    for b in range(blocks):
        for c in range(cores):
            goal = c ^ turn
            pairs.append((b * cores + c, (b ^ (odd_bit if goal % 2 else even_bit)) * cores + goal))
    return lax.ppermute(value, ("blk", "heads"), pairs)


def loop(count, body):
    if count <= 4:
        for i in range(count):
            body(i)
    else:
        lax.fori_loop(0, count, lambda i, carry: (body(i), carry)[1], 0)


def spread_rows(qheads, lanes):
    sub = lax.broadcasted_iota(jnp.int32, (qheads, lanes), 0)
    lane = lax.broadcasted_iota(jnp.int32, (qheads, lanes), 1)
    return sub == lane


def to_row(column, diagonal):
    return jnp.sum(jnp.where(diagonal, column, 0.0), axis=0, keepdims=True)


def to_column(row, diagonal):
    return jnp.sum(jnp.where(diagonal, row, 0.0), axis=1, keepdims=True)


def split(value):
    high = value.astype(jnp.bfloat16).astype(jnp.float32)
    return high, (value - high).astype(jnp.bfloat16).astype(jnp.float32)


def stat_block(top_row, total_row):
    top_high, top_low = split(top_row)
    total_high, total_low = split(total_row)
    blank = jnp.zeros((STAT_ROWS - 4, top_row.shape[1]), jnp.float32)
    return jnp.concatenate([top_high, top_low, total_high, total_low, blank], axis=0)


def suffix_rows(pool_refs, start, page_rows):
    return jnp.concatenate(
        [
            pool_ref[at + start : at + start + page_rows]
            for pool_ref in pool_refs
            for at in range(0, pool_ref.shape[0], 2 * page_rows)
        ],
        axis=0,
    )


def fold(function, values, lanes):
    tiles = [
        value[:, at : at + lanes] for value in values for at in range(0, value.shape[1], lanes)
    ]
    return functools.reduce(function, tiles)


def sort_heads(source, wide_ref, goal_ref):
    heads, tokens, _ = goal_ref.shape
    wide_ref[...] = source[...].astype(jnp.float32)
    for g in range(heads):
        goal_ref[g] = wide_ref[pl.ds(g, tokens, stride=heads), :].astype(goal_ref.dtype)


def fetch_kernel(
    queries_ref, far_key_ref, far_value_ref,
    owner_hbm, slot_hbm, len_hbm, request_hbm, key_hbm, value_hbm, pool_hbm,
    far_key_out, far_value_out, key_out, value_out, pool_out, mask_ref,
    owner_ref, slot_ref, len_ref, request_ref, key_ref, value_ref, wide_ref, sems,
    *, rows_dev, page_len, kv_heads,
):
    del queries_ref
    pairs = [
        (owner_hbm, owner_ref),
        (slot_hbm, slot_ref),
        (len_hbm, len_ref),
        (request_hbm, request_ref),
        (key_hbm, key_ref),
        (value_hbm, value_ref),
        (pool_hbm, pool_out),
    ]
    copies = [pltpu.make_async_copy(*pair, sems.at[i]) for i, pair in enumerate(pairs)]
    for copy in copies:
        copy.start()
    sort_heads(far_key_ref, wide_ref.at[0], far_key_out)
    sort_heads(far_value_ref, wide_ref.at[1], far_value_out)
    for copy in copies[:4]:
        copy.wait()
    blocks = lax.axis_size("blk")
    me = lax.axis_index("blk")
    odd_core = lax.axis_index("heads") % 2
    query_bit, key_bit = 2 - odd_core, 1 + odd_core
    width = mask_ref.shape[1]
    all_rows = request_ref.shape[0]
    column = lax.broadcasted_iota(jnp.int32, (1, width), 1)

    def one(i):
        place = i // rows_dev
        device = me ^ jnp.where(place % 2 == 1, query_bit, 0) ^ ((place // 2) * 4)
        row = device * rows_dev + i % rows_dev
        request = request_ref[row]

        def count(j, later):
            return later + jnp.where((request_ref[j] == request) & (j > row), 1, 0)

        if all_rows <= 16:
            later = jnp.int32(0)
            for j in range(all_rows):
                later = count(j, later)
        else:
            later = lax.fori_loop(0, all_rows, count, jnp.int32(0))
        limit = len_ref[request] - later
        visible = column < 0
        for holder, start in ((me, 0), (me ^ key_bit, width // 2)):
            page = lax.rem(holder - owner_ref[request, 0] + blocks, blocks)
            shown = jnp.clip(limit - page * page_len, 0, page_len) * kv_heads
            first = start + slot_ref[request, page] * (page_len * kv_heads)
            visible = visible | ((column >= first) & (column < first + shown))
        mask_ref[pl.ds(i, 1), :] = jnp.where(visible, 0.0, -jnp.inf)

    loop(mask_ref.shape[0], one)
    for copy in copies[4:]:
        copy.wait()
    sort_heads(key_ref, wide_ref.at[2], key_out)
    sort_heads(value_ref, wide_ref.at[3], value_out)


def attend(query, sides, pool_refs, mask, sizes):
    kv_heads, page_rows, scale = sizes
    rows, head_dim = query.shape
    share = rows // kv_heads

    def product(left, right):
        return lax.dot_general(
            left, right, (((1,), (1,)), ((), ())), preferred_element_type=jnp.float32
        )

    def own_head(width):
        row = lax.broadcasted_iota(jnp.int32, (rows, width), 0)
        column = lax.broadcasted_iota(jnp.int32, (rows, width), 1)
        return row // share == column % kv_heads

    def by_head(function):
        return jnp.concatenate(
            [function(g, slice(g * share, (g + 1) * share)) for g in range(kv_heads)], axis=0
        )

    parts = [
        (by_head(lambda g, at, ref=key_ref: product(query[at], ref[g])), value_ref, None)
        for key_ref, value_ref in sides
    ]
    page = product(query, suffix_rows(pool_refs, 0, page_rows))
    page = jnp.where(own_head(page.shape[1]), page, -jnp.inf) + mask
    parts.append((page, None, suffix_rows(pool_refs, page_rows, page_rows)))
    top = jnp.max(
        fold(jnp.maximum, [part[0] for part in parts], head_dim), axis=1, keepdims=True
    )
    high, low = split(top)
    point = high + low
    weights = [jnp.exp2((part[0] - point) * scale) for part in parts]
    total = jnp.sum(fold(jnp.add, weights, head_dim), axis=1, keepdims=True)
    mixed = 0.0
    for weight, (_, value_ref, page_value) in zip(weights, parts):
        weight = weight.astype(jnp.bfloat16)
        if page_value is None:
            mixed = mixed + by_head(
                lambda g, at, left=weight, ref=value_ref: jnp.dot(
                    left[at], ref[g], preferred_element_type=jnp.float32
                )
            )
        else:
            mixed = mixed + jnp.dot(weight, page_value, preferred_element_type=jnp.float32)
    return point, total, mixed / total


def attend_kernel(
    first_ref, second_ref, near_key_ref, near_value_ref, near_pool_ref,
    far_key_ref, far_value_ref, far_pool_ref, mask_ref, send_ref, keep_ref, *, rows_dev, sizes
):
    half, qheads, head_dim = first_ref.shape
    part = 2 * rows_dev
    diagonal = spread_rows(qheads, head_dim)

    kv_heads = sizes[0]
    group = qheads // kv_heads

    def one(i):
        taken = [(ref, i * part + j) for ref in (first_ref, second_ref) for j in range(part)]
        wide = [ref[place].astype(jnp.float32) for ref, place in taken]
        query = jnp.concatenate(
            [row[g * group : (g + 1) * group] for g in range(kv_heads) for row in wide], axis=0
        ).astype(first_ref.dtype)

        places = [i * part + j for j in range(part)] + [half + i * part + j for j in range(part)]
        masks = [mask_ref[pl.ds(place, 1), :] for place in places]
        block = jnp.concatenate(
            [jnp.broadcast_to(row, (group, row.shape[1])) for row in masks], axis=0
        )
        point, total, mixed = attend(
            query, ((near_key_ref, near_value_ref), (far_key_ref, far_value_ref)),
            (near_pool_ref, far_pool_ref), jnp.concatenate([block] * kv_heads, axis=0), sizes,
        )

        def of_row(value, j):
            share = 2 * part * group
            return jnp.concatenate(
                [
                    value[g * share + j * group : g * share + (j + 1) * group]
                    for g in range(kv_heads)
                ],
                axis=0,
            )

        for j in range(2 * part):
            own, inner = divmod(j % part, rows_dev)
            out_ref = send_ref if own else keep_ref
            out_ref[j // part * (half // 2) + i * rows_dev + inner] = write(
                of_row(mixed, j),
                to_row(of_row(point, j), diagonal), to_row(of_row(total, j), diagonal),
                out_ref.dtype,
            )

    loop(half // part, one)


def read(parcel):
    parcel = parcel.astype(jnp.float32)
    qheads = parcel.shape[0] - STAT_ROWS
    stats = parcel[qheads:]
    return parcel[:qheads], stats[0:1] + stats[1:2], stats[2:3] + stats[3:4]


def write(mixed, top, total, dtype):
    return jnp.concatenate([mixed, stat_block(top, total)], axis=0).astype(dtype)


def merged(keep_ref, parcel_ref, i, diagonal, scale):
    keep, top, total = read(keep_ref[i])
    other, other_top, other_total = read(parcel_ref[i])
    point = jnp.maximum(top, other_top)
    own_weight = total * jnp.exp2((top - point) * scale)
    other_weight = other_total * jnp.exp2((other_top - point) * scale)
    total = own_weight + other_weight
    return keep + (other - keep) * to_column(other_weight / total, diagonal), point, total


def merge_kernel(parcel_ref, keep_in, send_ref, keep_ref, *, scale):
    count, rows, head_dim = keep_in.shape
    diagonal = spread_rows(rows - STAT_ROWS, head_dim)
    half = count // 2

    def one(i):
        send_ref[i] = write(*merged(keep_in, parcel_ref, half + i, diagonal, scale), send_ref.dtype)
        keep_ref[i] = write(*merged(keep_in, parcel_ref, i, diagonal, scale), keep_ref.dtype)

    loop(half, one)


def last_kernel(parcel_ref, keep_in, out_ref, *, scale):
    count, rows, head_dim = keep_in.shape
    diagonal = spread_rows(rows - STAT_ROWS, head_dim)

    def one(i):
        mixed, _, _ = merged(keep_in, parcel_ref, i, diagonal, scale)
        out_ref[i] = mixed.astype(out_ref.dtype)

    loop(count, one)


def call(kernel, outs, operands, **static):
    return pl.pallas_call(
        functools.partial(kernel, **static),
        out_shape=outs,
        in_specs=[pl.BlockSpec(memory_space=pltpu.VMEM)] * len(operands),
        compiler_params=pltpu.CompilerParams(vmem_limit_bytes=VMEM_BYTES),
    )(*operands)


def on_device(
    queries, prefix_keys, prefix_values, suffix_pool, page_owner, page_slot, suffix_len, row_request
):
    blocks = lax.axis_size("blk")
    me = lax.axis_index("blk")
    odd_core = lax.axis_index("heads") % 2
    rows_dev, qheads, head_dim = queries.shape
    slots, _, page_len, kv_heads, _ = suffix_pool.shape
    prefix_rows = prefix_keys.shape[0] * kv_heads
    page_rows = page_len * kv_heads
    scale = math.log2(math.e) / math.sqrt(head_dim)
    sizes = (kv_heads, page_rows, scale)
    shared_bits = [1 << b for b in range(2, blocks.bit_length() - 1)]

    values = prefix_values.reshape(prefix_rows, head_dim)
    keys = prefix_keys.reshape(prefix_rows, head_dim)
    pool = suffix_pool.reshape(slots * 2 * page_rows, head_dim)
    far_keys = exchange(keys, 1, 2)
    far_values = exchange(values, 1, 2)
    far_pool = exchange(pool, 1, 2)
    first = queries
    second = exchange(first, 2, 1)
    for bit in shared_bits:
        first = jnp.concatenate([first, second], axis=0)
        second = exchange(first, bit, bit)
    half = first.shape[0]

    tables = (page_owner, page_slot, suffix_len, row_request)
    arrays = (keys, values, pool)
    mask = jax.ShapeDtypeStruct((2 * half, pool.shape[0]), jnp.float32)
    sorted_shape = (kv_heads, prefix_rows // kv_heads, head_dim)
    sorted_heads = jax.ShapeDtypeStruct(sorted_shape, keys.dtype)
    far_keys, far_values, near_keys, near_values, near_pool, near_and_far = pl.pallas_call(
        functools.partial(
            fetch_kernel, rows_dev=rows_dev, page_len=page_len, kv_heads=kv_heads
        ),
        out_shape=[sorted_heads] * 4 + [jax.ShapeDtypeStruct(pool.shape, pool.dtype), mask],
        in_specs=[pl.BlockSpec(memory_space=pltpu.VMEM)] * 3
        + [pl.BlockSpec(memory_space=pltpu.HBM)] * (len(tables) + len(arrays)),
        out_specs=[pl.BlockSpec(memory_space=pltpu.VMEM)] * 6,
        scratch_shapes=[pltpu.SMEM(table.shape, table.dtype) for table in tables]
        + [pltpu.VMEM(keys.shape, keys.dtype)] * 2
        + [
            pltpu.VMEM((4, *keys.shape), jnp.float32),
            pltpu.SemaphoreType.DMA((len(tables) + len(arrays),)),
        ],
        compiler_params=pltpu.CompilerParams(vmem_limit_bytes=VMEM_BYTES),
    )(
        first, far_keys, far_values,
        *(pltpu.with_memory_space_constraint(operand, pltpu.HBM) for operand in tables + arrays),
    )

    def parcels(count):
        shape = (count, qheads + STAT_ROWS, head_dim)
        return jax.ShapeDtypeStruct(shape, jnp.bfloat16), jax.ShapeDtypeStruct(shape, jnp.bfloat16)

    send, keep = call(
        attend_kernel, parcels(half),
        (
            first, second, near_keys, near_values, near_pool,
            far_keys, far_values, far_pool, near_and_far,
        ),
        rows_dev=rows_dev, sizes=sizes,
    )
    cross = 1 if shared_bits and lax.axis_size("heads") % 2 == 0 else 0
    arrived = exchange(send, 1, 2, 1) if cross else exchange(send, 2, 1)
    turn = cross
    for bit in reversed(shared_bits):
        if turn:
            keep = exchange(keep, 0, 0, turn)
        half //= 2
        send, keep = call(merge_kernel, parcels(half), (arrived, keep), scale=scale)
        turn = cross if bit == shared_bits[0] else 0
        arrived = exchange(send, bit, bit, turn)
    if cross:
        keep = exchange(keep, 0, 0, cross)
    return call(
        last_kernel, jax.ShapeDtypeStruct(queries.shape, queries.dtype), (arrived, keep), scale=scale
    )


def solution(mesh):
    placed = (
        P(("groups", "blk"), "heads", None),
        P(("groups", "blk"), "heads", None),
        P(("groups", "blk"), "heads", None),
        P(("groups", "blk"), None, None, "heads", None),
        P("groups", None),
        P("groups", None),
        P("groups"),
        P("groups"),
    )
    return jax.shard_map(
        on_device,
        mesh=mesh,
        in_specs=placed,
        out_specs=P(("groups", "blk"), "heads", None),
        check_vma=False,
    )
```

```python
import functools
import math

import jax
import jax.numpy as jnp
from jax import lax
from jax.experimental import pallas as pl
from jax.experimental.pallas import tpu as pltpu
from jax.sharding import PartitionSpec as P

VMEM_BYTES = 32 * 1024 * 1024
STAT_ROWS = 16


def exchange(value, even_bit, odd_bit, turn=0):
    blocks = lax.axis_size("blk")
    cores = lax.axis_size("heads")
    pairs = []
    for b in range(blocks):
        for c in range(cores):
            goal = c ^ turn
            pairs.append((b * cores + c, (b ^ (odd_bit if goal % 2 else even_bit)) * cores + goal))
    return lax.ppermute(value, ("blk", "heads"), pairs)


def loop(count, body):
    if count <= 4:
        for i in range(count):
            body(i)
    else:
        lax.fori_loop(0, count, lambda i, carry: (body(i), carry)[1], 0)


def spread_rows(qheads, lanes):
    sub = lax.broadcasted_iota(jnp.int32, (qheads, lanes), 0)
    lane = lax.broadcasted_iota(jnp.int32, (qheads, lanes), 1)
    return sub == lane


def to_row(column, diagonal):
    return jnp.sum(jnp.where(diagonal, column, 0.0), axis=0, keepdims=True)


def to_column(row, diagonal):
    return jnp.sum(jnp.where(diagonal, row, 0.0), axis=1, keepdims=True)


def split(value):
    high = value.astype(jnp.bfloat16).astype(jnp.float32)
    return high, (value - high).astype(jnp.bfloat16).astype(jnp.float32)


def stat_block(top_row, total_row):
    top_high, top_low = split(top_row)
    total_high, total_low = split(total_row)
    blank = jnp.zeros((STAT_ROWS - 4, top_row.shape[1]), jnp.float32)
    return jnp.concatenate([top_high, top_low, total_high, total_low, blank], axis=0)


def suffix_rows(pool_ref, start, slots, page_rows, width):
    rows = [
        pool_ref[start + s * 2 * page_rows : start + s * 2 * page_rows + page_rows]
        for s in range(slots)
    ]
    if width > slots * page_rows:
        rows.append(jnp.zeros((width - slots * page_rows, pool_ref.shape[1]), pool_ref.dtype))
    return jnp.concatenate(rows, axis=0)


def fold(function, values, lanes):
    tiles = [
        value[:, at : at + lanes] for value in values for at in range(0, value.shape[1], lanes)
    ]
    return functools.reduce(function, tiles)


def sort_heads(source, wide_ref, goal_ref):
    heads, tokens, _ = goal_ref.shape
    wide_ref[...] = source[...].astype(jnp.float32)
    for g in range(heads):
        goal_ref[g] = wide_ref[pl.ds(g, tokens, stride=heads), :].astype(goal_ref.dtype)


def fetch_kernel(
    queries_ref, far_key_ref, far_value_ref,
    owner_hbm, slot_hbm, len_hbm, request_hbm, key_hbm, value_hbm, pool_hbm,
    far_key_out, far_value_out, key_out, value_out, pool_out, near_ref, far_ref,
    owner_ref, slot_ref, len_ref, request_ref, key_ref, value_ref, wide_ref, sems,
    *, rows_dev, page_len, kv_heads,
):
    del queries_ref
    pairs = [
        (owner_hbm, owner_ref),
        (slot_hbm, slot_ref),
        (len_hbm, len_ref),
        (request_hbm, request_ref),
        (key_hbm, key_ref),
        (value_hbm, value_ref),
        (pool_hbm, pool_out),
    ]
    copies = [pltpu.make_async_copy(*pair, sems.at[i]) for i, pair in enumerate(pairs)]
    for copy in copies:
        copy.start()
    sort_heads(far_key_ref, wide_ref.at[0], far_key_out)
    sort_heads(far_value_ref, wide_ref.at[1], far_value_out)
    for copy in copies[:4]:
        copy.wait()
    blocks = lax.axis_size("blk")
    me = lax.axis_index("blk")
    odd_core = lax.axis_index("heads") % 2
    query_bit, key_bit = 2 - odd_core, 1 + odd_core
    width = near_ref.shape[1]
    all_rows = request_ref.shape[0]
    column = lax.broadcasted_iota(jnp.int32, (1, width), 1)

    def one(i):
        place = i // rows_dev
        device = me ^ jnp.where(place % 2 == 1, query_bit, 0) ^ ((place // 2) * 4)
        row = device * rows_dev + i % rows_dev
        request = request_ref[row]

        def count(j, later):
            return later + jnp.where((request_ref[j] == request) & (j > row), 1, 0)

        if all_rows <= 16:
            later = jnp.int32(0)
            for j in range(all_rows):
                later = count(j, later)
        else:
            later = lax.fori_loop(0, all_rows, count, jnp.int32(0))
        limit = len_ref[request] - later
        for holder, out_ref in ((me, near_ref), (me ^ key_bit, far_ref)):
            page = lax.rem(holder - owner_ref[request, 0] + blocks, blocks)
            shown = jnp.clip(limit - page * page_len, 0, page_len) * kv_heads
            first = slot_ref[request, page] * (page_len * kv_heads)
            out_ref[pl.ds(i, 1), :] = jnp.where(
                (column >= first) & (column < first + shown), 0.0, -jnp.inf
            )

    loop(near_ref.shape[0], one)
    for copy in copies[4:]:
        copy.wait()
    sort_heads(key_ref, wide_ref.at[2], key_out)
    sort_heads(value_ref, wide_ref.at[3], value_out)


def attend(query, sides, sizes):
    kv_heads, slots, page_rows, scale = sizes
    rows, head_dim = query.shape
    share = rows // kv_heads

    def product(left, right):
        return lax.dot_general(
            left, right, (((1,), (1,)), ((), ())), preferred_element_type=jnp.float32
        )

    def own_head(width):
        row = lax.broadcasted_iota(jnp.int32, (rows, width), 0)
        column = lax.broadcasted_iota(jnp.int32, (rows, width), 1)
        return row // share == column % kv_heads

    def by_head(function):
        return jnp.concatenate(
            [function(g, slice(g * share, (g + 1) * share)) for g in range(kv_heads)], axis=0
        )

    parts = []
    for key_ref, value_ref, pool_ref, mask in sides:
        width = mask.shape[1]
        page_key = suffix_rows(pool_ref, 0, slots, page_rows, width)
        page_value = suffix_rows(pool_ref, page_rows, slots, page_rows, width)
        parts.append((by_head(lambda g, at, ref=key_ref: product(query[at], ref[g])), value_ref, None))
        page = jnp.where(own_head(width), product(query, page_key), -jnp.inf) + mask
        parts.append((page, None, page_value))
    top = jnp.max(
        fold(jnp.maximum, [part[0] for part in parts], head_dim), axis=1, keepdims=True
    )
    high, low = split(top)
    point = high + low
    weights = [jnp.exp2((part[0] - point) * scale) for part in parts]
    total = jnp.sum(fold(jnp.add, weights, head_dim), axis=1, keepdims=True)
    mixed = 0.0
    for weight, (_, value_ref, page_value) in zip(weights, parts):
        weight = weight.astype(jnp.bfloat16)
        if page_value is None:
            mixed = mixed + by_head(
                lambda g, at, left=weight, ref=value_ref: jnp.dot(
                    left[at], ref[g], preferred_element_type=jnp.float32
                )
            )
        else:
            mixed = mixed + jnp.dot(weight, page_value, preferred_element_type=jnp.float32)
    return point, total, mixed / total


def attend_kernel(first_ref, second_ref, *refs, rows_dev, sizes):
    *side_refs, send_ref, keep_ref = refs
    half, qheads, head_dim = first_ref.shape
    part = 2 * rows_dev
    diagonal = spread_rows(qheads, head_dim)

    kv_heads = sizes[0]
    group = qheads // kv_heads

    def one(i):
        taken = [(ref, i * part + j) for ref in (first_ref, second_ref) for j in range(part)]
        wide = [ref[place].astype(jnp.float32) for ref, place in taken]
        query = jnp.concatenate(
            [row[g * group : (g + 1) * group] for g in range(kv_heads) for row in wide], axis=0
        ).astype(first_ref.dtype)

        def mask(ref):
            rows = [ref[pl.ds(i * part + j, 1), :] for j in range(part)]
            rows += [ref[pl.ds(half + i * part + j, 1), :] for j in range(part)]
            block = jnp.concatenate(
                [jnp.broadcast_to(row, (group, row.shape[1])) for row in rows], axis=0
            )
            return jnp.concatenate([block] * kv_heads, axis=0)

        sides = [(*side_refs[j : j + 3], mask(side_refs[j + 3])) for j in (0, 4)]
        point, total, mixed = attend(query, sides, sizes)

        def of_row(value, j):
            share = 2 * part * group
            return jnp.concatenate(
                [
                    value[g * share + j * group : g * share + (j + 1) * group]
                    for g in range(kv_heads)
                ],
                axis=0,
            )

        for j in range(2 * part):
            out_ref = keep_ref if j < part else send_ref
            out_ref[i * part + j % part] = write(
                of_row(mixed, j),
                to_row(of_row(point, j), diagonal), to_row(of_row(total, j), diagonal),
                out_ref.dtype,
            )

    loop(half // part, one)


def read(parcel):
    parcel = parcel.astype(jnp.float32)
    qheads = parcel.shape[0] - STAT_ROWS
    stats = parcel[qheads:]
    return parcel[:qheads], stats[0:1] + stats[1:2], stats[2:3] + stats[3:4]


def write(mixed, top, total, dtype):
    return jnp.concatenate([mixed, stat_block(top, total)], axis=0).astype(dtype)


def merged(keep_ref, parcel_ref, i, diagonal, scale):
    keep, top, total = read(keep_ref[i])
    other, other_top, other_total = read(parcel_ref[i])
    point = jnp.maximum(top, other_top)
    own_weight = total * jnp.exp2((top - point) * scale)
    other_weight = other_total * jnp.exp2((other_top - point) * scale)
    total = own_weight + other_weight
    return keep + (other - keep) * to_column(other_weight / total, diagonal), point, total


def merge_kernel(parcel_ref, keep_in, send_ref, keep_ref, *, scale):
    count, rows, head_dim = keep_in.shape
    diagonal = spread_rows(rows - STAT_ROWS, head_dim)
    half = count // 2

    def one(i):
        send_ref[i] = write(*merged(keep_in, parcel_ref, half + i, diagonal, scale), send_ref.dtype)
        keep_ref[i] = write(*merged(keep_in, parcel_ref, i, diagonal, scale), keep_ref.dtype)

    loop(half, one)


def last_kernel(parcel_ref, keep_in, out_ref, *, scale):
    count, rows, head_dim = keep_in.shape
    diagonal = spread_rows(rows - STAT_ROWS, head_dim)

    def one(i):
        mixed, _, _ = merged(keep_in, parcel_ref, i, diagonal, scale)
        out_ref[i] = mixed.astype(out_ref.dtype)

    loop(count, one)


def call(kernel, outs, operands, **static):
    return pl.pallas_call(
        functools.partial(kernel, **static),
        out_shape=outs,
        in_specs=[pl.BlockSpec(memory_space=pltpu.VMEM)] * len(operands),
        compiler_params=pltpu.CompilerParams(vmem_limit_bytes=VMEM_BYTES),
    )(*operands)


def on_device(
    queries, prefix_keys, prefix_values, suffix_pool, page_owner, page_slot, suffix_len, row_request
):
    blocks = lax.axis_size("blk")
    me = lax.axis_index("blk")
    odd_core = lax.axis_index("heads") % 2
    rows_dev, qheads, head_dim = queries.shape
    slots, _, page_len, kv_heads, _ = suffix_pool.shape
    prefix_rows = prefix_keys.shape[0] * kv_heads
    page_rows = page_len * kv_heads
    scale = math.log2(math.e) / math.sqrt(head_dim)
    sizes = (kv_heads, slots, page_rows, scale)
    shared_bits = [1 << b for b in range(2, blocks.bit_length() - 1)]

    values = prefix_values.reshape(prefix_rows, head_dim)
    keys = prefix_keys.reshape(prefix_rows, head_dim)
    pool = suffix_pool.reshape(slots * 2 * page_rows, head_dim)
    far_keys = exchange(keys, 1, 2)
    far_values = exchange(values, 1, 2)
    far_pool = exchange(pool, 1, 2)
    first = queries
    second = exchange(first, 2, 1)
    for bit in shared_bits:
        first = jnp.concatenate([first, second], axis=0)
        second = exchange(first, bit, bit)
    half = first.shape[0]

    tables = (page_owner, page_slot, suffix_len, row_request)
    arrays = (keys, values, pool)
    width = -(-slots * page_rows // head_dim) * head_dim
    mask = jax.ShapeDtypeStruct((2 * half, width), jnp.float32)
    sorted_shape = (kv_heads, prefix_rows // kv_heads, head_dim)
    sorted_heads = jax.ShapeDtypeStruct(sorted_shape, keys.dtype)
    far_keys, far_values, near_keys, near_values, near_pool, near_mask, far_mask = pl.pallas_call(
        functools.partial(
            fetch_kernel, rows_dev=rows_dev, page_len=page_len, kv_heads=kv_heads
        ),
        out_shape=[sorted_heads] * 4 + [jax.ShapeDtypeStruct(pool.shape, pool.dtype)] + [mask] * 2,
        in_specs=[pl.BlockSpec(memory_space=pltpu.VMEM)] * 3
        + [pl.BlockSpec(memory_space=pltpu.HBM)] * (len(tables) + len(arrays)),
        out_specs=[pl.BlockSpec(memory_space=pltpu.VMEM)] * 7,
        scratch_shapes=[pltpu.SMEM(table.shape, table.dtype) for table in tables]
        + [pltpu.VMEM(keys.shape, keys.dtype)] * 2
        + [
            pltpu.VMEM((4, *keys.shape), jnp.float32),
            pltpu.SemaphoreType.DMA((len(tables) + len(arrays),)),
        ],
        compiler_params=pltpu.CompilerParams(vmem_limit_bytes=VMEM_BYTES),
    )(
        first, far_keys, far_values,
        *(pltpu.with_memory_space_constraint(operand, pltpu.HBM) for operand in tables + arrays),
    )

    def parcels(count):
        shape = (count, qheads + STAT_ROWS, head_dim)
        return jax.ShapeDtypeStruct(shape, jnp.bfloat16), jax.ShapeDtypeStruct(shape, jnp.bfloat16)

    send, keep = call(
        attend_kernel, parcels(half),
        (
            first, second, near_keys, near_values, near_pool, near_mask,
            far_keys, far_values, far_pool, far_mask,
        ),
        rows_dev=rows_dev, sizes=sizes,
    )
    cross = 1 if shared_bits and lax.axis_size("heads") % 2 == 0 else 0
    turn = cross
    for bit in reversed(shared_bits):
        arrived = exchange(send, bit, bit, turn)
        if turn:
            keep = exchange(keep, 0, 0, turn)
        half //= 2
        send, keep = call(merge_kernel, parcels(half), (arrived, keep), scale=scale)
        turn = 0
    arrived = exchange(send, 2, 1, cross)
    if cross:
        keep = exchange(keep, 0, 0, cross)
    return call(
        last_kernel, jax.ShapeDtypeStruct(queries.shape, queries.dtype), (arrived, keep), scale=scale
    )


def solution(mesh):
    placed = (
        P(("groups", "blk"), "heads", None),
        P(("groups", "blk"), "heads", None),
        P(("groups", "blk"), "heads", None),
        P(("groups", "blk"), None, None, "heads", None),
        P("groups", None),
        P("groups", None),
        P("groups"),
        P("groups"),
    )
    return jax.shard_map(
        on_device,
        mesh=mesh,
        in_specs=placed,
        out_specs=P(("groups", "blk"), "heads", None),
        check_vma=False,
    )
```
